32 devices in a mesh: dp: 16 (over z, y, core), tensor: 2 (over x).
Axes of the slice: x: 2, y: 2, z: 4, core: 2. Of those that a mesh axis runs over, the one named last changes fastest.
Arguments:
- tokens: bfloat16 [8192, 2048], P('dp'), may hold values from -6 to 6
- segments: int32 [8192], P('dp'), may hold values from 0 to 2, as said below
- gain_attend: bfloat16 [2048], P('dp'), may hold values from 0.5 to 1.5
- w_query: bfloat16 [2048, 2048], P('dp', 'tensor'), may hold values from -0.125 to 0.125
- w_key: bfloat16 [2048, 256], P('dp', 'tensor'), may hold values from -0.125 to 0.125
- w_value: bfloat16 [2048, 256], P('dp', 'tensor'), may hold values from -0.125 to 0.125
- w_output: bfloat16 [2048, 2048], P('tensor', 'dp'), may hold values from -0.5 to 0.5
- gain_mixer: bfloat16 [2048], P('dp'), may hold values from 0.5 to 1.5
- w_gate: bfloat16 [2048, 5632], P('dp', 'tensor'), may hold values from -0.125 to 0.125
- w_up: bfloat16 [2048, 5632], P('dp', 'tensor'), may hold values from -0.125 to 0.125
- w_down: bfloat16 [5632, 2048], P('tensor', 'dp'), may hold values from -0.078125 to 0.078125
- cotangent: bfloat16 [8192, 2048], P('dp'), may hold values from -6 to 6
Outputs:
- output: bfloat16 [8192, 2048], P('dp')
- grad_tokens: bfloat16 [8192, 2048], P('dp')
- grad_gain_attend: float32 [2048], P('dp')
- grad_query: float32 [2048, 2048], P('dp', 'tensor')
- grad_key: float32 [2048, 256], P('dp', 'tensor')
- grad_value: float32 [2048, 256], P('dp', 'tensor')
- grad_output: float32 [2048, 2048], P('tensor', 'dp')
- grad_gain_mixer: float32 [2048], P('dp')
- grad_gate: float32 [2048, 5632], P('dp', 'tensor')
- grad_up: float32 [2048, 5632], P('dp', 'tensor')
- grad_down: float32 [5632, 2048], P('tensor', 'dp')
The draws below stay inside these ranges and needn't reach their ends.
Inputs may be any that keep to these rules, and one draw needn't show every extreme that they name: `segments`: within each group of 512 tokens the ids start at 0 and never fall, each document has 64 tokens or more, and the first group holds three documents.
All inputs are finite; a program needn't handle non-finite values.
Results may differ from the reference program's by a relative error of at most 0.017.
Values may be sent and summed in bfloat16 or wider, within the bound.
No kernel may reach another device: no remote copies, remote signals or barrier semaphores. Data moves between devices by JAX's collectives and lax.ppermute only.
A program may use at most 320 MiB of HBM per device.

```python
import math
import jax
import jax.numpy as jnp
from jax import lax

D = 2048
H = 32
KV = 4
HD = 64
FF = 5632
TOK_DEV = 512
MIN_DOC = 64
TOKENS = 8192
N_DP = 16


def draw_segments(key, part):
    key = jax.random.fold_in(key, 11)
    first_key, second_key, count_key = jax.random.split(key, 3)
    first_cut = jax.random.randint(first_key, (N_DP, 1), MIN_DOC, TOK_DEV // 2 + 1)
    second_cut = jax.random.randint(second_key, (N_DP, 1), TOK_DEV // 2 + MIN_DOC, TOK_DEV - MIN_DOC + 1)
    numbers = jax.random.randint(count_key, (N_DP, 1), 1, 4)
    numbers = jnp.where(jnp.arange(N_DP)[:, None] == 0, 3, numbers)
    places = jnp.arange(TOK_DEV)[None, :]
    ids = jnp.where(places >= first_cut, 1, 0) * jnp.where(numbers >= 2, 1, 0)
    ids = ids + jnp.where(places >= second_cut, 1, 0) * jnp.where(numbers >= 3, 1, 0)
    return ids.reshape(TOKENS).astype(jnp.int32)


def spiked(entries, stream_key, source, target, blocks, factor):
    def block_of(position):
        return (jnp.arange(entries.shape[position]) // (entries.shape[position] // blocks)).reshape((-1,) + (1,) * (entries.ndim - 1 - position))

    near = jax.random.permutation(stream_key, blocks)[block_of(target)]
    far = (block_of(target) + blocks // 2) % blocks
    return jnp.where((block_of(source) == near) | (block_of(source) == far), factor * entries, entries)


def levels(own_key, dims, cuts, least, largest):
    def one(position, parts):
        heights = jax.random.uniform(jax.random.fold_in(jax.random.fold_in(own_key, 6), position), (parts,), jnp.float32, least / len(cuts), largest / len(cuts))
        return jnp.repeat(jnp.exp(heights), dims[position] // parts).reshape((-1,) + (1,) * (len(dims) - position - 1))

    gain = one(*cuts[0])
    for cut in cuts[1:]:
        gain = gain * one(*cut)
    return gain


def normal_values(rng, shape, deviation, bound, shards=(), kind=jnp.bfloat16):
    entries = jax.random.normal(rng, shape, jnp.float32) * deviation
    if len(shards) > 0:
        entries = levels(rng, shape, shards, -0.22, 0.18) * entries
    return jnp.clip(entries, min=-bound, max=bound).astype(kind)


def bell_draw_with(own_key, extent, scale, most, shards, heavy, kind=jnp.bfloat16):
    array = scale * jax.random.normal(own_key, extent, jnp.float32)
    if shards:
        array = array * levels(own_key, extent, shards, -0.22, 0.18)
    return jnp.clip(spiked(array, jax.random.fold_in(own_key, 3), *heavy), -most, most).astype(kind)


def setup_inputs(seed: int = 0) -> dict:
    key_of = jax.random.split(jax.random.key(seed), 13)
    return {
        "tokens": bell_draw_with(key_of[0], (TOKENS, D), 1.0, 6.0, ((0, 16),), (0, 1, 16, 2.0)),
        "segments": draw_segments(jax.random.fold_in(key_of[12], 71), 0),
        "gain_attend": jnp.clip(1.0 + 0.1 * jax.random.normal(key_of[2], (D,), jnp.float32), 0.5, 1.5).astype(jnp.bfloat16),
        "w_query": normal_values(key_of[3], (D, H * HD), D ** -0.5, 0.125, ((0, 16), (1, 2))),
        "w_key": normal_values(key_of[4], (D, KV * HD), D ** -0.5, 0.125, ((0, 16), (1, 2))),
        "w_value": normal_values(key_of[5], (D, KV * HD), D ** -0.5, 0.125, ((0, 16), (1, 2))),
        "w_output": normal_values(key_of[6], (H * HD, D), (H * HD // 16) ** -0.5, 0.5, ((0, 2), (1, 16))),
        "gain_mixer": jnp.clip(1.0 + 0.1 * jax.random.normal(key_of[7], (D,), jnp.float32), 0.5, 1.5).astype(jnp.bfloat16),
        "w_gate": normal_values(key_of[8], (D, FF), D ** -0.5, 0.125, ((0, 16), (1, 2))),
        "w_up": normal_values(key_of[9], (D, FF), D ** -0.5, 0.125, ((0, 16), (1, 2))),
        "w_down": normal_values(key_of[10], (FF, D), FF ** -0.5, 0.078125, ((0, 2), (1, 16))),
        "cotangent": bell_draw_with(key_of[11], (TOKENS, D), 1.0, 6.0, ((0, 16),), (0, 1, 16, 2.0)),
    }


@jax.custom_vjp
def low(v):
    return lax.optimization_barrier(v.astype(jnp.bfloat16)).astype(jnp.float32)

@jax.custom_vjp
def low_back(v):
    return v

def low_keep(v):
    return (low(v), None)

def low_pass(kept, grad):
    return (grad,)

def back_keep(v):
    return (v, None)

def back_low(kept, grad):
    return (low(grad),)
low.defvjp(low_keep, low_pass)
low_back.defvjp(back_keep, back_low)
EPSILON = 1e-05
HIGHEST = lax.Precision.HIGHEST

def product(left, right):
    return jnp.dot(left, right, precision=HIGHEST)

def rms_scale(values):
    return lax.rsqrt(lax.optimization_barrier(jnp.mean(values * values, axis=-1, keepdims=True)) + EPSILON)

def rotary(field, cosine, sine):
    half = field.shape[-1] // 2
    first = field[..., :half]
    second = field[..., half:]
    return jnp.concatenate([first * cosine - second * sine, second * cosine + first * sine], axis=-1)

def positions_of(segment_ids):
    places = jnp.broadcast_to(jnp.arange(segment_ids.shape[-1], dtype=jnp.int32), segment_ids.shape)
    leading = jnp.ones(segment_ids.shape[:-1] + (1,), dtype=bool)
    fresh = jnp.concatenate([leading, segment_ids[..., 1:] != segment_ids[..., :-1]], axis=-1)
    starts = lax.cummax(jnp.where(fresh, places, 0).astype(jnp.int32), axis=segment_ids.ndim - 1)
    return (places - starts).astype(jnp.int32)

def angles_of(positions):
    indices = jnp.arange(HD // 2, dtype=jnp.float32)
    freqs = jnp.exp(indices * (-2.0 * math.log(10000.0) / HD))
    angle = positions.astype(jnp.float32)[:, None] * freqs[None, :]
    return (jnp.cos(angle)[:, None, :], jnp.sin(angle)[:, None, :])

def attend_group(pieces):
    queries, keys_rot, values_b, segment_ids = pieces
    places = jnp.arange(segment_ids.shape[0], dtype=jnp.int32)
    scores = low_back(jnp.einsum('qgrd,kgd->grqk', queries, keys_rot, precision=HIGHEST) * 0.125)
    allowed = (segment_ids[:, None] == segment_ids[None, :]) & (places[None, :] <= places[:, None])
    scores = jnp.where(allowed, scores, -1e+30)
    top = lax.optimization_barrier(jnp.max(scores, axis=-1, keepdims=True))
    expo = jnp.exp(scores - top)
    probs = expo / lax.optimization_barrier(jnp.sum(expo, axis=-1, keepdims=True))
    return jnp.einsum('grqk,kgd->qgrd', low(probs), values_b, precision=HIGHEST)

def layer(inputs, weights, segment_ids, groups):
    gain_one, w_query, w_key, w_value, w_output, gain_two, w_gate, w_up, w_down = weights
    rows = inputs.shape[0]
    heads = w_query.shape[1] // HD
    kv_heads = w_key.shape[1] // HD
    repeat = heads // kv_heads
    positions = positions_of(segment_ids.reshape(groups, -1)).reshape(rows)
    cosine, sine = angles_of(positions)
    normed_one = low(inputs * rms_scale(inputs) * gain_one)
    q_lin = low_back(product(normed_one, w_query))
    k_lin = low_back(product(normed_one, w_key))
    v_lin = low(low_back(product(normed_one, w_value)))
    queries = low(rotary(q_lin.reshape(rows, heads, HD), cosine, sine)).reshape(groups, -1, kv_heads, repeat, HD)
    keys_rot = low(rotary(k_lin.reshape(rows, kv_heads, HD), cosine, sine)).reshape(groups, -1, kv_heads, HD)
    values_b = v_lin.reshape(groups, -1, kv_heads, HD)
    attended = lax.map(jax.checkpoint(attend_group), (queries, keys_rot, values_b, segment_ids.reshape(groups, -1)))
    attended = low(low_back(attended.reshape(rows, heads * HD)))
    resid = inputs + low_back(product(attended, w_output))
    normed_two = low(resid * rms_scale(resid) * gain_two)
    gate_value = low_back(product(normed_two, w_gate))
    lifted = low_back(product(normed_two, w_up))
    act = low(jax.nn.silu(gate_value) * lifted)
    return resid + low_back(product(act, w_down))

def reference(tokens, segments, gain_attend, w_query, w_key, w_value, w_output, gain_mixer, w_gate, w_up, w_down, cotangent):
    groups = 1
    while groups * 2 * TOK_DEV <= 4096 and N_DP % (groups * 2) == 0:
        groups = groups * 2
    rounds = N_DP // groups
    rows = groups * TOK_DEV
    weights = tuple((w.astype(jnp.float32) for w in (gain_attend, w_query, w_key, w_value, w_output, gain_mixer, w_gate, w_up, w_down)))

    def one_round(carry, pieces):
        block_tokens, block_segments, block_cot = pieces

        def apply_layer(inputs, *params):
            return layer(inputs, params, block_segments, groups)
        result, pullback = jax.vjp(apply_layer, block_tokens.astype(jnp.float32), *weights)
        grads = pullback(block_cot.astype(jnp.float32))
        summed = tuple((total + grad for total, grad in zip(carry, grads[1:])))
        return (summed, (result.astype(jnp.bfloat16), grads[0].astype(jnp.bfloat16)))
    start = tuple((jnp.zeros(w.shape, jnp.float32) for w in weights))
    inputs = (tokens.reshape(rounds, rows, -1), segments.reshape(rounds, rows), cotangent.reshape(rounds, rows, -1))
    totals, (outputs, grad_inputs) = lax.scan(one_round, start, inputs)
    width = tokens.shape[1]
    return (outputs.reshape(-1, width), grad_inputs.reshape(-1, width), totals[0], totals[1], totals[2], totals[3], totals[4], totals[5], totals[6], totals[7], totals[8])
```

```python
import math

import jax
import jax.numpy as jnp
from jax import lax
from jax.sharding import PartitionSpec as P

HD = 64
EPSILON = 1e-05
BF = jnp.bfloat16
F32 = jnp.float32


def rotate(field, cosine, sine):
    half = field.shape[-1] // 2
    first, second = field[..., :half], field[..., half:]
    return jnp.concatenate(
        [first * cosine - second * sine, second * cosine + first * sine], axis=-1
    )


def rms_scale(values):
    return lax.rsqrt(jnp.mean(values * values, axis=-1, keepdims=True) + EPSILON)


def norm_back(resid, rstd, gain, grad_normed):
    scaled = gain * grad_normed
    inner = jnp.mean(scaled * resid, axis=-1, keepdims=True)
    return rstd * scaled - resid * (rstd * rstd * rstd) * inner


def dot(a, b):
    return jnp.dot(a, b, preferred_element_type=F32)


def dot_tn(a, b):
    return lax.dot_general(a, b, (((0,), (0,)), ((), ())), preferred_element_type=F32)


def dot_nt(a, b):
    return lax.dot_general(a, b, (((1,), (1,)), ((), ())), preferred_element_type=F32)


class Ring:
    def __init__(self, devices):
        self.n = devices // 2
        n = self.n
        order = list(range(0, n, 2)) + list(range(n - 1 - n % 2, 0, -2))
        self.order = order
        place = [0] * n
        for position, chip in enumerate(order):
            place[chip] = position
        self.place = place
        self.forward, self.backward = [], []
        for position, chip in enumerate(order):
            after = order[(position + 1) % n]
            for core in (0, 1):
                self.forward.append((2 * chip + core, 2 * after + core))
                self.backward.append((2 * after + core, 2 * chip + core))
        self.swap = [(i, i ^ 1) for i in range(devices)]

    def pass_on(self, block, way):
        return lax.ppermute(block, "dp", self.forward if way > 0 else self.backward)

    def gather(self, block, way):
        n = self.n
        slots = [block]
        for _ in range(n - 1):
            slots.append(self.pass_on(slots[-1], way))
        return slots if way > 0 else [slots[(n - i) % n] for i in range(n)]

    def scatter(self, term, way):
        n = self.n
        if n == 1:
            return term(0)
        along = list(range(1, n)) if way > 0 else list(range(n - 1, 0, -1))
        held = term(along[0]).astype(BF)
        for i in along[1:] + [0]:
            came = self.pass_on(held, way).astype(F32)
            total = came + term(i)
            held = total.astype(BF)
        return total

    def exchange(self, block):
        return lax.ppermute(block, "dp", self.swap)


def per_device(
    shape,
    tokens,
    segments,
    gain_attend,
    w_query,
    w_key,
    w_value,
    w_output,
    gain_mixer,
    w_gate,
    w_up,
    w_down,
    cotangent,
):
    devices, tensors = shape
    ring = Ring(devices)
    n = ring.n
    rows, depth = tokens.shape
    part = depth // devices
    wide = 2 * part
    index = lax.axis_index("dp")
    core = index % 2
    first = core == 0
    position = jnp.asarray(ring.place, jnp.int32)[index // 2]
    blocks = jnp.asarray(ring.order, jnp.int32)[(position - jnp.arange(n, dtype=jnp.int32)) % n]

    def swap(block):
        return ring.exchange(block)

    def across(block):
        if tensors == 1:
            return jnp.zeros_like(block)
        return lax.ppermute(block, "tensor", [(i, i ^ 1) for i in range(tensors)])

    def cols(w, half):
        return lax.dynamic_slice_in_dim(w, half * (w.shape[1] // 2), w.shape[1] // 2, 1)

    def rws(w, half):
        return lax.dynamic_slice_in_dim(w, half * (w.shape[0] // 2), w.shape[0] // 2, 0)

    def paired(pick, axis):
        mine, came = pick(core), swap(pick(1 - core))
        return jnp.concatenate(
            [jnp.where(first, mine, came), jnp.where(first, came, mine)], axis=axis
        )

    gains = jnp.zeros((16, (w_query.shape[1] + 2 * w_key.shape[1]) // 2), BF)
    gains = gains.at[0, :part].set(gain_attend).at[1, :part].set(gain_mixer)

    def qkv_pick(half):
        return jnp.concatenate(
            [jnp.concatenate([cols(w_query, half), cols(w_key, half), cols(w_value, half)], axis=1), gains],
            axis=0,
        )

    mine, came = qkv_pick(core), swap(qkv_pick(1 - core))
    low, high = jnp.where(first, mine, came), jnp.where(first, came, mine)
    q_cols = w_query.shape[1] // 2
    k_cols = w_key.shape[1] // 2
    all_cols = q_cols + 2 * k_cols
    cut = (all_cols // 2 + 127) // 128 * 128
    gain_rows = jnp.concatenate(
        [low[part:, :part], high[part:, :part], jnp.zeros((16, cut - wide), BF)], axis=1
    )
    qkv_one = jnp.concatenate([low[:part, :cut], high[:part, :cut], gain_rows], axis=0)
    qkv_two = jnp.concatenate([low[:part, cut:], high[:part, cut:]], axis=0)
    qkv_one = ring.gather(qkv_one, 1)
    qkv_two = ring.gather(qkv_two, -1)
    out_block = paired(lambda half: rws(w_output, half), 1)
    half_rows = out_block.shape[0] // 2
    out_one = ring.gather(out_block[:half_rows], 1)
    out_two = ring.gather(out_block[half_rows:], -1)
    gate_slots = ring.gather(paired(lambda half: cols(w_gate, half), 0), 1)
    up_slots = ring.gather(paired(lambda half: cols(w_up, half), 0), -1)
    down_block = paired(lambda half: rws(w_down, half), 1)
    half_units = down_block.shape[0] // 2
    down_one = ring.gather(down_block[:half_units], 1)
    down_two = ring.gather(down_block[half_units:], -1)

    def to_ring(field):
        return jnp.take(field.reshape(rows, n, wide), blocks, axis=1).reshape(rows, depth)

    inverse = jnp.zeros((n,), jnp.int32).at[blocks].set(jnp.arange(n, dtype=jnp.int32))

    def from_ring(field):
        return jnp.take(field.reshape(rows, n, wide), inverse, axis=1).reshape(rows, depth)

    x_mine = to_ring(tokens)
    dy_mine = to_ring(cotangent)
    x_all = jnp.concatenate([x_mine, swap(x_mine)], axis=0)
    dy_all = jnp.concatenate([dy_mine, swap(dy_mine)], axis=0)
    seg_all = jnp.stack([segments, swap(segments)])

    places = jnp.arange(rows, dtype=jnp.int32)
    fresh = jnp.concatenate(
        [jnp.ones((2, 1), dtype=bool), seg_all[:, 1:] != seg_all[:, :-1]], axis=1
    )
    starts = lax.cummax(jnp.where(fresh, places, 0), axis=1)
    freqs = jnp.exp(jnp.arange(HD // 2, dtype=F32) * (-2.0 * math.log(10000.0) / HD))
    angle = (places - starts).astype(F32).reshape(2 * rows, 1) * freqs[None, :]
    cosine = jnp.cos(angle)[:, None, :]
    sine = jnp.sin(angle)[:, None, :]
    allowed = (seg_all[:, :, None] == seg_all[:, None, :]) & (places[None, :] <= places[:, None])
    allowed = allowed[:, None]

    gain_one = jnp.concatenate([b[wide : wide + 1, :wide] for b in qkv_one], axis=1).astype(F32)
    gain_two = jnp.concatenate([b[wide + 1 : wide + 2, :wide] for b in qkv_one], axis=1).astype(F32)
    w_qkv = jnp.concatenate(
        [
            jnp.concatenate([b[:wide] for b in qkv_one], axis=0),
            jnp.concatenate(qkv_two, axis=0),
        ],
        axis=1,
    )
    inputs = x_all.astype(F32)
    rstd_one = rms_scale(inputs)
    normed_one = (inputs * rstd_one * gain_one).astype(BF)
    qkv = dot(normed_one, w_qkv)
    heads = q_cols // HD
    kv_heads = k_cols // HD
    repeat = heads // kv_heads
    queries = rotate(qkv[:, :q_cols].reshape(2 * rows, heads, HD), cosine, sine).astype(BF)
    queries = queries.reshape(2, rows, kv_heads, repeat, HD)
    keys = rotate(qkv[:, q_cols : q_cols + k_cols].reshape(2 * rows, kv_heads, HD), cosine, sine)
    keys = keys.astype(BF).reshape(2, rows, kv_heads, HD)
    values = qkv[:, q_cols + k_cols :].astype(BF).reshape(2, rows, kv_heads, HD)
    scores = jnp.einsum("bqgrd,bkgd->bgrqk", queries, keys, preferred_element_type=F32) * 0.125
    scores = jnp.where(allowed[:, None], scores, -1e30)
    top = jnp.max(scores, axis=-1, keepdims=True)
    expo = jnp.exp(scores - top)
    totals = jnp.sum(expo, axis=-1, keepdims=True)
    probs = expo / totals
    log_totals = top + jnp.log(totals)
    attended = jnp.einsum("bgrqk,bkgd->bqgrd", probs.astype(BF), values, preferred_element_type=F32)
    attended = attended.astype(BF).reshape(2 * rows, q_cols)

    def sum_quad(partial):
        came = swap(partial[rows:].astype(BF)).astype(F32)
        mine = (partial[:rows] + came).astype(BF)
        return mine.astype(F32) + across(mine).astype(F32)

    w_out = jnp.concatenate(
        [jnp.concatenate(out_one, axis=1), jnp.concatenate(out_two, axis=1)], axis=0
    )
    resid = x_mine.astype(F32) + sum_quad(dot(attended, w_out))
    rstd_two = rms_scale(resid)
    normed_mine = (resid * rstd_two * gain_two).astype(BF)
    normed_two = jnp.concatenate([normed_mine, swap(normed_mine)], axis=0)
    w_gate_full = jnp.concatenate(gate_slots, axis=0)
    w_up_full = jnp.concatenate(up_slots, axis=0)
    gate_value = dot(normed_two, w_gate_full)
    lifted = dot(normed_two, w_up_full)
    sigmoid_gate = jax.nn.sigmoid(gate_value)
    silu_gate = gate_value * sigmoid_gate
    act = (silu_gate * lifted).astype(BF)

    def block_of(field, i):
        return field[:, i * wide : (i + 1) * wide]

    grad_down_one = ring.scatter(lambda i: dot_tn(act[:, :half_units], block_of(dy_all, i)), 1)
    grad_down_two = ring.scatter(lambda i: dot_tn(act[:, half_units:], block_of(dy_all, i)), -1)
    w_down_full = jnp.concatenate(
        [jnp.concatenate(down_one, axis=1), jnp.concatenate(down_two, axis=1)], axis=0
    )
    grad_act = dot_nt(dy_all, w_down_full)
    grad_gate_value = (
        grad_act * lifted * sigmoid_gate * (1.0 + gate_value * (1.0 - sigmoid_gate))
    ).astype(BF)
    grad_lifted = (grad_act * silu_gate).astype(BF)
    partial_two = dot_nt(grad_gate_value, w_gate_full) + dot_nt(grad_lifted, w_up_full)
    grad_normed_two = sum_quad(partial_two)
    grad_gate = ring.scatter(lambda i: dot_tn(block_of(normed_two, i), grad_gate_value), 1)
    grad_up = ring.scatter(lambda i: dot_tn(block_of(normed_two, i), grad_lifted), -1)
    grad_gain_two = jnp.sum(grad_normed_two * resid * rstd_two, axis=0)
    grad_resid = norm_back(resid, rstd_two, gain_two, grad_normed_two) + dy_mine.astype(F32)
    branch_mine = grad_resid.astype(BF)
    grad_branch = jnp.concatenate([branch_mine, swap(branch_mine)], axis=0)

    output = from_ring((resid + sum_quad(dot(act, w_down_full))).astype(BF))

    grad_attended = dot_nt(grad_branch, w_out).astype(BF).reshape(2, rows, kv_heads, repeat, HD)
    half_q = q_cols // 2
    grad_out_one = ring.scatter(lambda i: dot_tn(attended[:, :half_q], block_of(grad_branch, i)), 1)
    grad_out_two = ring.scatter(lambda i: dot_tn(attended[:, half_q:], block_of(grad_branch, i)), -1)
    scores = jnp.einsum("bqgrd,bkgd->bgrqk", queries, keys, preferred_element_type=F32) * 0.125
    scores = jnp.where(allowed[:, None], scores, -1e30)
    probs = jnp.exp(scores - log_totals)
    grad_probs = jnp.einsum("bqgrd,bkgd->bgrqk", grad_attended, values, preferred_element_type=F32)
    inner = jnp.sum(probs * grad_probs, axis=-1, keepdims=True)
    grad_scores = (probs * (grad_probs - inner)).astype(BF)
    grad_queries = jnp.einsum("bgrqk,bkgd->bqgrd", grad_scores, keys, preferred_element_type=F32)
    grad_keys = jnp.einsum("bgrqk,bqgrd->bkgd", grad_scores, queries, preferred_element_type=F32)
    grad_values = jnp.einsum(
        "bgrqk,bqgrd->bkgd", probs.astype(BF), grad_attended, preferred_element_type=F32
    )
    grad_q_lin = rotate(grad_queries.reshape(2 * rows, heads, HD) * 0.125, cosine, -sine)
    grad_k_lin = rotate(grad_keys.reshape(2 * rows, kv_heads, HD) * 0.125, cosine, -sine)
    grad_qkv = jnp.concatenate(
        [
            grad_q_lin.reshape(2 * rows, q_cols),
            grad_k_lin.reshape(2 * rows, k_cols),
            grad_values.reshape(2 * rows, k_cols),
        ],
        axis=1,
    ).astype(BF)
    partial_one = dot_nt(grad_qkv, w_qkv)
    grad_gain_one = jnp.sum(partial_one * inputs * rstd_one, axis=0)

    def with_gains(i):
        main = dot_tn(block_of(normed_one, i), grad_qkv[:, :cut])
        a = grad_gain_one[i * wide : (i + 1) * wide][None]
        b = grad_gain_two[i * wide : (i + 1) * wide][None]
        gain = jnp.concatenate([a, b, jnp.zeros((14, wide), F32)], axis=0)
        gain = jnp.concatenate([gain, jnp.zeros((16, cut - wide), F32)], axis=1)
        return jnp.concatenate([main, gain], axis=0)

    grad_qkv_one = ring.scatter(with_gains, 1)
    grad_qkv_two = ring.scatter(lambda i: dot_tn(block_of(normed_one, i), grad_qkv[:, cut:]), -1)
    grad_normed_one = sum_quad(partial_one)
    grad_inputs = norm_back(inputs[:rows], rstd_one[:rows], gain_one, grad_normed_one)
    grad_tokens = from_ring((grad_resid + grad_inputs).astype(BF))

    def own(field, axis, which):
        return lax.dynamic_slice_in_dim(field, which * part, part, axis)

    def spread(field, axis):
        mine, came = own(field, axis, core), swap(own(field, axis, 1 - core))
        return jnp.where(first, mine, came), jnp.where(first, came, mine)

    qkv_grad = jnp.concatenate([grad_qkv_one[:wide], grad_qkv_two], axis=1)
    low, high = spread(qkv_grad, 0)
    g_query = jnp.concatenate([low[:, :q_cols], high[:, :q_cols]], axis=1)
    g_key = jnp.concatenate(
        [low[:, q_cols : q_cols + k_cols], high[:, q_cols : q_cols + k_cols]], axis=1
    )
    g_value = jnp.concatenate([low[:, q_cols + k_cols :], high[:, q_cols + k_cols :]], axis=1)
    gain_sums = grad_qkv_one[wide : wide + 2, :wide]
    gain_sums = gain_sums[:1], gain_sums[1:]
    g_one = gain_sums[0][0]
    g_two = gain_sums[1][0]
    if tensors > 1:
        g_one = lax.psum(g_one, "tensor")
    g_one = g_one + swap(g_one)
    g_two = g_two + swap(g_two)
    g_one = own(g_one, 0, core)
    g_two = own(g_two, 0, core)
    g_out = jnp.concatenate(spread(jnp.concatenate([grad_out_one, grad_out_two], axis=0), 1), axis=0)
    g_gate = jnp.concatenate(spread(grad_gate, 0), axis=1)
    g_up = jnp.concatenate(spread(grad_up, 0), axis=1)
    g_down = jnp.concatenate(spread(jnp.concatenate([grad_down_one, grad_down_two], axis=0), 1), axis=0)
    return output, grad_tokens, g_one, g_query, g_key, g_value, g_out, g_two, g_gate, g_up, g_down


def solution(mesh):
    shape = (mesh.shape["dp"], mesh.shape["tensor"])
    weight_in, weight_out = P("dp", "tensor"), P("tensor", "dp")
    in_specs = (
        P("dp", None),
        P("dp"),
        P("dp"),
        weight_in,
        weight_in,
        weight_in,
        weight_out,
        P("dp"),
        weight_in,
        weight_in,
        weight_out,
        P("dp", None),
    )
    out_specs = (
        P("dp", None),
        P("dp", None),
        P("dp"),
        weight_in,
        weight_in,
        weight_in,
        weight_out,
        P("dp"),
        weight_in,
        weight_in,
        weight_out,
    )

    def whole(*arguments):
        return per_device(shape, *arguments)

    return jax.shard_map(whole, mesh=mesh, in_specs=in_specs, out_specs=out_specs, check_vma=False)
```

```python
import functools
import math

import jax
import jax.numpy as jnp
from jax import lax
from jax.experimental import pallas as pl
from jax.experimental.pallas import tpu as pltpu
from jax.sharding import PartitionSpec as P

HD = 64
EPSILON = 1e-05
BF = jnp.bfloat16
F32 = jnp.float32
TILE = 256
PIECES = 4


def rms_scale(values):
    return lax.rsqrt(jnp.mean(values * values, axis=-1, keepdims=True) + EPSILON)


def norm_back(resid, rstd, gain, grad_normed):
    scaled = gain * grad_normed
    inner = jnp.mean(scaled * resid, axis=-1, keepdims=True)
    return rstd * scaled - resid * (rstd * rstd * rstd) * inner


def dot(a, b):
    return jnp.dot(a, b, preferred_element_type=F32)


def dot_tn(a, b):
    return lax.dot_general(a, b, (((0,), (0,)), ((), ())), preferred_element_type=F32)


def dot_nt(a, b):
    return lax.dot_general(a, b, (((1,), (1,)), ((), ())), preferred_element_type=F32)


def call(body, name, out_shape, grid, in_specs, out_specs, scratch=(), prefetch=0, mib=24):
    spec = pltpu.PrefetchScalarGridSpec(
        num_scalar_prefetch=prefetch,
        grid=grid,
        in_specs=in_specs,
        out_specs=out_specs,
        scratch_shapes=list(scratch),
    )
    return pl.pallas_call(
        body,
        out_shape=out_shape,
        grid_spec=spec,
        name=name,
        compiler_params=pltpu.CompilerParams(
            vmem_limit_bytes=mib * 2**20, dimension_semantics=("arbitrary",) * len(grid)
        ),
        cost_estimate=pl.CostEstimate(flops=0, bytes_accessed=0, transcendentals=0),
    )


def struct(shape, dtype):
    return jax.ShapeDtypeStruct(shape, dtype)


def tiles(width, offset=0):
    return pl.BlockSpec((TILE, width), lambda i, *_: (i + offset, 0))


def whole(shape):
    return pl.BlockSpec(shape, lambda *_: (0,) * len(shape), pipeline_mode=pl.Buffered(1))


ANY = pl.BlockSpec(memory_space=pl.ANY)


class Slots:
    def __init__(self, parts, step):
        self.parts = parts
        self.step = step
        self.shape = (len(parts) * step, sum(p.shape[1] for p in parts[0]))

    def flat(self):
        return [p for pieces in self.parts for p in pieces]

    def scratch(self):
        return [pltpu.VMEM(self.shape, BF), pltpu.SemaphoreType.DMA((len(self.flat()),))]

    def copies(self, refs, buffer, sem):
        found, k = [], 0
        for i, pieces in enumerate(self.parts):
            at, mine = 0, []
            for piece in pieces:
                source, cols = refs[k], piece.shape[1]
                if piece.shape[0] != self.step:
                    source = source.at[pl.ds(0, self.step), :]
                target = buffer.at[pl.ds(i * self.step, self.step), pl.ds(at, cols)]
                mine.append(pltpu.make_async_copy(source, target, sem.at[k]))
                at += cols
                k += 1
            found.append(mine)
        return found


def product_as_it_comes(x, copies, buffer, step):
    for pieces in copies:
        for copy in pieces:
            copy.start()
    total = None
    group = max(1, 512 // step)
    for i in range(0, len(copies), group):
        for pieces in copies[i : i + group]:
            for copy in pieces:
                copy.wait()
        rows = slice(i * step, min(i + group, len(copies)) * step)
        term = dot(x[:, rows], buffer[rows])
        total = term if total is None else total + term
    return total


def lane_blocks(width, wide):
    return [slice(i * wide, (i + 1) * wide) for i in range(width // wide)]


def to_ring(mine, theirs, order, wide):
    rows, depth = mine.shape
    n = depth // wide
    if wide % 128 or rows % TILE:
        both = jnp.concatenate([mine, theirs], axis=0)
        return jnp.take(both.reshape(2 * rows, n, wide), order, axis=1).reshape(2 * rows, depth)
    half = rows // TILE

    def body(order_ref, mine_ref, theirs_ref, out_ref):
        def put(ref):
            for i, block in enumerate(lane_blocks(depth, wide)):
                out_ref[:, block] = ref[:, pl.ds(pl.multiple_of(order_ref[i] * wide, wide), wide)]

        @pl.when(pl.program_id(0) < half)
        def _():
            put(mine_ref)

        @pl.when(pl.program_id(0) >= half)
        def _():
            put(theirs_ref)

    return call(
        body,
        "to_ring",
        struct((2 * rows, depth), mine.dtype),
        (2 * half,),
        [
            pl.BlockSpec((TILE, depth), lambda i, o: (jnp.minimum(i, half - 1), 0)),
            pl.BlockSpec((TILE, depth), lambda i, o: (jnp.maximum(i - half, 0), 0)),
        ],
        pl.BlockSpec((TILE, depth), lambda i, o: (i, 0)),
        prefetch=1,
        mib=12,
    )(order, mine, theirs)


def rope(block, cosine, sine):
    lane = lax.broadcasted_iota(jnp.int32, block.shape, 1)
    low = lane % HD < HD // 2
    other = jnp.where(low, pltpu.roll(block, 128 - HD // 2, 1), pltpu.roll(block, HD // 2, 1))
    return block * cosine + other * sine


def rope_kv(block, cosine, sine):
    lane = lax.broadcasted_iota(jnp.int32, block.shape, 1)
    return jnp.where(lane < HD, rope(block, cosine, sine), block)


def qkv_forward(x, gain, slots, cosine, sine):
    rows, depth = x.shape
    width = slots.shape[1]
    arrays = slots.flat()

    def body(x_ref, gain_ref, cos_ref, sin_ref, *refs):
        weights, (normed_ref, q_ref, kv_ref), (buffer, sem, qkv_ref) = (
            refs[: len(arrays)],
            refs[len(arrays) : -3],
            refs[-3:],
        )
        field = x_ref[...].astype(F32)
        normed = (field * rms_scale(field) * gain_ref[...]).astype(BF)
        normed_ref[...] = normed

        @pl.when(pl.program_id(0) == 0)
        def _():
            copies = slots.copies(weights, buffer, sem)
            qkv_ref[...] = product_as_it_comes(normed, copies, buffer, slots.step)

        @pl.when(pl.program_id(0) > 0)
        def _():
            qkv_ref[...] = dot(normed, buffer[...])

        cosv, sinv = cos_ref[...], sin_ref[...]
        for block in lane_blocks(width - 128, 128):
            q_ref[:, block] = rope(qkv_ref[:, block], cosv, sinv).astype(BF)
        kv_ref[...] = rope_kv(qkv_ref[:, width - 128 :], cosv, sinv).astype(BF)

    return call(
        body,
        "qkv_forward",
        [
            struct((rows, depth), BF),
            struct((rows, width - 128), BF),
            struct((rows, 128), BF),
        ],
        (rows // TILE,),
        [tiles(depth), whole((1, depth)), tiles(128), tiles(128)] + [ANY] * len(arrays),
        [tiles(depth), tiles(width - 128), tiles(128)],
        slots.scratch() + [pltpu.VMEM((TILE, width), F32)],
        mib=20,
    )(x, gain, cosine, sine, *arrays)


def masks(seg_row, seg_col, rows, begin, finish):
    key = lax.broadcasted_iota(jnp.int32, (finish, finish - begin), 0)
    query = lax.broadcasted_iota(jnp.int32, (finish, finish - begin), 1) + begin
    return (seg_col[:finish] == seg_row[:, begin:finish]) & (key <= query)


def query_blocks(rows):
    half = rows // 2
    return [(0, half), (half, rows)] if half % 128 == 0 else [(0, rows)]


def attention_forward(q, kv, seg_row, seg_col, rows):
    width = q.shape[1]
    heads = width // HD
    groups = q.shape[0] // rows

    def body(q_ref, kv_ref, row_ref, col_ref, out_ref, lse_ref, turned):
        keys = kv_ref[:, :HD]
        values = kv_ref[...].astype(F32).T[HD:].astype(BF)
        for begin, finish in query_blocks(rows):
            allowed = masks(row_ref[0], col_ref[0], rows, begin, finish)
            for h in range(heads):
                scores = dot_nt(keys[:finish], q_ref[begin:finish, h * HD : (h + 1) * HD]) * 0.125
                scores = jnp.where(allowed, scores, -1e30)
                top = jnp.max(scores, axis=0, keepdims=True)
                expo = jnp.exp(scores - top)
                total = jnp.sum(expo, axis=0, keepdims=True)
                probs = (expo * (1.0 / total)).astype(BF)
                turned[h * HD : (h + 1) * HD, begin:finish] = dot(values[:, :finish], probs)
                lse_ref[0, h : h + 1, begin:finish] = top + jnp.log(total)
        out_ref[...] = turned[...].T.astype(BF)

    return call(
        body,
        "attention_forward",
        [struct(q.shape, BF), struct((groups, heads, rows), F32)],
        (groups,),
        [
            pl.BlockSpec((rows, width), lambda i: (i, 0)),
            pl.BlockSpec((rows, 128), lambda i: (i, 0)),
            pl.BlockSpec((1, 1, rows), lambda i: (i, 0, 0)),
            pl.BlockSpec((1, rows, 1), lambda i: (i, 0, 0)),
        ],
        [
            pl.BlockSpec((rows, width), lambda i: (i, 0)),
            pl.BlockSpec((1, heads, rows), lambda i: (i, 0, 0)),
        ],
        [pltpu.VMEM((width, rows), F32)],
        mib=16,
    )(q, kv, seg_row, seg_col)


def attention_backward(q, kv, grad, lse, seg_row, seg_col, cosine, sine, rows):
    width = q.shape[1]
    heads = width // HD
    groups = q.shape[0] // rows

    def body(q_ref, kv_ref, grad_ref, lse_ref, row_ref, col_ref, cos_ref, sin_ref, out_ref, turned, total_k, total_v):
        keys = kv_ref[:, :HD]
        values = kv_ref[:, HD:]
        keys_t = kv_ref[...].astype(F32).T[:HD].astype(BF)
        total_k[...] = jnp.zeros_like(total_k)
        total_v[...] = jnp.zeros_like(total_v)
        for begin, finish in query_blocks(rows):
            allowed = masks(row_ref[0], col_ref[0], rows, begin, finish)
            for h in range(heads):
                head = slice(h * HD, (h + 1) * HD)
                query, grads = q_ref[begin:finish, head], grad_ref[begin:finish, head]
                scores = dot_nt(keys[:finish], query) * 0.125
                scores = jnp.where(allowed, scores, -1e30)
                probs = jnp.exp(scores - lse_ref[0, h : h + 1, begin:finish])
                grad_probs = dot_nt(values[:finish], grads)
                inner = jnp.sum(probs * grad_probs, axis=0, keepdims=True)
                grad_scores = (probs * (grad_probs - inner)).astype(BF)
                turned[head, begin:finish] = dot(keys_t[:, :finish], grad_scores)
                total_k[:finish] += dot(grad_scores, query)
                total_v[:finish] += dot(probs.astype(BF), grads)
        cosv, sinv = cos_ref[...], -sin_ref[...]
        grad_q = turned[...].T * 0.125
        for block in lane_blocks(width, 128):
            out_ref[:, block] = rope(grad_q[:, block], cosv, sinv).astype(BF)
        grad_kv = jnp.concatenate([total_k[...] * 0.125, total_v[...]], axis=1)
        out_ref[:, width:] = rope_kv(grad_kv, cosv, sinv).astype(BF)

    group = lambda w: pl.BlockSpec((rows, w), lambda i: (i, 0))
    return call(
        body,
        "attention_backward",
        struct((q.shape[0], width + 128), BF),
        (groups,),
        [
            group(width),
            group(128),
            group(width),
            pl.BlockSpec((1, heads, rows), lambda i: (i, 0, 0)),
            pl.BlockSpec((1, 1, rows), lambda i: (i, 0, 0)),
            pl.BlockSpec((1, rows, 1), lambda i: (i, 0, 0)),
            group(128),
            group(128),
        ],
        group(width + 128),
        [pltpu.VMEM((width, rows), F32), pltpu.VMEM((rows, HD), F32), pltpu.VMEM((rows, HD), F32)],
        mib=20,
    )(q, kv, grad, lse, seg_row, seg_col, cosine, sine)


def project(lefts, slots, rows, name):
    depth = slots[0].shape[0]
    cols = min(256, depth)
    per = cols // slots[0].step
    counts = [len(s.flat()) for s in slots]
    arrays = [b for s in slots for b in s.flat()]
    k, a = len(lefts), len(arrays)

    def body(*refs):
        left_refs, weights, out_refs = refs[:k], refs[k:][:a], refs[k + a :][: 1 + PIECES]
        scratch = refs[k + a + 1 + PIECES :]
        step = pl.program_id(0)
        copies, at = [], 0
        for j, (s, count) in enumerate(zip(slots, counts)):
            copies.append(s.copies(weights[at : at + count], scratch[2 * j], scratch[2 * j + 1]))
            at += count

        @pl.when(step == 0)
        def _():
            for i in range(len(copies[0])):
                for chain in copies:
                    for copy in chain[i]:
                        copy.start()

        for i in range(len(copies[0])):

            @pl.when(step == i // per)
            def _():
                for chain in copies:
                    for copy in chain[i]:
                        copy.wait()

        total = None
        block = pl.ds(pl.multiple_of(step * cols, cols), cols)
        for j in range(k):
            term = dot_nt(left_refs[j][...], scratch[2 * j][block, :])
            total = term if total is None else total + term
        out_refs[0][...] = total[:rows].astype(BF)
        for j in range(PIECES):
            out_refs[1 + j][...] = total[rows + j * piece : rows + (j + 1) * piece].astype(BF)

    piece = rows // PIECES
    column = lambda r: pl.BlockSpec((r, cols), lambda i: (0, i))
    mine, *theirs = call(
        body,
        name,
        [struct((rows, depth), BF)] + [struct((piece, depth), BF)] * PIECES,
        (depth // cols,),
        [whole((2 * rows, left.shape[1])) for left in lefts] + [ANY] * a,
        [column(rows)] + [column(piece)] * PIECES,
        [x for s in slots for x in s.scratch()],
        mib=28,
    )(*lefts, *arrays)
    return mine, theirs


def both_tiles(width, half):
    return [
        pl.BlockSpec((TILE, width // PIECES), lambda i, *_: (jnp.minimum(i, half - 1), 0))
    ] * PIECES + [
        pl.BlockSpec((TILE, width // PIECES), lambda i, *_: (jnp.maximum(i - half, 0), 0))
    ] * PIECES


def pick(half, refs):
    mine = pl.program_id(0) < half
    return jnp.concatenate(
        [jnp.where(mine, a[...], b[...]) for a, b in zip(refs[:PIECES], refs[PIECES:])], axis=1
    )


def join_cores(mine, came):
    rows, depth = mine.shape
    piece = rows // PIECES

    def body(mine_ref, *refs):
        for j in range(PIECES):
            part = slice(j * piece, (j + 1) * piece)
            total = mine_ref[part].astype(F32) + refs[j][...].astype(F32)
            refs[-1][part] = total.astype(BF)

    half = depth // 2
    return call(
        body,
        "join_cores",
        struct((rows, depth), BF),
        (2,),
        [pl.BlockSpec((rows, half), lambda i: (0, i))]
        + [pl.BlockSpec((piece, half), lambda i: (0, i))] * PIECES,
        pl.BlockSpec((rows, half), lambda i: (0, i)),
        mib=12,
    )(mine, *came)


def mixer_forward(mine, theirs, gate, up):
    rows, depth = mine[0].shape[0], gate.shape[0]
    units = gate.shape[1]
    half = rows // TILE
    arrays = gate.flat() + up.flat()
    g = len(gate.flat())

    def body(*refs):
        x_refs, refs = refs[: 2 * PIECES], refs[2 * PIECES :]
        weights, (gate_ref, lifted_ref, act_ref, both_ref), scratch = (
            refs[: len(arrays)],
            refs[len(arrays) : len(arrays) + 4],
            refs[len(arrays) + 4 :],
        )
        x = pick(half, x_refs)
        both_ref[...] = x

        @pl.when(pl.program_id(0) == 0)
        def _():
            one = gate.copies(weights[:g], scratch[0], scratch[1])
            two = up.copies(weights[g:], scratch[2], scratch[3])
            for pieces in two:
                for copy in pieces:
                    copy.start()
            gate_ref[...] = product_as_it_comes(x, one, scratch[0], gate.step)
            for pieces in two:
                for copy in pieces:
                    copy.wait()

        @pl.when(pl.program_id(0) > 0)
        def _():
            gate_ref[...] = dot(x, scratch[0][...])

        lifted = dot(x, scratch[2][...])
        lifted_ref[...] = lifted
        gate_value = gate_ref[...]
        act_ref[...] = (gate_value * jax.nn.sigmoid(gate_value) * lifted).astype(BF)

    shape = (2 * rows, units)
    return call(
        body,
        "mixer_forward",
        [struct(shape, F32), struct(shape, F32), struct(shape, BF), struct((2 * rows, depth), BF)],
        (2 * half,),
        both_tiles(depth, half) + [ANY] * len(arrays),
        [tiles(units)] * 3 + [tiles(depth)],
        gate.scratch() + up.scratch(),
        mib=36,
    )(*mine, *theirs, *arrays)


def mixer_backward(dy, down, gate_value, lifted):
    rows, depth = dy.shape
    units = down.shape[1]
    arrays = down.flat()

    def body(dy_ref, gate_ref, lifted_ref, *refs):
        weights, (grad_gate_ref, grad_lifted_ref), (buffer, sem, act_ref) = (
            refs[: len(arrays)],
            refs[len(arrays) : -3],
            refs[-3:],
        )

        @pl.when(pl.program_id(0) == 0)
        def _():
            copies = down.copies(weights, buffer, sem)
            act_ref[...] = product_as_it_comes(dy_ref, copies, buffer, down.step)

        @pl.when(pl.program_id(0) > 0)
        def _():
            act_ref[...] = dot(dy_ref[...], buffer[...])

        grad_act, gate_value = act_ref[...], gate_ref[...]
        s = jax.nn.sigmoid(gate_value)
        grad_lifted_ref[...] = (grad_act * (gate_value * s)).astype(BF)
        grad_gate_ref[...] = (
            grad_act * lifted_ref[...] * s * (1.0 + gate_value * (1.0 - s))
        ).astype(BF)

    return call(
        body,
        "mixer_backward",
        [struct((rows, units), BF)] * 2,
        (rows // TILE,),
        [tiles(depth), tiles(units), tiles(units)] + [ANY] * len(arrays),
        [tiles(units)] * 2,
        down.scratch() + [pltpu.VMEM((TILE, units), F32)],
        mib=28,
    )(dy, gate_value, lifted, *arrays)


def attended_backward(mine, theirs, out):
    rows, depth = mine[0].shape[0], out.shape[0]
    width = out.shape[1]
    half = rows // TILE
    arrays = out.flat()

    def body(*refs):
        x_refs, refs = refs[: 2 * PIECES], refs[2 * PIECES :]
        weights, (grad_ref, both_ref), (buffer, sem) = (
            refs[: len(arrays)],
            refs[len(arrays) : -2],
            refs[-2:],
        )
        x = pick(half, x_refs)
        both_ref[...] = x

        @pl.when(pl.program_id(0) == 0)
        def _():
            copies = out.copies(weights, buffer, sem)
            grad_ref[...] = product_as_it_comes(x, copies, buffer, out.step).astype(BF)

        @pl.when(pl.program_id(0) > 0)
        def _():
            grad_ref[...] = dot(x, buffer[...]).astype(BF)

    return call(
        body,
        "attended_backward",
        [struct((2 * rows, width), BF), struct((2 * rows, depth), BF)],
        (2 * half,),
        both_tiles(depth, half) + [ANY] * len(arrays),
        [tiles(width), tiles(depth)],
        out.scratch(),
        mib=16,
    )(*mine, *theirs, *arrays)


def norm_forward(x, mine, other, gain, rows):
    depth = x.shape[1]

    def body(x_ref, mine_ref, other_ref, gain_ref, resid_ref, *normed_refs):
        resid = x_ref[...].astype(F32) + (mine_ref[...].astype(F32) + other_ref[...].astype(F32))
        resid_ref[...] = resid
        normed = (resid * rms_scale(resid) * gain_ref[...]).astype(BF)
        for ref, block in zip(normed_refs, lane_blocks(depth, depth // PIECES)):
            ref[...] = normed[:, block]

    resid, *normed = call(
        body,
        "norm_forward",
        [struct((rows, depth), F32)] + [struct((rows, depth // PIECES), BF)] * PIECES,
        (rows // TILE,),
        [tiles(depth), tiles(depth), tiles(depth), whole((1, depth))],
        [tiles(depth)] + [tiles(depth // PIECES)] * PIECES,
        mib=22,
    )(x, mine, other, gain)
    return resid, normed


def norm_backward(resid, mine, other, dy, gain, rows):
    depth = dy.shape[1]

    def body(resid_ref, mine_ref, other_ref, dy_ref, gain_ref, grad_ref, *branch_refs):
        resid = resid_ref[...]
        grad_normed = mine_ref[...].astype(F32) + other_ref[...].astype(F32)
        rstd = rms_scale(resid)
        grad = norm_back(resid, rstd, gain_ref[...], grad_normed) + dy_ref[...].astype(F32)
        grad_ref[...] = grad
        for ref, block in zip(branch_refs, lane_blocks(depth, depth // PIECES)):
            ref[...] = grad[:, block].astype(BF)

    grad_resid, *branch = call(
        body,
        "norm_backward",
        [struct((rows, depth), F32)] + [struct((rows, depth // PIECES), BF)] * PIECES,
        (rows // TILE,),
        [tiles(depth)] * 4 + [whole((1, depth))],
        [tiles(depth)] + [tiles(depth // PIECES)] * PIECES,
        mib=28,
    )(resid, mine, other, dy, gain)
    return grad_resid, branch


def leave_ring(fn, arrays, gain, order, wide, rows, name):
    depth = arrays[0].shape[1]
    n = depth // wide
    if wide % 128 or rows % TILE:
        field = fn(*[a[:rows] for a in arrays], gain).astype(BF)
        back = jnp.zeros((n,), jnp.int32).at[order].set(jnp.arange(n, dtype=jnp.int32))
        return jnp.take(field.reshape(rows, n, wide), back, axis=1).reshape(rows, depth)
    k = len(arrays)

    def body(order_ref, *refs):
        field = fn(*[r[...] for r in refs[:k]], refs[k][...]).astype(BF)
        for i, block in enumerate(lane_blocks(depth, wide)):
            refs[k + 1][:, pl.ds(pl.multiple_of(order_ref[i] * wide, wide), wide)] = field[:, block]

    return call(
        body,
        name,
        struct((rows, depth), BF),
        (rows // TILE,),
        [tiles(depth)] * k + [whole((1, depth))],
        tiles(depth),
        prefetch=1,
        mib=32,
    )(order, *arrays, gain)


def after(value, *others):
    return lax.optimization_barrier((value,) + others)[0]


class Ring:
    def __init__(self, devices):
        self.n = devices // 2
        n = self.n
        order = list(range(0, n, 2)) + list(range(n - 1 - n % 2, 0, -2))
        self.order = order
        place = [0] * n
        for position, chip in enumerate(order):
            place[chip] = position
        self.place = place
        self.steps = {1: [], -1: []}
        for position, chip in enumerate(order):
            then = order[(position + 1) % n]
            for core in (0, 1):
                self.steps[1].append((2 * chip + core, 2 * then + core))
                self.steps[-1].append((2 * then + core, 2 * chip + core))
        self.cores = [(i, i ^ 1) for i in range(devices)]
        self.hops = n // 2

    def pass_on(self, block, way):
        return lax.ppermute(block, "dp", self.steps[way])

    def halves(self, width):
        cut = min(width, (width // 2 + 127) // 128 * 128)
        return slice(0, cut), slice(cut, width)

    def swap(self, block):
        return lax.ppermute(block, "dp", self.cores)


class Gather:
    def __init__(self, ring, block):
        self.ring, self.hop = ring, 0
        self.found = [[block]] + [None] * (ring.n - 1)
        self.last = (block,)

    def step(self, *others):
        ring, n = self.ring, self.ring.n
        self.hop += 1
        hop = self.hop
        if 2 * hop > n:
            return
        before = [self.found[(hop - 1) * way % n][0] for way in (1, -1)]
        if others:
            before = [after(b, *others) for b in before]
        if 2 * hop < n:
            for way, block in zip((1, -1), before):
                self.found[hop * way % n] = [ring.pass_on(block, way)]
            self.last = tuple(self.found[hop * way % n][0] for way in (1, -1))
        else:
            parts = ring.halves(before[0].shape[1])
            self.found[hop] = [
                ring.pass_on(b[:, part], way) for b, way, part in zip(before, (1, -1), parts)
            ]
            self.last = tuple(self.found[hop])

    def finish(self):
        while 2 * (self.hop + 1) <= self.ring.n:
            self.step()
        return self.found


class Line:
    def __init__(self):
        self.marks = ()

    def after(self, value):
        return after(value, *self.marks) if self.marks else value

    def mark(self, *found):
        self.marks = found

    def wait(self, *found):
        self.marks = self.marks + found


class Scatter:
    def __init__(self, ring, line, field, grads):
        self.ring, self.line, self.field, self.grads = ring, line, field, grads
        self.width, self.hop = grads.shape[1], 0
        self.wide = field.shape[1] // ring.n
        self.held = {1: None, -1: None}
        self.last = ()

    def term(self, i, part):
        field = self.line.after(self.field)
        return dot_tn(field[:, i * self.wide : (i + 1) * self.wide], self.grads[:, part])

    def step(self):
        ring, n = self.ring, self.ring.n
        far = n // 2 - self.hop
        if far == 0:
            return
        self.hop += 1
        for way, part in zip((1, -1), ring.halves(self.width)):
            if 2 * far == n:
                total = self.term(far, part)
            else:
                part = slice(0, self.width)
                total = self.term(-far * way % n, part) + self.came(way)
            total = total.astype(BF)
            self.line.mark(total)
            self.held[way] = (ring.pass_on(total, way), part)
        self.last = tuple(self.held[way][0] for way in (1, -1))

    def came(self, way):
        if self.held[way] is None:
            return 0.0
        came, part = self.held[way]
        edges = ((0, 0, 0), (part.start, self.width - part.stop, 0))
        return lax.pad(came.astype(F32), jnp.zeros((), F32), edges)

    def finish(self):
        while self.hop < self.ring.n // 2:
            self.step()
        total = self.term(0, slice(0, self.width)) + self.came(1) + self.came(-1)
        self.line.mark(total)
        return total


def per_device(
    shape,
    tokens,
    segments,
    gain_attend,
    w_query,
    w_key,
    w_value,
    w_output,
    gain_mixer,
    w_gate,
    w_up,
    w_down,
    cotangent,
):
    devices, tensors = shape
    ring = Ring(devices)
    swap = ring.swap
    n = ring.n
    rows, depth = tokens.shape
    part = depth // devices
    wide = 2 * part
    index = lax.axis_index("dp")
    core = index % 2
    first = core == 0
    position = jnp.asarray(ring.place, jnp.int32)[index // 2]
    blocks = jnp.asarray(ring.order, jnp.int32)[(position - jnp.arange(n, dtype=jnp.int32)) % n]

    def across(block):
        if tensors == 1:
            return jnp.zeros_like(block)
        return lax.ppermute(block, "tensor", [(i, i ^ 1) for i in range(tensors)])

    def cols(w, half):
        return lax.dynamic_slice_in_dim(w, half * (w.shape[1] // 2), w.shape[1] // 2, 1)

    def paired(cut):
        mine, came = cut(core), swap(cut(1 - core))
        return jnp.where(first, mine, came), jnp.where(first, came, mine)

    line = Line()

    q_cols = w_query.shape[1] // 2
    k_cols = w_key.shape[1] // 2
    all_cols = q_cols + 2 * k_cols
    gains = jnp.zeros((16, all_cols), BF)
    gains = gains.at[0, :part].set(gain_attend).at[1, :part].set(gain_mixer)

    def qkv_cut(half):
        main = jnp.concatenate([cols(w_query, half), cols(w_key, half), cols(w_value, half)], axis=1)
        return jnp.concatenate([main, gains], axis=0)

    low, high = paired(qkv_cut)
    gain_rows = jnp.concatenate(
        [low[part:, :part], high[part:, :part], jnp.zeros((16, all_cols - wide), BF)], axis=1
    )
    qkv_block = jnp.concatenate([low[:part], high[:part], gain_rows])
    ring_q = Gather(ring, qkv_block)
    ring_q.step()
    out_block = jnp.concatenate(paired(lambda half: cols(after(w_output, qkv_block).T, half)))
    ring_o = Gather(ring, out_block)
    ring_o.step()

    x = to_ring(after(tokens, out_block), swap(after(tokens, out_block)), blocks, wide)
    line.mark(x, *ring_q.last)
    ring_q.step()
    w_gate = line.after(w_gate)
    gate_block = jnp.concatenate(paired(lambda half: cols(w_gate, half)))
    line.mark(gate_block, *ring_o.last)
    ring_o.step()
    w_up = line.after(w_up)
    up_block = jnp.concatenate(paired(lambda half: cols(w_up, half)))
    line.mark(up_block, *ring_q.last)
    ring_q.step()
    w_down = line.after(w_down)
    down_block = jnp.concatenate(paired(lambda half: cols(w_down.T, half)))
    line.mark(down_block, *ring_o.last)
    ring_o.step()
    cotangent = line.after(cotangent)
    dy = to_ring(cotangent, swap(cotangent), blocks, wide)
    line.mark(dy)
    ring_g, ring_u, ring_d = (Gather(ring, b) for b in (gate_block, up_block, down_block))

    segs = jnp.stack([segments, swap(segments)])
    places = jnp.arange(rows, dtype=jnp.int32)
    fresh = jnp.concatenate([jnp.ones((2, 1), dtype=bool), segs[:, 1:] != segs[:, :-1]], axis=1)
    starts = lax.cummax(jnp.where(fresh, places, 0), axis=1)
    lanes = jnp.arange(128, dtype=jnp.int32)
    freqs = jnp.exp((lanes % (HD // 2)).astype(F32) * (-2.0 * math.log(10000.0) / HD))
    angle = (places - starts).astype(F32).reshape(2 * rows, 1) * freqs[None, :]
    cosine = jnp.cos(angle)
    sine = jnp.sin(angle) * jnp.where(lanes % HD < HD // 2, -1.0, 1.0)
    seg_row, seg_col = segs.reshape(2, 1, rows), segs.reshape(2, rows, 1)

    early = ring_q.last + ring_o.last
    qkv_parts = ring_q.finish()
    w_out = Slots(ring_o.finish(), wide)
    w_qkv = Slots(qkv_parts, wide)
    ring_g.step(*early)
    ring_u.step(*early)

    def gain_of(row):
        return jnp.concatenate(
            [p[0][wide + row : wide + row + 1, :wide] for p in qkv_parts], axis=1
        ).astype(F32)

    gain_one, gain_two = gain_of(0), gain_of(1)

    def swap_all(pieces):
        return [swap(piece) for piece in pieces]

    def joined(mine, came):
        mine = join_cores(line.after(mine), came)
        line.mark(mine)
        return mine

    normed_one, queries, kv = qkv_forward(line.after(x), gain_one, w_qkv, cosine, sine)
    line.mark(normed_one, *ring_g.last)
    ring_g.step()
    attended, lse = attention_forward(line.after(queries), kv, seg_row, seg_col, rows)
    line.mark(attended, *ring_u.last)
    mine, theirs = project([line.after(attended)], [w_out], rows, "attended_out")
    line.mark(mine, *ring_g.last)
    mine = joined(mine, swap_all(theirs))
    other = across(mine)
    ring_u.step(mine)
    ring_g.step(mine)
    line.wait(*ring_u.last)
    ring_u.step()
    line.wait(*ring_g.last)
    ring_g.step()
    line.wait(*ring_u.last)
    late = ring_g.last + ring_u.last
    gate, up = Slots(ring_g.finish(), wide), Slots(ring_u.finish(), wide)
    ring_d.step(*late[2:])
    resid, normed_mine = norm_forward(x, line.after(mine), other, gain_two, rows)
    line.mark(resid)
    came = swap_all(normed_mine)
    normed_mine[0] = line.after(normed_mine[0])
    gate_value, lifted, act, normed_two = mixer_forward(normed_mine, came, gate, up)
    line.mark(act)

    grad_down = Scatter(ring, line, dy, act)
    ring_d.step()
    grad_down.step()
    line.wait(*ring_d.last)
    ring_d.step()
    grad_down.step()
    line.wait(*ring_d.last)
    down = Slots(ring_d.finish(), wide)
    grad_down.step()
    line.wait(*ring_d.last)
    grad_gate_value, grad_lifted = mixer_backward(line.after(dy), down, gate_value, lifted)
    line.mark(grad_lifted)
    grad_down.step()
    grad_gate = Scatter(ring, line, normed_two, grad_gate_value)
    grad_up = Scatter(ring, line, normed_two, grad_lifted)
    grad_gate.step()
    grad_up.step()
    mine, theirs = project(
        [line.after(grad_gate_value), grad_lifted], [gate, up], rows, "grad_normed_two"
    )
    line.mark(mine, *grad_down.last, *grad_gate.last, *grad_up.last)
    came = swap_all(theirs)
    grad_gate.step()
    mine = joined(mine, came)
    other = across(mine)
    grad_up.step()
    out_mine, out_theirs = project([line.after(act)], [down], rows, "act_out")
    line.mark(out_mine, *grad_gate.last)
    came = swap_all(out_theirs)
    grad_gate.step()
    out_mine = joined(out_mine, came)
    down_sum = grad_down.finish()
    grad_up.step()
    line.wait(other)
    grad_resid, branch_mine = norm_backward(line.after(resid), mine, other, dy, gain_two, rows)
    line.mark(grad_resid, *grad_gate.last)
    came = swap_all(branch_mine)
    out_other = across(after(out_mine, grad_resid))
    grad_gate.step()
    branch_mine[0] = line.after(branch_mine[0])
    grad_attended, grad_branch = attended_backward(branch_mine, came, w_out)
    line.mark(grad_attended)
    grad_qkv = attention_backward(
        line.after(queries), kv, grad_attended, lse, seg_row, seg_col, cosine, sine, rows
    )
    line.mark(grad_qkv, *grad_up.last)
    grad_up.step()
    grad_out = Scatter(ring, line, grad_branch, attended)
    grad_out.step()
    mine, theirs = project([line.after(grad_qkv)], [w_qkv], rows, "grad_normed_one")
    line.mark(mine, *grad_gate.last)
    came = swap_all(theirs)
    grad_projections = Scatter(ring, line, normed_one, grad_qkv)
    grad_projections.step()
    mine = joined(mine, came)
    other = across(mine)
    gate_sum = grad_gate.finish()
    grad_out.step()
    grad_projections.step()
    up_sum = grad_up.finish()
    grad_out.step()
    grad_projections.step()
    grad_out.step()
    grad_projections.step()
    out_sum = grad_out.finish()

    output = leave_ring(
        lambda r, m, o, _: r + (m.astype(F32) + o.astype(F32)),
        [line.after(resid), out_mine, out_other],
        gain_two,
        blocks,
        wide,
        rows,
        "leave_output",
    )
    line.mark(output)

    def leave(mine, other, x, grad_resid, gain):
        x = x.astype(F32)
        grad_normed = mine.astype(F32) + other.astype(F32)
        return grad_resid + norm_back(x, rms_scale(x), gain, grad_normed)

    def own(field, axis, which):
        return lax.dynamic_slice_in_dim(field, which * part, part, axis)

    def spread(field):
        mine, came = own(field, 0, core), swap(own(field, 0, 1 - core))
        return jnp.where(first, mine, came), jnp.where(first, came, mine)

    g_gate = jnp.concatenate(spread(line.after(gate_sum)), axis=1)
    g_up = jnp.concatenate(spread(line.after(up_sum)), axis=1)
    g_down = jnp.concatenate(spread(line.after(down_sum)), axis=1).T
    g_out = jnp.concatenate(spread(line.after(out_sum)), axis=1).T

    def gain_grad(pairs, gain):
        total = sum(jnp.sum(w.astype(F32) * g, axis=1) for w, g in pairs)
        return (total + across(total)) / gain.astype(F32)

    g_two = gain_grad([(w_gate, g_gate), (w_up, g_up)], gain_mixer)
    low, high = spread(grad_projections.finish())

    def sides(begin, finish):
        return jnp.concatenate([low[:, begin:finish], high[:, begin:finish]], axis=1)

    g_query = sides(0, q_cols)
    g_key = sides(q_cols, q_cols + k_cols)
    g_value = sides(q_cols + k_cols, all_cols)
    g_one = gain_grad([(w_query, g_query), (w_key, g_key), (w_value, g_value)], gain_attend)
    grad_tokens = leave_ring(
        leave, [mine, other, x, grad_resid], gain_one, blocks, wide, rows, "leave_grad_tokens"
    )
    return output, grad_tokens, g_one, g_query, g_key, g_value, g_out, g_two, g_gate, g_up, g_down


def solution(mesh):
    shape = (mesh.shape["dp"], mesh.shape["tensor"])
    rows, weight_in, weight_out = P("dp", None), P("dp", "tensor"), P("tensor", "dp")
    attend = (P("dp"), weight_in, weight_in, weight_in, weight_out)
    mixer = (P("dp"), weight_in, weight_in, weight_out)

    def layer(*arguments):
        return per_device(shape, *arguments)

    return jax.shard_map(
        layer,
        mesh=mesh,
        in_specs=(rows, P("dp")) + attend + mixer + (rows,),
        out_specs=(rows, rows) + attend + mixer,
        check_vma=False,
    )
```

```python
import functools
import math

import jax
import jax.numpy as jnp
from jax import lax
from jax.experimental import pallas as pl
from jax.experimental.pallas import tpu as pltpu
from jax.sharding import PartitionSpec as P

HD = 64
EPSILON = 1e-05
BF = jnp.bfloat16
F32 = jnp.float32
TILE = 256


def rms_scale(values):
    return lax.rsqrt(jnp.mean(values * values, axis=-1, keepdims=True) + EPSILON)


def norm_back(resid, rstd, gain, grad_normed):
    scaled = gain * grad_normed
    inner = jnp.mean(scaled * resid, axis=-1, keepdims=True)
    return rstd * scaled - resid * (rstd * rstd * rstd) * inner


def dot(a, b):
    return jnp.dot(a, b, preferred_element_type=F32)


def dot_tn(a, b):
    return lax.dot_general(a, b, (((0,), (0,)), ((), ())), preferred_element_type=F32)


def dot_nt(a, b):
    return lax.dot_general(a, b, (((1,), (1,)), ((), ())), preferred_element_type=F32)


def call(body, name, out_shape, grid, in_specs, out_specs, scratch=(), prefetch=0, mib=24):
    spec = pltpu.PrefetchScalarGridSpec(
        num_scalar_prefetch=prefetch,
        grid=grid,
        in_specs=in_specs,
        out_specs=out_specs,
        scratch_shapes=list(scratch),
    )
    return pl.pallas_call(
        body,
        out_shape=out_shape,
        grid_spec=spec,
        name=name,
        compiler_params=pltpu.CompilerParams(
            vmem_limit_bytes=mib * 2**20, dimension_semantics=("arbitrary",) * len(grid)
        ),
        cost_estimate=pl.CostEstimate(flops=0, bytes_accessed=0, transcendentals=0),
    )


def struct(shape, dtype):
    return jax.ShapeDtypeStruct(shape, dtype)


def tiles(width, tile=TILE):
    return pl.BlockSpec((tile, width), lambda i, *_: (i, 0))


def whole(shape):
    return pl.BlockSpec(shape, lambda *_: (0,) * len(shape), pipeline_mode=pl.Buffered(1))


HBM = pl.BlockSpec(memory_space=pltpu.HBM)


class Slots:
    def __init__(self, parts, step):
        self.parts = parts
        self.step = step
        self.shape = (len(parts) * step, sum(p.shape[1] for p in parts[0]))

    def flat(self):
        return [p for pieces in self.parts for p in pieces]

    def scratch(self):
        return [pltpu.VMEM(self.shape, BF), pltpu.SemaphoreType.DMA((len(self.flat()),))]

    def copies(self, refs, buffer, sem):
        found, k = [], 0
        for i, pieces in enumerate(self.parts):
            at, mine = 0, []
            for piece in pieces:
                source, cols = refs[k], piece.shape[1]
                if piece.shape[0] != self.step:
                    source = source.at[pl.ds(0, self.step), :]
                target = buffer.at[pl.ds(i * self.step, self.step), pl.ds(at, cols)]
                mine.append(pltpu.make_async_copy(source, target, sem.at[k]))
                at += cols
                k += 1
            found.append(mine)
        return found


def started(copies):
    for pieces in copies:
        for copy in pieces:
            copy.start()
    return copies


def product_as_it_comes(x, copies, buffer, step):
    total = None
    group = max(1, 512 // step)
    for i in range(0, len(copies), group):
        for pieces in copies[i : i + group]:
            for copy in pieces:
                copy.wait()
        rows = slice(i * step, min(i + group, len(copies)) * step)
        term = dot(x[:, rows], buffer[rows])
        total = term if total is None else total + term
    return total


def lane_blocks(width, wide):
    return [slice(i * wide, (i + 1) * wide) for i in range(width // wide)]


def to_ring(mine, theirs, order, wide):
    rows, depth = mine.shape
    n = depth // wide
    if wide % 128 or rows % TILE:
        both = jnp.concatenate([mine, theirs], axis=0)
        return jnp.take(both.reshape(2 * rows, n, wide), order, axis=1).reshape(2 * rows, depth)
    half = rows // TILE

    def body(order_ref, mine_ref, theirs_ref, out_ref):
        def put(ref):
            for i, block in enumerate(lane_blocks(depth, wide)):
                out_ref[:, block] = ref[:, pl.ds(pl.multiple_of(order_ref[i] * wide, wide), wide)]

        @pl.when(pl.program_id(0) < half)
        def _():
            put(mine_ref)

        @pl.when(pl.program_id(0) >= half)
        def _():
            put(theirs_ref)

    return call(
        body,
        "to_ring",
        struct((2 * rows, depth), mine.dtype),
        (2 * half,),
        [
            pl.BlockSpec((TILE, depth), lambda i, o: (jnp.minimum(i, half - 1), 0)),
            pl.BlockSpec((TILE, depth), lambda i, o: (jnp.maximum(i - half, 0), 0)),
        ],
        pl.BlockSpec((TILE, depth), lambda i, o: (i, 0)),
        prefetch=1,
        mib=12,
    )(order, mine, theirs)


def rope(block, cosine, sine):
    lane = lax.broadcasted_iota(jnp.int32, block.shape, 1)
    low = lane % HD < HD // 2
    other = jnp.where(low, pltpu.roll(block, 128 - HD // 2, 1), pltpu.roll(block, HD // 2, 1))
    return block * cosine + other * sine


def rope_kv(block, cosine, sine):
    lane = lax.broadcasted_iota(jnp.int32, block.shape, 1)
    return jnp.where(lane < HD, rope(block, cosine, sine), block)


def qkv_forward(x, gain, slots, cosine, sine):
    rows, depth = x.shape
    width = slots.shape[1]
    arrays = slots.flat()

    def body(x_ref, gain_ref, cos_ref, sin_ref, *refs):
        weights, (normed_ref, q_ref, kv_ref), (buffer, sem, qkv_ref) = (
            refs[: len(arrays)],
            refs[len(arrays) : -3],
            refs[-3:],
        )
        field = x_ref[...].astype(F32)
        normed = (field * rms_scale(field) * gain_ref[...]).astype(BF)
        normed_ref[...] = normed

        @pl.when(pl.program_id(0) == 0)
        def _():
            copies = started(slots.copies(weights, buffer, sem))
            qkv_ref[...] = product_as_it_comes(normed, copies, buffer, slots.step)

        @pl.when(pl.program_id(0) > 0)
        def _():
            qkv_ref[...] = dot(normed, buffer[...])

        cosv, sinv = cos_ref[...], sin_ref[...]
        for block in lane_blocks(width - 128, 128):
            q_ref[:, block] = rope(qkv_ref[:, block], cosv, sinv).astype(BF)
        kv_ref[...] = rope_kv(qkv_ref[:, width - 128 :], cosv, sinv).astype(BF)

    return call(
        body,
        "qkv_forward",
        [
            struct((rows, depth), BF),
            struct((rows, width - 128), BF),
            struct((rows, 128), BF),
        ],
        (rows // TILE,),
        [tiles(depth), whole((1, depth)), tiles(128), tiles(128)] + [HBM] * len(arrays),
        [tiles(depth), tiles(width - 128), tiles(128)],
        slots.scratch() + [pltpu.VMEM((TILE, width), F32)],
        mib=58,
    )(x, gain, cosine, sine, *arrays)


def masks(seg_row, seg_col, rows, begin, finish):
    key = lax.broadcasted_iota(jnp.int32, (finish, finish - begin), 0)
    query = lax.broadcasted_iota(jnp.int32, (finish, finish - begin), 1) + begin
    return (seg_col[:finish] == seg_row[:, begin:finish]) & (key <= query)


def query_blocks(rows):
    half = rows // 2
    return [(0, half), (half, rows)] if half % 128 == 0 else [(0, rows)]


def attention_forward(q, kv, seg_row, seg_col, rows):
    width = q.shape[1]
    heads = width // HD
    groups = q.shape[0] // rows

    def body(q_ref, kv_ref, row_ref, col_ref, out_ref, lse_ref, turned):
        keys = kv_ref[:, :HD]
        values = kv_ref[...].astype(F32).T[HD:].astype(BF)
        for begin, finish in query_blocks(rows):
            allowed = masks(row_ref[0], col_ref[0], rows, begin, finish)
            for h in range(heads):
                scores = dot_nt(keys[:finish], q_ref[begin:finish, h * HD : (h + 1) * HD]) * 0.125
                scores = jnp.where(allowed, scores, -1e30)
                top = jnp.max(scores, axis=0, keepdims=True)
                expo = jnp.exp(scores - top)
                total = jnp.sum(expo, axis=0, keepdims=True)
                probs = (expo * (1.0 / total)).astype(BF)
                turned[h * HD : (h + 1) * HD, begin:finish] = dot(values[:, :finish], probs)
                lse_ref[0, h : h + 1, begin:finish] = top + jnp.log(total)
        out_ref[...] = turned[...].T.astype(BF)

    return call(
        body,
        "attention_forward",
        [struct(q.shape, BF), struct((groups, heads, rows), F32)],
        (groups,),
        [
            pl.BlockSpec((rows, width), lambda i: (i, 0)),
            pl.BlockSpec((rows, 128), lambda i: (i, 0)),
            pl.BlockSpec((1, 1, rows), lambda i: (i, 0, 0)),
            pl.BlockSpec((1, rows, 1), lambda i: (i, 0, 0)),
        ],
        [
            pl.BlockSpec((rows, width), lambda i: (i, 0)),
            pl.BlockSpec((1, heads, rows), lambda i: (i, 0, 0)),
        ],
        [pltpu.VMEM((width, rows), F32)],
        mib=16,
    )(q, kv, seg_row, seg_col)


def attention_backward(q, kv, grad, lse, seg_row, seg_col, cosine, sine, rows, which, before=None):
    width = q.shape[1]
    heads = width // HD
    old = [] if before is None else [before]

    def body(q_ref, kv_ref, grad_ref, lse_ref, row_ref, col_ref, cos_ref, sin_ref, *refs):
        out_ref, turned, total_k, total_v = refs[len(old) :]
        keys = kv_ref[:, :HD]
        values = kv_ref[:, HD:]
        keys_t = kv_ref[...].astype(F32).T[:HD].astype(BF)
        total_k[...] = jnp.zeros_like(total_k)
        total_v[...] = jnp.zeros_like(total_v)
        for begin, finish in query_blocks(rows):
            allowed = masks(row_ref[0], col_ref[0], rows, begin, finish)
            for h in range(heads):
                head = slice(h * HD, (h + 1) * HD)
                query, grads = q_ref[begin:finish, head], grad_ref[begin:finish, head]
                scores = dot_nt(keys[:finish], query) * 0.125
                scores = jnp.where(allowed, scores, -1e30)
                probs = jnp.exp(scores - lse_ref[0, h : h + 1, begin:finish])
                grad_probs = dot_nt(values[:finish], grads)
                inner = jnp.sum(probs * grad_probs, axis=0, keepdims=True)
                grad_scores = (probs * (grad_probs - inner)).astype(BF)
                turned[head, begin:finish] = dot(keys_t[:, :finish], grad_scores)
                total_k[:finish] += dot(grad_scores, query)
                total_v[:finish] += dot(probs.astype(BF), grads)
        cosv, sinv = cos_ref[...], -sin_ref[...]
        grad_q = turned[...].T * 0.125
        for block in lane_blocks(width, 128):
            out_ref[:, block] = rope(grad_q[:, block], cosv, sinv).astype(BF)
        grad_kv = jnp.concatenate([total_k[...] * 0.125, total_v[...]], axis=1)
        out_ref[:, width:] = rope_kv(grad_kv, cosv, sinv).astype(BF)

    group = lambda w: pl.BlockSpec((rows, w), lambda i: (which, 0))
    one = lambda *shape: pl.BlockSpec((1,) + shape, lambda i: (which, 0, 0))
    return pl.pallas_call(
        body,
        out_shape=struct((q.shape[0], width + 128), BF),
        grid=(1,),
        in_specs=[group(width), group(128), group(width), one(heads, rows), one(1, rows), one(rows, 1)]
        + [group(128), group(128)]
        + [HBM] * len(old),
        out_specs=group(width + 128),
        scratch_shapes=[
            pltpu.VMEM((width, rows), F32),
            pltpu.VMEM((rows, HD), F32),
            pltpu.VMEM((rows, HD), F32),
        ],
        input_output_aliases={8: 0} if old else {},
        name="attention_backward",
        compiler_params=pltpu.CompilerParams(vmem_limit_bytes=20 * 2**20),
        cost_estimate=pl.CostEstimate(flops=0, bytes_accessed=0, transcendentals=0),
    )(q, kv, grad, lse, seg_row, seg_col, cosine, sine, *old)


def pieces_of(rows, count):
    each = -(-rows // 16 // count) * 16
    cuts = [min(rows, i * each) for i in range(count)] + [rows]
    return [slice(x, y) for x, y in zip(cuts[:-1], cuts[1:])]


def project(lefts, slots, rows, name, split=2, mib=28):
    depth = slots[0].shape[0]
    cols = min(256, depth)
    per = cols // slots[0].step
    counts = [len(s.flat()) for s in slots]
    arrays = [b for s in slots for b in s.flat()]
    k, a = len(lefts), len(arrays)

    def body(*refs):
        left_refs, weights, out_refs = refs[:k], refs[k:][:a], refs[k + a :][: 1 + split]
        scratch = refs[k + a + 1 + split :]
        step = pl.program_id(0)
        copies, at = [], 0
        for j, (s, count) in enumerate(zip(slots, counts)):
            copies.append(s.copies(weights[at : at + count], scratch[2 * j], scratch[2 * j + 1]))
            at += count

        @pl.when(step == 0)
        def _():
            for i in range(len(copies[0])):
                for chain in copies:
                    for copy in chain[i]:
                        copy.start()

        for i in range(len(copies[0])):

            @pl.when(step == i // per)
            def _():
                for chain in copies:
                    for copy in chain[i]:
                        copy.wait()

        total = None
        block = pl.ds(pl.multiple_of(step * cols, cols), cols)
        for j in range(k):
            term = dot_nt(left_refs[j][...], scratch[2 * j][block, :])
            total = term if total is None else total + term
        out_refs[0][...] = total[:rows].astype(BF)
        for ref, part in zip(out_refs[1:], pieces):
            ref[...] = total[rows + part.start : rows + part.stop].astype(BF)

    pieces = pieces_of(rows, split)
    column = lambda r: pl.BlockSpec((r, cols), lambda i: (0, i))
    mine, *theirs = call(
        body,
        name,
        [struct((rows, depth), BF)] + [struct((p.stop - p.start, depth), BF) for p in pieces],
        (depth // cols,),
        [whole((2 * rows, left.shape[1])) for left in lefts] + [HBM] * a,
        [column(rows)] + [column(p.stop - p.start) for p in pieces],
        [x for s in slots for x in s.scratch()],
        mib=mib,
    )(*lefts, *arrays)
    return mine, theirs


def parts_of(depth, count):
    tiles_each = -(-depth // 128 // count)
    cuts = [min(depth, i * tiles_each * 128) for i in range(count)] + [depth]
    return [slice(x, y) for x, y in zip(cuts[:-1], cuts[1:])]


def join_cores(mine, came):
    rows, depth = mine.shape

    def body(mine_ref, *refs):
        at = 0
        for ref in refs[:-1]:
            part = slice(at, at + ref.shape[0])
            refs[-1][part] = (mine_ref[part].astype(F32) + ref[...].astype(F32)).astype(BF)
            at = part.stop

    return call(
        body,
        "join_cores",
        struct((rows, depth), BF),
        (1,),
        [whole((rows, depth))] + [whole(c.shape) for c in came],
        whole((rows, depth)),
        mib=16,
    )(mine, *came)


def mixer_forward(field, both, begin, rows, before=None):
    tile, depth = field.shape
    units = both.shape[1] // 2
    at = begin // tile
    arrays = both.flat()
    old = [] if before is None else list(before)

    def body(*refs):
        x = refs[0][...]
        weights, refs = refs[1 : 1 + len(arrays)], refs[1 + len(arrays) + len(old) :]
        lin_ref, act_ref, x_ref, mark_ref, mem, sem = refs
        x_ref[...] = x
        mark_ref[...] = jnp.zeros_like(mark_ref)
        copies = started(both.copies(weights, mem, sem))
        lin = product_as_it_comes(x, copies, mem, both.step)
        lin_ref[...] = lin.astype(BF)
        gate_value, lifted = lin[:, :units], lin[:, units:]
        act_ref[...] = (gate_value * jax.nn.sigmoid(gate_value) * lifted).astype(BF)

    block = lambda w: pl.BlockSpec((tile, w), lambda i: (at, 0))
    first = 1 + len(arrays)
    widths = [2 * units, units, depth]
    return pl.pallas_call(
        body,
        out_shape=[struct((rows, w), BF) for w in widths] + [struct((8, 128), F32)],
        grid=(1,),
        in_specs=[whole((tile, depth))] + [HBM] * (len(arrays) + len(old)),
        out_specs=[block(w) for w in widths] + [whole((8, 128))],
        scratch_shapes=both.scratch(),
        input_output_aliases={first + i: i for i in range(len(old))},
        name="mixer_forward",
        compiler_params=pltpu.CompilerParams(vmem_limit_bytes=58 * 2**20),
        cost_estimate=pl.CostEstimate(flops=0, bytes_accessed=0, transcendentals=0),
    )(field, *arrays, *old)


def mixer_backward(dy, down, lin):
    rows, depth = dy.shape
    units = down.shape[1]
    arrays = down.flat()
    tile = min(256, rows)

    def body(dy_ref, lin_ref, *refs):
        weights, grad_ref, (buffer, sem, act_ref) = refs[: len(arrays)], refs[-4], refs[-3:]

        @pl.when(pl.program_id(0) == 0)
        def _():
            copies = started(down.copies(weights, buffer, sem))
            act_ref[...] = product_as_it_comes(dy_ref, copies, buffer, down.step)

        @pl.when(pl.program_id(0) > 0)
        def _():
            act_ref[...] = dot(dy_ref[...], buffer[...])

        grad_act, gate_value = act_ref[...], lin_ref[:, :units].astype(F32)
        lifted = lin_ref[:, units:].astype(F32)
        s = jax.nn.sigmoid(gate_value)
        grad_ref[:, :units] = (
            grad_act * lifted * s * (1.0 + gate_value * (1.0 - s))
        ).astype(BF)
        grad_ref[:, units:] = (grad_act * (gate_value * s)).astype(BF)

    return call(
        body,
        "mixer_backward",
        struct((rows, 2 * units), BF),
        (rows // tile,),
        [tiles(depth, tile), tiles(2 * units, tile)] + [HBM] * len(arrays),
        tiles(2 * units, tile),
        down.scratch() + [pltpu.VMEM((tile, units), F32)],
        mib=28,
    )(dy, lin, *arrays)


def attended_backward(mine, theirs, out):
    rows, depth = mine[0].shape[0], out.shape[0]
    width = out.shape[1]
    half = rows // TILE
    arrays = out.flat()
    k = len(mine)

    def body(*refs):
        own = pl.program_id(0) < half
        x = jnp.concatenate(
            [jnp.where(own, a[...], b[...]) for a, b in zip(refs[:k], refs[k : 2 * k])], axis=1
        )
        refs = refs[2 * k :]
        weights, (grad_ref, both_ref), (buffer, sem) = (
            refs[: len(arrays)],
            refs[len(arrays) : -2],
            refs[-2:],
        )
        both_ref[...] = x

        @pl.when(pl.program_id(0) == 0)
        def _():
            copies = started(out.copies(weights, buffer, sem))
            grad_ref[...] = product_as_it_comes(x, copies, buffer, out.step).astype(BF)

        @pl.when(pl.program_id(0) > 0)
        def _():
            grad_ref[...] = dot(x, buffer[...]).astype(BF)

    own_rows = [pl.BlockSpec((TILE, m.shape[1]), lambda i: (jnp.minimum(i, half - 1), 0)) for m in mine]
    their_rows = [pl.BlockSpec((TILE, m.shape[1]), lambda i: (jnp.maximum(i - half, 0), 0)) for m in mine]
    return call(
        body,
        "attended_backward",
        [struct((2 * rows, width), BF), struct((2 * rows, depth), BF)],
        (2 * half,),
        own_rows + their_rows + [HBM] * len(arrays),
        [tiles(width), tiles(depth)],
        out.scratch(),
        mib=16,
    )(*mine, *theirs, *arrays)


def norm_forward(x, mine, other, gain, rows):
    depth = x.shape[1]

    def body(x_ref, gain_ref, mine_ref, other_ref, resid_ref, normed_ref):
        resid = x_ref[...].astype(F32) + (mine_ref[...].astype(F32) + other_ref[...].astype(F32))
        resid_ref[...] = resid
        normed_ref[...] = (resid * rms_scale(resid) * gain_ref[...]).astype(BF)

    return call(
        body,
        "norm_forward",
        [struct((rows, depth), F32), struct((rows, depth), BF)],
        (rows // TILE,),
        [tiles(depth), whole((1, depth)), tiles(depth), tiles(depth)],
        [tiles(depth)] * 2,
        mib=24,
    )(x, gain, mine, other)


def norm_backward(resid, mine, other, dy, gain, rows):
    depth = dy.shape[1]
    parts = parts_of(depth, 2)

    def body(resid_ref, dy_ref, gain_ref, mine_ref, other_ref, grad_ref, *branch_refs):
        resid = resid_ref[...]
        grad_normed = mine_ref[...].astype(F32) + other_ref[...].astype(F32)
        grad = norm_back(resid, rms_scale(resid), gain_ref[...], grad_normed)
        grad = grad + dy_ref[...].astype(F32)
        grad_ref[...] = grad
        for ref, block in zip(branch_refs, parts):
            ref[...] = grad[:, block].astype(BF)

    grad_resid, *branch = call(
        body,
        "norm_backward",
        [struct((rows, depth), F32)] + [struct((rows, p.stop - p.start), BF) for p in parts],
        (rows // TILE,),
        [tiles(depth), tiles(depth), whole((1, depth)), tiles(depth), tiles(depth)],
        [tiles(depth)] + [tiles(p.stop - p.start) for p in parts],
        mib=28,
    )(resid, dy, gain, mine, other)
    return grad_resid, branch


def leave_ring(fn, arrays, gain, order, wide, rows, name):
    depth = arrays[0].shape[1]
    n = depth // wide
    if wide % 128 or rows % TILE:
        field = fn(*[a[:rows] for a in arrays], gain).astype(BF)
        back = jnp.zeros((n,), jnp.int32).at[order].set(jnp.arange(n, dtype=jnp.int32))
        return jnp.take(field.reshape(rows, n, wide), back, axis=1).reshape(rows, depth)
    k = len(arrays)

    def body(order_ref, *refs):
        field = fn(*[r[...] for r in refs[:k]], refs[k][...]).astype(BF)
        for i, block in enumerate(lane_blocks(depth, wide)):
            refs[k + 1][:, pl.ds(pl.multiple_of(order_ref[i] * wide, wide), wide)] = field[:, block]

    return call(
        body,
        name,
        struct((rows, depth), BF),
        (rows // TILE,),
        [tiles(depth)] * k + [whole((1, depth))],
        tiles(depth),
        prefetch=1,
        mib=32,
    )(order, *arrays, gain)


def turned(block):
    return block.astype(F32).T.astype(BF)


def fetch(pairs, sem):
    copies = [pltpu.make_async_copy(a, b, sem.at[i]) for i, (a, b) in enumerate(pairs)]
    for copy in copies:
        copy.start()
    for copy in copies:
        copy.wait()


def columns(ref, half):
    size = ref.shape[1] // 2
    return ref.at[:, pl.ds(pl.multiple_of(half * size, 128), size)]


def rows_of(ref, half):
    size = ref.shape[0] // 2
    return ref.at[pl.ds(pl.multiple_of(half * size, 128), size), :]


def halves(core, w_query, w_key, w_value, w_output, gain_attend, gain_mixer):
    part, q_cols = w_query.shape[0], w_query.shape[1] // 2
    k_cols = w_key.shape[1] // 2
    width, out_width = q_cols + 2 * k_cols, w_output.shape[0] // 2

    def body(
        core_ref, q_ref, k_ref, v_ref, o_ref, one_ref, two_ref, qkv_ref, out_ref, k_mem, v_mem, o_mem, sem
    ):
        there = 1 - core_ref[0]
        low = there == 0
        fetch(
            [
                (columns(q_ref, there), qkv_ref.at[pl.ds(0, part), pl.ds(0, q_cols)]),
                (k_ref, k_mem),
                (v_ref, v_mem),
                (rows_of(o_ref, there), o_mem),
            ],
            sem,
        )
        k, v = k_mem[...], v_mem[...]
        qkv_ref[:part, q_cols:] = jnp.concatenate(
            [jnp.where(low, w[:, :k_cols], w[:, k_cols:]) for w in (k, v)], axis=1
        )
        qkv_ref[part:, :] = jnp.zeros((16, width), BF)
        qkv_ref[part : part + 1, :part] = one_ref[...]
        qkv_ref[part + 1 : part + 2, :part] = two_ref[...]
        out_ref[...] = turned(o_mem[...])

    shapes = [(part + 16, width), (part, out_width)]
    return call(
        body,
        "halves",
        [struct(shape, BF) for shape in shapes],
        (1,),
        [HBM] * 4 + [whole((1, part))] * 2,
        [whole(shape) for shape in shapes],
        [
            pltpu.VMEM((part, 2 * k_cols), BF),
            pltpu.VMEM((part, 2 * k_cols), BF),
            pltpu.VMEM((out_width, part), BF),
            pltpu.SemaphoreType.DMA((4,)),
        ],
        prefetch=1,
        mib=58,
    )(core, w_query, w_key, w_value, w_output, gain_attend, gain_mixer)


def mixer_halves(core, w_gate, w_up, w_down):
    part, units = w_gate.shape[0], w_gate.shape[1] // 2

    def body(core_ref, gate_ref, up_ref, down_ref, mixer_ref, down_mem, sem):
        there = 1 - core_ref[0]
        fetch(
            [
                (columns(gate_ref, there), mixer_ref.at[:, pl.ds(0, units)]),
                (columns(up_ref, there), mixer_ref.at[:, pl.ds(units, units)]),
                (rows_of(down_ref, there), down_mem),
            ],
            sem,
        )
        mixer_ref[:, 2 * units :] = turned(down_mem[...])

    return call(
        body,
        "mixer_halves",
        struct((part, 3 * units), BF),
        (1,),
        [HBM] * 3,
        whole((part, 3 * units)),
        [pltpu.VMEM((units, part), BF), pltpu.SemaphoreType.DMA((3,))],
        prefetch=1,
        mib=58,
    )(core, w_gate, w_up, w_down)


def put_rows(core_ref, out_ref, mine, came, part, cols=slice(None)):
    @pl.when(core_ref[0] == 0)
    def _():
        out_ref[:part, cols], out_ref[part : 2 * part, cols] = mine, came

    @pl.when(core_ref[0] == 1)
    def _():
        out_ref[:part, cols], out_ref[part : 2 * part, cols] = came, mine


def chip_rows(core, w_query, w_key, w_value, w_output, gain_attend, gain_mixer, came, came_out):
    part, q_cols = w_query.shape[0], w_query.shape[1] // 2
    k_cols = w_key.shape[1] // 2
    width, out_width = came.shape[1], came_out.shape[1]

    def body(
        core_ref, q_ref, k_ref, v_ref, o_ref, one_ref, two_ref, came_ref, came_out_ref,
        qkv_ref, out_ref, q_mem, k_mem, v_mem, o_mem, sem,
    ):
        here = core_ref[0]
        first = here == 0
        fetch(
            [
                (columns(q_ref, here), q_mem),
                (k_ref, k_mem),
                (v_ref, v_mem),
                (rows_of(o_ref, here), o_mem),
            ],
            sem,
        )
        k, v = k_mem[...], v_mem[...]
        own = [jnp.where(first, w[:, :k_cols], w[:, k_cols:]) for w in (k, v)]
        put_rows(core_ref, qkv_ref, jnp.concatenate([q_mem[...]] + own, axis=1), came_ref[:part], part)
        put_rows(core_ref, out_ref, turned(o_mem[...]), came_out_ref[...], part)
        qkv_ref[2 * part :, :] = jnp.zeros((16, width), BF)
        for row, ref in enumerate((one_ref, two_ref)):
            mine, other = ref[...], came_ref[part + row : part + row + 1, :part]
            at = slice(2 * part + row, 2 * part + row + 1)
            qkv_ref[at, :part] = jnp.where(first, mine, other)
            qkv_ref[at, part : 2 * part] = jnp.where(first, other, mine)

    return call(
        body,
        "chip_rows",
        [struct((2 * part + 16, width), BF), struct((2 * part, out_width), BF)],
        (1,),
        [HBM] * 4 + [whole((1, part))] * 2 + [whole(came.shape), whole(came_out.shape)],
        [whole((2 * part + 16, width)), whole((2 * part, out_width))],
        [
            pltpu.VMEM((part, q_cols), BF),
            pltpu.VMEM((part, 2 * k_cols), BF),
            pltpu.VMEM((part, 2 * k_cols), BF),
            pltpu.VMEM((out_width, part), BF),
            pltpu.SemaphoreType.DMA((4,)),
        ],
        prefetch=1,
        mib=58,
    )(core, w_query, w_key, w_value, w_output, gain_attend, gain_mixer, came, came_out)


def mixer_rows(core, w_gate, w_up, w_down, came):
    part, units = w_gate.shape[0], w_gate.shape[1] // 2

    def body(core_ref, gate_ref, up_ref, down_ref, came_ref, both_ref, turned_ref, gate_mem, up_mem, down_mem, sem):
        here = core_ref[0]
        fetch(
            [
                (columns(gate_ref, here), gate_mem),
                (columns(up_ref, here), up_mem),
                (rows_of(down_ref, here), down_mem),
            ],
            sem,
        )
        for i, mem in enumerate((gate_mem, up_mem)):
            cols = slice(i * units, (i + 1) * units)
            put_rows(core_ref, both_ref, mem[...], came_ref[:, cols], part, cols)
        put_rows(core_ref, turned_ref, turned(down_mem[...]), came_ref[:, 2 * units :], part)

    shapes = [(2 * part, 2 * units), (2 * part, units)]
    return call(
        body,
        "mixer_rows",
        [struct(shape, BF) for shape in shapes],
        (1,),
        [HBM] * 3 + [whole(came.shape)],
        [whole(shape) for shape in shapes],
        [pltpu.VMEM((part, units), BF)] * 2
        + [pltpu.VMEM((units, part), BF), pltpu.SemaphoreType.DMA((3,))],
        prefetch=1,
        mib=58,
    )(core, w_gate, w_up, w_down, came)


def beside(core, mine, came, turn):
    part, width = mine.shape
    shape = (2 * width, part) if turn else (part, 2 * width)

    def body(core_ref, mine_ref, came_ref, out_ref):
        def put(low, high):
            if turn:
                out_ref[:width], out_ref[width:] = low[...].T, high[...].T
            else:
                out_ref[:, :width], out_ref[:, width:] = low[...], high[...]

        @pl.when(core_ref[0] == 0)
        def _():
            put(mine_ref, came_ref)

        @pl.when(core_ref[0] == 1)
        def _():
            put(came_ref, mine_ref)

    return call(
        body,
        "beside",
        struct(shape, F32),
        (1,),
        [whole((part, width))] * 2,
        whole(shape),
        prefetch=1,
        mib=16,
    )(core, mine, came)


def after(value, *others):
    return lax.optimization_barrier((value,) + others)[0]


class Ring:
    def __init__(self, devices):
        self.n = devices // 2
        n = self.n
        order = list(range(0, n, 2)) + list(range(n - 1 - n % 2, 0, -2))
        self.order = order
        place = [0] * n
        for position, chip in enumerate(order):
            place[chip] = position
        self.place = place
        self.steps = {1: [], -1: []}
        for position, chip in enumerate(order):
            then = order[(position + 1) % n]
            for core in (0, 1):
                self.steps[1].append((2 * chip + core, 2 * then + core))
                self.steps[-1].append((2 * then + core, 2 * chip + core))
        self.cores = [(i, i ^ 1) for i in range(devices)]
        self.hops = n // 2

    def pass_on(self, block, way):
        return lax.ppermute(block, "dp", self.steps[way])

    def halves(self, width):
        cut = min(width, (width // 2 + 127) // 128 * 128)
        return slice(0, cut), slice(cut, width)

    def swap(self, block):
        return lax.ppermute(block, "dp", self.cores)


class Gather:
    def __init__(self, ring, block):
        self.ring, self.hop = ring, 0
        self.found = [[block]] + [None] * (ring.n - 1)
        self.last = (block,)

    def step(self, *others):
        ring, n = self.ring, self.ring.n
        self.hop += 1
        hop = self.hop
        if 2 * hop > n:
            return
        before = [self.found[(hop - 1) * way % n][0] for way in (1, -1)]
        if others:
            before = [after(b, *others) for b in before]
        if 2 * hop < n:
            for way, block in zip((1, -1), before):
                self.found[hop * way % n] = [ring.pass_on(block, way)]
            self.last = tuple(self.found[hop * way % n][0] for way in (1, -1))
        else:
            parts = ring.halves(before[0].shape[1])
            self.found[hop] = [
                ring.pass_on(b[:, part], way) for b, way, part in zip(before, (1, -1), parts)
            ]
            self.last = tuple(self.found[hop])

    def finish(self):
        while 2 * (self.hop + 1) <= self.ring.n:
            self.step()
        return self.found


class Line:
    def __init__(self):
        self.marks = ()

    def after(self, value):
        return after(value, *self.marks) if self.marks else value

    def mark(self, *found):
        self.marks = found

    def wait(self, *found):
        self.marks = self.marks + found


class Scatter:
    def __init__(self, ring, line, field, grads):
        self.ring, self.line, self.field, self.grads = ring, line, field, grads
        self.width, self.hop = grads.shape[1], 0
        self.wide = field.shape[1] // ring.n
        self.held = {1: None, -1: None}
        self.last = ()

    def term(self, i, part):
        field = self.line.after(self.field)
        return dot_tn(field[:, i * self.wide : (i + 1) * self.wide], self.grads[:, part])

    def step(self):
        ring, n = self.ring, self.ring.n
        far = n // 2 - self.hop
        if far == 0:
            return
        self.hop += 1
        for way, part in zip((1, -1), ring.halves(self.width)):
            if 2 * far == n:
                total = self.term(far, part)
            else:
                part = slice(0, self.width)
                total = self.term(-far * way % n, part) + self.came(way)
            total = total.astype(BF)
            self.line.mark(total)
            self.held[way] = (ring.pass_on(total, way), part)
        self.last = tuple(self.held[way][0] for way in (1, -1))

    def came(self, way):
        if self.held[way] is None:
            return 0.0
        came, part = self.held[way]
        edges = ((0, 0, 0), (part.start, self.width - part.stop, 0))
        return lax.pad(came.astype(F32), jnp.zeros((), F32), edges)

    def finish(self):
        while self.hop < self.ring.n // 2:
            self.step()
        total = self.term(0, slice(0, self.width)) + self.came(1) + self.came(-1)
        self.line.mark(total)
        return total


def half_of(w, half, axis):
    size = w.shape[axis] // 2
    return lax.dynamic_slice_in_dim(w, half * size, size, axis)


def slow_rows(core, swap, pick):
    mine, came = pick(core), swap(pick(1 - core))
    first = core == 0
    return jnp.where(first, mine, came), jnp.where(first, came, mine)


def slow_attend_rows(core, swap, w_query, w_key, w_value, w_output, gain_attend, gain_mixer):
    part = w_query.shape[0]
    qkv = slow_rows(
        core,
        swap,
        lambda half: jnp.concatenate([half_of(w, half, 1) for w in (w_query, w_key, w_value)], axis=1),
    )
    out = slow_rows(core, swap, lambda half: half_of(w_output, half, 0).T)
    gains = slow_rows(core, swap, lambda half: jnp.concatenate([gain_attend, gain_mixer]))
    below = jnp.concatenate(gains, axis=1)
    below = jnp.pad(below, ((0, 14), (0, qkv[0].shape[1] - 2 * part)))
    return jnp.concatenate(qkv + (below,)), jnp.concatenate(out)


def slow_mixer_rows(core, swap, w_gate, w_up, w_down):
    picks = (
        lambda half: half_of(w_gate, half, 1),
        lambda half: half_of(w_up, half, 1),
        lambda half: half_of(w_down, half, 0).T,
    )
    gate, up, down = [jnp.concatenate(slow_rows(core, swap, pick)) for pick in picks]
    return jnp.concatenate([gate, up], axis=1), down


def per_device(
    shape,
    tokens,
    segments,
    gain_attend,
    w_query,
    w_key,
    w_value,
    w_output,
    gain_mixer,
    w_gate,
    w_up,
    w_down,
    cotangent,
):
    devices, tensors = shape
    ring = Ring(devices)
    swap = ring.swap
    n = ring.n
    rows, depth = tokens.shape
    part = depth // devices
    wide = 2 * part
    index = lax.axis_index("dp")
    core = index % 2
    first = core == 0
    position = jnp.asarray(ring.place, jnp.int32)[index // 2]
    blocks = jnp.asarray(ring.order, jnp.int32)[(position - jnp.arange(n, dtype=jnp.int32)) % n]

    def across(block):
        if tensors == 1:
            return jnp.zeros_like(block)
        return lax.ppermute(block, "tensor", [(i, i ^ 1) for i in range(tensors)])

    line = Line()
    tokens_came, cotangent_came, segments_came = swap(tokens), swap(cotangent), swap(segments)

    q_cols = w_query.shape[1] // 2
    k_cols = w_key.shape[1] // 2
    all_cols = q_cols + 2 * k_cols
    attend = (w_query, w_key, w_value, w_output, gain_attend[None], gain_mixer[None])
    mixer = (w_gate, w_up, w_down)
    which = core.astype(jnp.int32)[None]
    if part % 128:
        qkv_block, out_block = slow_attend_rows(core, swap, *attend)
        both_block, down_block = slow_mixer_rows(core, swap, *mixer)
    else:
        sent = halves(which, *attend)
        line.mark(*sent)
        sent_mixer = mixer_halves(line.after(which), *mixer)
        line.mark(sent_mixer, tokens_came, cotangent_came, segments_came)
        qkv_block, out_block = chip_rows(line.after(which), *attend, *[swap(s) for s in sent])
        line.mark(qkv_block)
        both_block, down_block = mixer_rows(line.after(which), *mixer, swap(sent_mixer))
        line.mark(both_block)

    ring_q, ring_o = Gather(ring, qkv_block), Gather(ring, out_block)
    ring_q.step()
    ring_o.step()
    segs = jnp.stack([segments, segments_came])
    places = jnp.arange(rows, dtype=jnp.int32)
    fresh = jnp.concatenate([jnp.ones((2, 1), dtype=bool), segs[:, 1:] != segs[:, :-1]], axis=1)
    starts = lax.cummax(jnp.where(fresh, places, 0), axis=1)
    lanes = jnp.arange(128, dtype=jnp.int32)
    freqs = jnp.exp((lanes % (HD // 2)).astype(F32) * (-2.0 * math.log(10000.0) / HD))
    angle = (places - starts).astype(F32).reshape(2 * rows, 1) * freqs[None, :]
    seg_row, seg_col = segs.reshape(2, 1, rows), segs.reshape(2, rows, 1)
    x = to_ring(line.after(tokens), tokens_came, blocks, wide)
    line.mark(x, *ring_q.last)
    ring_q.step(x)
    angle = line.after(angle)
    cosine = jnp.cos(angle)
    sine = jnp.sin(angle) * jnp.where(lanes % HD < HD // 2, -1.0, 1.0)
    line.mark(cosine, *ring_o.last)
    ring_o.step(cosine)
    dy = to_ring(line.after(cotangent), cotangent_came, blocks, wide)
    line.mark(dy, *ring_q.last)
    ring_q.step(dy)
    line.wait(*ring_o.last)
    ring_o.step(dy)
    line.wait(*ring_q.last)
    ring_q.step()
    line.wait(*ring_o.last)
    ring_o.step()
    line.wait(*ring_q.last, *ring_o.last)
    qkv_parts = ring_q.finish()
    w_out = Slots(ring_o.finish(), wide)
    w_qkv = Slots(qkv_parts, wide)
    ring_g, ring_d = Gather(ring, both_block), Gather(ring, down_block)
    ring_g.step(*ring_q.last, *ring_o.last)

    def gain_of(row):
        return jnp.concatenate(
            [p[0][wide + row : wide + row + 1, :wide] for p in qkv_parts], axis=1
        ).astype(F32)

    gain_one, gain_two = gain_of(0), gain_of(1)

    def swap_all(pieces):
        return [swap(piece) for piece in pieces]

    def swap_late(pieces):
        return [swap(line.after(piece)) for piece in pieces]

    def joined(mine, came):
        mine = join_cores(line.after(mine), came)
        line.mark(mine)
        return mine

    normed_one, queries, kv = qkv_forward(line.after(x), gain_one, w_qkv, cosine, sine)
    line.mark(normed_one)
    attended, lse = attention_forward(line.after(queries), kv, seg_row, seg_col, rows)
    line.mark(attended, *ring_g.last)
    ring_g.step(attended)
    mine, theirs = project([line.after(attended)], [w_out], rows, "attended_out", 3, 58)
    line.mark(mine)
    mine = joined(mine, swap_late(theirs))
    other = across(mine)
    line.wait(*ring_g.last)
    ring_g.step(*line.marks)
    ring_d.step(*line.marks)
    resid, normed_mine = norm_forward(x, line.after(mine), other, gain_two, rows)
    line.mark(resid, *ring_g.last)
    came = swap(line.after(normed_mine))
    ring_g.step(resid)
    both = Slots(ring_g.finish(), wide)
    line.wait(*ring_d.last)
    ring_d.step()
    *first_rows, mark = mixer_forward(line.after(normed_mine), both, 0, 2 * rows)
    line.mark(mark, *ring_d.last)
    ring_d.step(*line.marks)
    lin, act, normed_two, mark = mixer_forward(line.after(came), both, rows, 2 * rows, first_rows)
    line.mark(mark)

    grad_down = Scatter(ring, line, dy, act)
    grad_down.step()
    line.wait(*ring_d.last)
    ring_d.step(*line.marks)
    grad_down.step()
    line.wait(*ring_d.last)
    down = Slots(ring_d.finish(), wide)
    grad_lin = mixer_backward(line.after(dy), down, lin)
    line.mark(grad_lin)
    grad_both = Scatter(ring, line, normed_two, grad_lin)
    grad_both.step()
    line.wait(*grad_down.last)
    grad_down.step()
    mine, theirs = project([line.after(grad_lin)], [both], rows, "grad_normed_two")
    line.mark(mine, *grad_both.last, *grad_down.last)
    came = swap_late(theirs)
    grad_both.step()
    mine = joined(mine, came)
    other = across(mine)
    grad_down.step()
    out_mine, out_theirs = project([line.after(act)], [down], rows, "act_out")
    line.mark(out_mine, *grad_both.last)
    came = swap_late(out_theirs)
    grad_both.step()
    out_mine = joined(out_mine, came)
    line.wait(other, *grad_down.last)
    out_other = across(line.after(out_mine))
    grad_resid, branch_mine = norm_backward(resid, line.after(mine), other, dy, gain_two, rows)
    line.mark(grad_resid)
    came = swap_all(branch_mine)
    branch_mine[0] = line.after(branch_mine[0])
    grad_attended, grad_branch = attended_backward(branch_mine, came, w_out)
    line.mark(grad_attended)
    pieces = (kv, grad_attended, lse, seg_row, seg_col, cosine, sine, rows)
    grad_qkv = attention_backward(line.after(queries), *pieces, 0)
    grad_out = Scatter(ring, line, grad_branch, attended)
    line.mark(grad_qkv)
    down_sum = grad_down.finish()
    line.wait(*grad_both.last)
    grad_out.step()
    grad_qkv = attention_backward(line.after(queries), *pieces, 1, grad_qkv)
    line.mark(grad_qkv, *grad_out.last)
    grad_out.step()
    grad_projections = Scatter(ring, line, normed_one, grad_qkv)
    grad_projections.step()
    mine, theirs = project([line.after(grad_qkv)], [w_qkv], rows, "grad_normed_one")
    line.mark(mine, *grad_out.last, *grad_projections.last, out_other)
    came = swap_late(theirs)
    grad_projections.step()
    mine = joined(mine, came)
    other = across(mine)
    line.wait(*grad_projections.last)
    grad_both.step()
    output = leave_ring(
        lambda r, m, o, _: r + (m.astype(F32) + o.astype(F32)),
        [line.after(resid), out_mine, out_other],
        gain_two,
        blocks,
        wide,
        rows,
        "leave_output",
    )
    line.mark(output)
    grad_projections.step()

    def own(field, which):
        return lax.dynamic_slice_in_dim(field, which * part, part, 0)

    def send(field):
        rows_there = own(line.after(field), 1 - core)
        line.mark(rows_there)
        return field, swap(rows_there)

    def spread(pair):
        mine, came = own(line.after(pair[0]), core), pair[1]
        return jnp.where(first, mine, came), jnp.where(first, came, mine)

    def spread_turned(pair):
        mine, came = own(line.after(pair[0]), core), pair[1]
        if part % 128:
            low, high = jnp.where(first, mine, came), jnp.where(first, came, mine)
            return jnp.concatenate([low, high], axis=1).T
        return beside(which, mine, came, True)

    def done(*found):
        line.mark(*found)
        return found[0]

    def gain_grad(pairs):
        return sum(jnp.sum(w.astype(F32) * g, axis=1) for w, g in pairs)

    def leave(mine, other, x, grad_resid, gain):
        x = x.astype(F32)
        grad_normed = mine.astype(F32) + other.astype(F32)
        return grad_resid + norm_back(x, rms_scale(x), gain, grad_normed)

    line.wait(other, *grad_both.last)
    grad_out.step()
    grad_projections.step()
    both_sum = grad_both.finish()
    grad_out.step()
    qkv_sum = send(grad_projections.finish())
    down_sum = send(down_sum)
    both_sum = send(both_sum)
    grad_tokens = leave_ring(
        leave, [mine, other, line.after(x), grad_resid], gain_one, blocks, wide, rows, "leave_grad_tokens"
    )
    line.mark(grad_tokens)
    out_sum = send(grad_out.finish())
    g_down = done(spread_turned(down_sum))
    low, high = spread(both_sum)
    units = low.shape[1] // 2
    g_gate = done(jnp.concatenate([low[:, :units], high[:, :units]], axis=1))
    g_up = done(jnp.concatenate([low[:, units:], high[:, units:]], axis=1))
    g_two = done(gain_grad([(line.after(w_gate), g_gate), (w_up, g_up)]))
    g_two = (g_two + across(line.after(g_two))) / gain_mixer.astype(F32)
    low, high = spread(qkv_sum)
    g_out = spread_turned(out_sum)

    def sides(begin, finish):
        return jnp.concatenate([low[:, begin:finish], high[:, begin:finish]], axis=1)

    g_query = sides(0, q_cols)
    g_key = sides(q_cols, q_cols + k_cols)
    g_value = sides(q_cols + k_cols, all_cols)
    g_one = gain_grad([(w_query, g_query), (w_key, g_key), (w_value, g_value)])
    g_one = (g_one + across(g_one)) / gain_attend.astype(F32)
    return output, grad_tokens, g_one, g_query, g_key, g_value, g_out, g_two, g_gate, g_up, g_down


def solution(mesh):
    shape = (mesh.shape["dp"], mesh.shape["tensor"])
    rows, weight_in, weight_out = P("dp", None), P("dp", "tensor"), P("tensor", "dp")
    attend = (P("dp"), weight_in, weight_in, weight_in, weight_out)
    mixer = (P("dp"), weight_in, weight_in, weight_out)

    def layer(*arguments):
        return per_device(shape, *arguments)

    return jax.shard_map(
        layer,
        mesh=mesh,
        in_specs=(rows, P("dp")) + attend + mixer + (rows,),
        out_specs=(rows, rows) + attend + mixer,
        check_vma=False,
    )
```

```python
import functools
import math

import jax
import jax.numpy as jnp
from jax import lax
from jax.experimental import pallas as pl
from jax.experimental.pallas import tpu as pltpu
from jax.sharding import PartitionSpec as P

HD = 64
EPSILON = 1e-05
BF = jnp.bfloat16
F32 = jnp.float32
TILE = 256


def rms_scale(values):
    return lax.rsqrt(jnp.mean(values * values, axis=-1, keepdims=True) + EPSILON)


def norm_back(resid, rstd, gain, grad_normed):
    scaled = gain * grad_normed
    inner = jnp.mean(scaled * resid, axis=-1, keepdims=True)
    return rstd * scaled - resid * (rstd * rstd * rstd) * inner


def dot(a, b):
    return jnp.dot(a, b, preferred_element_type=F32)


def dot_tn(a, b):
    return lax.dot_general(a, b, (((0,), (0,)), ((), ())), preferred_element_type=F32)


def dot_nt(a, b):
    return lax.dot_general(a, b, (((1,), (1,)), ((), ())), preferred_element_type=F32)


def call(body, name, out_shape, grid, in_specs, out_specs, scratch=(), prefetch=0, mib=24):
    spec = pltpu.PrefetchScalarGridSpec(
        num_scalar_prefetch=prefetch,
        grid=grid,
        in_specs=in_specs,
        out_specs=out_specs,
        scratch_shapes=list(scratch),
    )
    return pl.pallas_call(
        body,
        out_shape=out_shape,
        grid_spec=spec,
        name=name,
        compiler_params=pltpu.CompilerParams(
            vmem_limit_bytes=mib * 2**20, dimension_semantics=("arbitrary",) * len(grid)
        ),
        cost_estimate=pl.CostEstimate(flops=0, bytes_accessed=0, transcendentals=0),
    )


def struct(shape, dtype):
    return jax.ShapeDtypeStruct(shape, dtype)


def tiles(width, tile=TILE):
    return pl.BlockSpec((tile, width), lambda i, *_: (i, 0))


def whole(shape):
    return pl.BlockSpec(shape, lambda *_: (0,) * len(shape), pipeline_mode=pl.Buffered(1))


HBM = pl.BlockSpec(memory_space=pltpu.HBM)


class Slots:
    def __init__(self, parts, step):
        self.parts = parts
        self.step = step
        self.shape = (len(parts) * step, sum(p.shape[1] for p in parts[0]))

    def flat(self):
        return [p for pieces in self.parts for p in pieces]

    def scratch(self):
        return [pltpu.VMEM(self.shape, BF), pltpu.SemaphoreType.DMA((len(self.flat()),))]

    def copies(self, refs, buffer, sem):
        found, k = [], 0
        for i, pieces in enumerate(self.parts):
            at, mine = 0, []
            for piece in pieces:
                source, cols = refs[k], piece.shape[1]
                if piece.shape[0] != self.step:
                    source = source.at[pl.ds(0, self.step), :]
                target = buffer.at[pl.ds(i * self.step, self.step), pl.ds(at, cols)]
                mine.append(pltpu.make_async_copy(source, target, sem.at[k]))
                at += cols
                k += 1
            found.append(mine)
        return found


def started(copies):
    for pieces in copies:
        for copy in pieces:
            copy.start()
    return copies


def product_as_it_comes(x, copies, buffer, step):
    total = None
    group = max(1, 512 // step)
    for i in range(0, len(copies), group):
        for pieces in copies[i : i + group]:
            for copy in pieces:
                copy.wait()
        rows = slice(i * step, min(i + group, len(copies)) * step)
        term = dot(x[:, rows], buffer[rows])
        total = term if total is None else total + term
    return total


def lane_blocks(width, wide):
    return [slice(i * wide, (i + 1) * wide) for i in range(width // wide)]


def to_ring(mine, theirs, order, wide):
    rows, depth = mine.shape
    n = depth // wide
    if wide % 128 or rows % TILE:
        both = jnp.concatenate([mine, theirs], axis=0)
        return jnp.take(both.reshape(2 * rows, n, wide), order, axis=1).reshape(2 * rows, depth)
    half = rows // TILE

    def body(order_ref, mine_ref, theirs_ref, out_ref):
        def put(ref):
            for i, block in enumerate(lane_blocks(depth, wide)):
                out_ref[:, block] = ref[:, pl.ds(pl.multiple_of(order_ref[i] * wide, wide), wide)]

        @pl.when(pl.program_id(0) < half)
        def _():
            put(mine_ref)

        @pl.when(pl.program_id(0) >= half)
        def _():
            put(theirs_ref)

    return call(
        body,
        "to_ring",
        struct((2 * rows, depth), mine.dtype),
        (2 * half,),
        [
            pl.BlockSpec((TILE, depth), lambda i, o: (jnp.minimum(i, half - 1), 0)),
            pl.BlockSpec((TILE, depth), lambda i, o: (jnp.maximum(i - half, 0), 0)),
        ],
        pl.BlockSpec((TILE, depth), lambda i, o: (i, 0)),
        prefetch=1,
        mib=12,
    )(order, mine, theirs)


def rope(block, cosine, sine):
    lane = lax.broadcasted_iota(jnp.int32, block.shape, 1)
    low = lane % HD < HD // 2
    other = jnp.where(low, pltpu.roll(block, 128 - HD // 2, 1), pltpu.roll(block, HD // 2, 1))
    return block * cosine + other * sine


def rope_kv(block, cosine, sine):
    lane = lax.broadcasted_iota(jnp.int32, block.shape, 1)
    return jnp.where(lane < HD, rope(block, cosine, sine), block)


def qkv_forward(x, gain, slots, cosine, sine):
    rows, depth = x.shape
    width = slots.shape[1]
    arrays = slots.flat()

    def body(x_ref, gain_ref, cos_ref, sin_ref, *refs):
        weights, (normed_ref, q_ref, kv_ref), (buffer, sem, qkv_ref) = (
            refs[: len(arrays)],
            refs[len(arrays) : -3],
            refs[-3:],
        )
        field = x_ref[...].astype(F32)
        normed = (field * rms_scale(field) * gain_ref[...]).astype(BF)
        normed_ref[...] = normed

        @pl.when(pl.program_id(0) == 0)
        def _():
            copies = started(slots.copies(weights, buffer, sem))
            qkv_ref[...] = product_as_it_comes(normed, copies, buffer, slots.step)

        @pl.when(pl.program_id(0) > 0)
        def _():
            qkv_ref[...] = dot(normed, buffer[...])

        cosv, sinv = cos_ref[...], sin_ref[...]
        for block in lane_blocks(width - 128, 128):
            q_ref[:, block] = rope(qkv_ref[:, block], cosv, sinv).astype(BF)
        kv_ref[...] = rope_kv(qkv_ref[:, width - 128 :], cosv, sinv).astype(BF)

    return call(
        body,
        "qkv_forward",
        [
            struct((rows, depth), BF),
            struct((rows, width - 128), BF),
            struct((rows, 128), BF),
        ],
        (rows // TILE,),
        [tiles(depth), whole((1, depth)), tiles(128), tiles(128)] + [HBM] * len(arrays),
        [tiles(depth), tiles(width - 128), tiles(128)],
        slots.scratch() + [pltpu.VMEM((TILE, width), F32)],
        mib=58,
    )(x, gain, cosine, sine, *arrays)


def masks(seg_row, seg_col, rows, begin, finish):
    key = lax.broadcasted_iota(jnp.int32, (finish, finish - begin), 0)
    query = lax.broadcasted_iota(jnp.int32, (finish, finish - begin), 1) + begin
    return (seg_col[:finish] == seg_row[:, begin:finish]) & (key <= query)


def query_blocks(rows):
    half = rows // 2
    return [(0, half), (half, rows)] if half % 128 == 0 else [(0, rows)]


def attention_forward(q, kv, seg_row, seg_col, rows):
    width = q.shape[1]
    heads = width // HD
    groups = q.shape[0] // rows

    def body(q_ref, kv_ref, row_ref, col_ref, out_ref, lse_ref, turned):
        keys = kv_ref[:, :HD]
        values = kv_ref[...].astype(F32).T[HD:].astype(BF)
        for begin, finish in query_blocks(rows):
            allowed = masks(row_ref[0], col_ref[0], rows, begin, finish)
            for h in range(heads):
                scores = dot_nt(keys[:finish], q_ref[begin:finish, h * HD : (h + 1) * HD]) * 0.125
                scores = jnp.where(allowed, scores, -1e30)
                top = jnp.max(scores, axis=0, keepdims=True)
                expo = jnp.exp(scores - top)
                total = jnp.sum(expo, axis=0, keepdims=True)
                probs = (expo * (1.0 / total)).astype(BF)
                turned[h * HD : (h + 1) * HD, begin:finish] = dot(values[:, :finish], probs)
                lse_ref[0, h : h + 1, begin:finish] = top + jnp.log(total)
        out_ref[...] = turned[...].T.astype(BF)

    return call(
        body,
        "attention_forward",
        [struct(q.shape, BF), struct((groups, heads, rows), F32)],
        (groups,),
        [
            pl.BlockSpec((rows, width), lambda i: (i, 0)),
            pl.BlockSpec((rows, 128), lambda i: (i, 0)),
            pl.BlockSpec((1, 1, rows), lambda i: (i, 0, 0)),
            pl.BlockSpec((1, rows, 1), lambda i: (i, 0, 0)),
        ],
        [
            pl.BlockSpec((rows, width), lambda i: (i, 0)),
            pl.BlockSpec((1, heads, rows), lambda i: (i, 0, 0)),
        ],
        [pltpu.VMEM((width, rows), F32)],
        mib=16,
    )(q, kv, seg_row, seg_col)


def attention_backward(q, kv, grad, lse, seg_row, seg_col, cosine, sine, rows, which, before=None):
    width = q.shape[1]
    heads = width // HD
    old = [] if before is None else [before]

    def body(q_ref, kv_ref, grad_ref, lse_ref, row_ref, col_ref, cos_ref, sin_ref, *refs):
        out_ref, turned, total_k, total_v = refs[len(old) :]
        keys = kv_ref[:, :HD]
        values = kv_ref[:, HD:]
        keys_t = kv_ref[...].astype(F32).T[:HD].astype(BF)
        total_k[...] = jnp.zeros_like(total_k)
        total_v[...] = jnp.zeros_like(total_v)
        for begin, finish in query_blocks(rows):
            allowed = masks(row_ref[0], col_ref[0], rows, begin, finish)
            for h in range(heads):
                head = slice(h * HD, (h + 1) * HD)
                query, grads = q_ref[begin:finish, head], grad_ref[begin:finish, head]
                scores = dot_nt(keys[:finish], query) * 0.125
                scores = jnp.where(allowed, scores, -1e30)
                probs = jnp.exp(scores - lse_ref[0, h : h + 1, begin:finish])
                grad_probs = dot_nt(values[:finish], grads)
                inner = jnp.sum(probs * grad_probs, axis=0, keepdims=True)
                grad_scores = (probs * (grad_probs - inner)).astype(BF)
                turned[head, begin:finish] = dot(keys_t[:, :finish], grad_scores)
                total_k[:finish] += dot(grad_scores, query)
                total_v[:finish] += dot(probs.astype(BF), grads)
        cosv, sinv = cos_ref[...], -sin_ref[...]
        grad_q = turned[...].T * 0.125
        for block in lane_blocks(width, 128):
            out_ref[:, block] = rope(grad_q[:, block], cosv, sinv).astype(BF)
        grad_kv = jnp.concatenate([total_k[...] * 0.125, total_v[...]], axis=1)
        out_ref[:, width:] = rope_kv(grad_kv, cosv, sinv).astype(BF)

    group = lambda w: pl.BlockSpec((rows, w), lambda i: (which, 0))
    one = lambda *shape: pl.BlockSpec((1,) + shape, lambda i: (which, 0, 0))
    return pl.pallas_call(
        body,
        out_shape=struct((q.shape[0], width + 128), BF),
        grid=(1,),
        in_specs=[group(width), group(128), group(width), one(heads, rows), one(1, rows), one(rows, 1)]
        + [group(128), group(128)]
        + [HBM] * len(old),
        out_specs=group(width + 128),
        scratch_shapes=[
            pltpu.VMEM((width, rows), F32),
            pltpu.VMEM((rows, HD), F32),
            pltpu.VMEM((rows, HD), F32),
        ],
        input_output_aliases={8: 0} if old else {},
        name="attention_backward",
        compiler_params=pltpu.CompilerParams(vmem_limit_bytes=20 * 2**20),
        cost_estimate=pl.CostEstimate(flops=0, bytes_accessed=0, transcendentals=0),
    )(q, kv, grad, lse, seg_row, seg_col, cosine, sine, *old)


def pieces_of(rows, count):
    each = -(-rows // 16 // count) * 16
    cuts = [min(rows, i * each) for i in range(count)] + [rows]
    return [slice(x, y) for x, y in zip(cuts[:-1], cuts[1:])]


def project(lefts, slots, rows, name, split=2, mib=28):
    depth = slots[0].shape[0]
    cols = min(256, depth)
    per = cols // slots[0].step
    counts = [len(s.flat()) for s in slots]
    arrays = [b for s in slots for b in s.flat()]
    k, a = len(lefts), len(arrays)

    def body(*refs):
        left_refs, weights, out_refs = refs[:k], refs[k:][:a], refs[k + a :][: 1 + split]
        scratch = refs[k + a + 1 + split :]
        step = pl.program_id(0)
        copies, at = [], 0
        for j, (s, count) in enumerate(zip(slots, counts)):
            copies.append(s.copies(weights[at : at + count], scratch[2 * j], scratch[2 * j + 1]))
            at += count

        @pl.when(step == 0)
        def _():
            for i in range(len(copies[0])):
                for chain in copies:
                    for copy in chain[i]:
                        copy.start()

        for i in range(len(copies[0])):

            @pl.when(step == i // per)
            def _():
                for chain in copies:
                    for copy in chain[i]:
                        copy.wait()

        total = None
        block = pl.ds(pl.multiple_of(step * cols, cols), cols)
        for j in range(k):
            term = dot_nt(left_refs[j][...], scratch[2 * j][block, :])
            total = term if total is None else total + term
        out_refs[0][...] = total[:rows].astype(BF)
        for ref, part in zip(out_refs[1:], pieces):
            ref[...] = total[rows + part.start : rows + part.stop].astype(BF)

    pieces = pieces_of(rows, split)
    column = lambda r: pl.BlockSpec((r, cols), lambda i: (0, i))
    mine, *theirs = call(
        body,
        name,
        [struct((rows, depth), BF)] + [struct((p.stop - p.start, depth), BF) for p in pieces],
        (depth // cols,),
        [whole((2 * rows, left.shape[1])) for left in lefts] + [HBM] * a,
        [column(rows)] + [column(p.stop - p.start) for p in pieces],
        [x for s in slots for x in s.scratch()],
        mib=mib,
    )(*lefts, *arrays)
    return mine, theirs


def parts_of(depth, count):
    tiles_each = -(-depth // 128 // count)
    cuts = [min(depth, i * tiles_each * 128) for i in range(count)] + [depth]
    return [slice(x, y) for x, y in zip(cuts[:-1], cuts[1:])]


def join_cores(mine, came):
    rows, depth = mine.shape

    def body(mine_ref, *refs):
        at = 0
        for ref in refs[:-1]:
            part = slice(at, at + ref.shape[0])
            refs[-1][part] = (mine_ref[part].astype(F32) + ref[...].astype(F32)).astype(BF)
            at = part.stop

    return call(
        body,
        "join_cores",
        struct((rows, depth), BF),
        (1,),
        [whole((rows, depth))] + [whole(c.shape) for c in came],
        whole((rows, depth)),
        mib=16,
    )(mine, *came)


def mixer_forward(field, both, begin, rows, before=None):
    tile, depth = field.shape
    units = both.shape[1] // 2
    at = begin // tile
    arrays = both.flat()
    old = [] if before is None else list(before)

    def body(*refs):
        x = refs[0][...]
        weights, refs = refs[1 : 1 + len(arrays)], refs[1 + len(arrays) + len(old) :]
        lin_ref, act_ref, x_ref, mark_ref, mem, sem = refs
        x_ref[...] = x
        mark_ref[...] = jnp.zeros_like(mark_ref)
        copies = started(both.copies(weights, mem, sem))
        lin = product_as_it_comes(x, copies, mem, both.step)
        lin_ref[...] = lin.astype(BF)
        gate_value, lifted = lin[:, :units], lin[:, units:]
        act_ref[...] = (gate_value * jax.nn.sigmoid(gate_value) * lifted).astype(BF)

    block = lambda w: pl.BlockSpec((tile, w), lambda i: (at, 0))
    first = 1 + len(arrays)
    widths = [2 * units, units, depth]
    return pl.pallas_call(
        body,
        out_shape=[struct((rows, w), BF) for w in widths] + [struct((8, 128), F32)],
        grid=(1,),
        in_specs=[whole((tile, depth))] + [HBM] * (len(arrays) + len(old)),
        out_specs=[block(w) for w in widths] + [whole((8, 128))],
        scratch_shapes=both.scratch(),
        input_output_aliases={first + i: i for i in range(len(old))},
        name="mixer_forward",
        compiler_params=pltpu.CompilerParams(vmem_limit_bytes=58 * 2**20),
        cost_estimate=pl.CostEstimate(flops=0, bytes_accessed=0, transcendentals=0),
    )(field, *arrays, *old)


def mixer_backward(dy, down, lin):
    rows, depth = dy.shape
    units = down.shape[1]
    arrays = down.flat()
    tile = min(256, rows)

    def body(dy_ref, lin_ref, *refs):
        weights, grad_ref, (buffer, sem, act_ref) = refs[: len(arrays)], refs[-4], refs[-3:]

        @pl.when(pl.program_id(0) == 0)
        def _():
            copies = started(down.copies(weights, buffer, sem))
            act_ref[...] = product_as_it_comes(dy_ref, copies, buffer, down.step)

        @pl.when(pl.program_id(0) > 0)
        def _():
            act_ref[...] = dot(dy_ref[...], buffer[...])

        grad_act, gate_value = act_ref[...], lin_ref[:, :units].astype(F32)
        lifted = lin_ref[:, units:].astype(F32)
        s = jax.nn.sigmoid(gate_value)
        grad_ref[:, :units] = (
            grad_act * lifted * s * (1.0 + gate_value * (1.0 - s))
        ).astype(BF)
        grad_ref[:, units:] = (grad_act * (gate_value * s)).astype(BF)

    return call(
        body,
        "mixer_backward",
        struct((rows, 2 * units), BF),
        (rows // tile,),
        [tiles(depth, tile), tiles(2 * units, tile)] + [HBM] * len(arrays),
        tiles(2 * units, tile),
        down.scratch() + [pltpu.VMEM((tile, units), F32)],
        mib=28,
    )(dy, lin, *arrays)


def attended_backward(mine, theirs, out):
    rows, depth = mine[0].shape[0], out.shape[0]
    width = out.shape[1]
    half = rows // TILE
    arrays = out.flat()
    k = len(mine)

    def body(*refs):
        own = pl.program_id(0) < half
        x = jnp.concatenate(
            [jnp.where(own, a[...], b[...]) for a, b in zip(refs[:k], refs[k : 2 * k])], axis=1
        )
        refs = refs[2 * k :]
        weights, (grad_ref, both_ref), (buffer, sem) = (
            refs[: len(arrays)],
            refs[len(arrays) : -2],
            refs[-2:],
        )
        both_ref[...] = x

        @pl.when(pl.program_id(0) == 0)
        def _():
            copies = started(out.copies(weights, buffer, sem))
            grad_ref[...] = product_as_it_comes(x, copies, buffer, out.step).astype(BF)

        @pl.when(pl.program_id(0) > 0)
        def _():
            grad_ref[...] = dot(x, buffer[...]).astype(BF)

    own_rows = [pl.BlockSpec((TILE, m.shape[1]), lambda i: (jnp.minimum(i, half - 1), 0)) for m in mine]
    their_rows = [pl.BlockSpec((TILE, m.shape[1]), lambda i: (jnp.maximum(i - half, 0), 0)) for m in mine]
    return call(
        body,
        "attended_backward",
        [struct((2 * rows, width), BF), struct((2 * rows, depth), BF)],
        (2 * half,),
        own_rows + their_rows + [HBM] * len(arrays),
        [tiles(width), tiles(depth)],
        out.scratch(),
        mib=16,
    )(*mine, *theirs, *arrays)


def norm_forward(x, mine, other, gain, rows):
    depth = x.shape[1]

    def body(x_ref, gain_ref, mine_ref, other_ref, resid_ref, normed_ref):
        resid = x_ref[...].astype(F32) + (mine_ref[...].astype(F32) + other_ref[...].astype(F32))
        resid_ref[...] = resid
        normed_ref[...] = (resid * rms_scale(resid) * gain_ref[...]).astype(BF)

    return call(
        body,
        "norm_forward",
        [struct((rows, depth), F32), struct((rows, depth), BF)],
        (rows // TILE,),
        [tiles(depth), whole((1, depth)), tiles(depth), tiles(depth)],
        [tiles(depth)] * 2,
        mib=24,
    )(x, gain, mine, other)


def norm_backward(resid, mine, other, dy, gain, rows):
    depth = dy.shape[1]
    parts = parts_of(depth, 2)

    def body(resid_ref, dy_ref, gain_ref, mine_ref, other_ref, *branch_refs):
        resid = resid_ref[...]
        grad_normed = mine_ref[...].astype(F32) + other_ref[...].astype(F32)
        grad = norm_back(resid, rms_scale(resid), gain_ref[...], grad_normed)
        grad = grad + dy_ref[...].astype(F32)
        for ref, block in zip(branch_refs, parts):
            ref[...] = grad[:, block].astype(BF)

    return call(
        body,
        "norm_backward",
        [struct((rows, p.stop - p.start), BF) for p in parts],
        (rows // TILE,),
        [tiles(depth), tiles(depth), whole((1, depth)), tiles(depth), tiles(depth)],
        [tiles(p.stop - p.start) for p in parts],
        mib=28,
    )(resid, dy, gain, mine, other)


def leave_ring(fn, arrays, gain, order, wide, rows, name, mib=32):
    depth = gain.shape[1]
    n = depth // wide
    if wide % 128 or rows % TILE:
        field = fn(*[a[:rows] for a in arrays], gain).astype(BF)
        back = jnp.zeros((n,), jnp.int32).at[order].set(jnp.arange(n, dtype=jnp.int32))
        return jnp.take(field.reshape(rows, n, wide), back, axis=1).reshape(rows, depth)
    k = len(arrays)

    def body(order_ref, *refs):
        field = fn(*[r[...] for r in refs[:k]], refs[k][...]).astype(BF)
        for i, block in enumerate(lane_blocks(depth, wide)):
            refs[k + 1][:, pl.ds(pl.multiple_of(order_ref[i] * wide, wide), wide)] = field[:, block]

    return call(
        body,
        name,
        struct((rows, depth), BF),
        (rows // TILE,),
        [tiles(a.shape[1]) for a in arrays] + [whole((1, depth))],
        tiles(depth),
        prefetch=1,
        mib=mib,
    )(order, *arrays, gain)


def turned(block):
    return block.astype(F32).T.astype(BF)


def fetch(pairs, sem):
    copies = [pltpu.make_async_copy(a, b, sem.at[i]) for i, (a, b) in enumerate(pairs)]
    for copy in copies:
        copy.start()
    for copy in copies:
        copy.wait()


def columns(ref, half):
    size = ref.shape[1] // 2
    return ref.at[:, pl.ds(pl.multiple_of(half * size, 128), size)]


def rows_of(ref, half):
    size = ref.shape[0] // 2
    return ref.at[pl.ds(pl.multiple_of(half * size, 128), size), :]


def halves(core, w_query, w_key, w_value, w_output, gain_attend, gain_mixer):
    part, q_cols = w_query.shape[0], w_query.shape[1] // 2
    k_cols = w_key.shape[1] // 2
    width, out_width = q_cols + 2 * k_cols, w_output.shape[0] // 2

    def body(
        core_ref, q_ref, k_ref, v_ref, o_ref, one_ref, two_ref, qkv_ref, out_ref, k_mem, v_mem, o_mem, sem
    ):
        there = 1 - core_ref[0]
        low = there == 0
        fetch(
            [
                (columns(q_ref, there), qkv_ref.at[pl.ds(0, part), pl.ds(0, q_cols)]),
                (k_ref, k_mem),
                (v_ref, v_mem),
                (rows_of(o_ref, there), o_mem),
            ],
            sem,
        )
        k, v = k_mem[...], v_mem[...]
        qkv_ref[:part, q_cols:] = jnp.concatenate(
            [jnp.where(low, w[:, :k_cols], w[:, k_cols:]) for w in (k, v)], axis=1
        )
        qkv_ref[part:, :] = jnp.zeros((16, width), BF)
        qkv_ref[part : part + 1, :part] = one_ref[...]
        qkv_ref[part + 1 : part + 2, :part] = two_ref[...]
        out_ref[...] = turned(o_mem[...])

    shapes = [(part + 16, width), (part, out_width)]
    return call(
        body,
        "halves",
        [struct(shape, BF) for shape in shapes],
        (1,),
        [HBM] * 4 + [whole((1, part))] * 2,
        [whole(shape) for shape in shapes],
        [
            pltpu.VMEM((part, 2 * k_cols), BF),
            pltpu.VMEM((part, 2 * k_cols), BF),
            pltpu.VMEM((out_width, part), BF),
            pltpu.SemaphoreType.DMA((4,)),
        ],
        prefetch=1,
        mib=58,
    )(core, w_query, w_key, w_value, w_output, gain_attend, gain_mixer)


def mixer_halves(core, w_gate, w_up, w_down):
    part, units = w_gate.shape[0], w_gate.shape[1] // 2

    def body(core_ref, gate_ref, up_ref, down_ref, mixer_ref, down_mem, sem):
        there = 1 - core_ref[0]
        fetch(
            [
                (columns(gate_ref, there), mixer_ref.at[:, pl.ds(0, units)]),
                (columns(up_ref, there), mixer_ref.at[:, pl.ds(units, units)]),
                (rows_of(down_ref, there), down_mem),
            ],
            sem,
        )
        mixer_ref[:, 2 * units :] = turned(down_mem[...])

    return call(
        body,
        "mixer_halves",
        struct((part, 3 * units), BF),
        (1,),
        [HBM] * 3,
        whole((part, 3 * units)),
        [pltpu.VMEM((units, part), BF), pltpu.SemaphoreType.DMA((3,))],
        prefetch=1,
        mib=58,
    )(core, w_gate, w_up, w_down)


def put_rows(core_ref, out_ref, mine, came, part, cols=slice(None)):
    @pl.when(core_ref[0] == 0)
    def _():
        out_ref[:part, cols], out_ref[part : 2 * part, cols] = mine, came

    @pl.when(core_ref[0] == 1)
    def _():
        out_ref[:part, cols], out_ref[part : 2 * part, cols] = came, mine


def chip_rows(core, w_query, w_key, w_value, w_output, gain_attend, gain_mixer, came, came_out):
    part, q_cols = w_query.shape[0], w_query.shape[1] // 2
    k_cols = w_key.shape[1] // 2
    width, out_width = came.shape[1], came_out.shape[1]

    def body(
        core_ref, q_ref, k_ref, v_ref, o_ref, one_ref, two_ref, came_ref, came_out_ref,
        qkv_ref, out_ref, q_mem, k_mem, v_mem, o_mem, sem,
    ):
        here = core_ref[0]
        first = here == 0
        fetch(
            [
                (columns(q_ref, here), q_mem),
                (k_ref, k_mem),
                (v_ref, v_mem),
                (rows_of(o_ref, here), o_mem),
            ],
            sem,
        )
        k, v = k_mem[...], v_mem[...]
        own = [jnp.where(first, w[:, :k_cols], w[:, k_cols:]) for w in (k, v)]
        put_rows(core_ref, qkv_ref, jnp.concatenate([q_mem[...]] + own, axis=1), came_ref[:part], part)
        put_rows(core_ref, out_ref, turned(o_mem[...]), came_out_ref[...], part)
        qkv_ref[2 * part :, :] = jnp.zeros((16, width), BF)
        for row, ref in enumerate((one_ref, two_ref)):
            mine, other = ref[...], came_ref[part + row : part + row + 1, :part]
            at = slice(2 * part + row, 2 * part + row + 1)
            qkv_ref[at, :part] = jnp.where(first, mine, other)
            qkv_ref[at, part : 2 * part] = jnp.where(first, other, mine)

    return call(
        body,
        "chip_rows",
        [struct((2 * part + 16, width), BF), struct((2 * part, out_width), BF)],
        (1,),
        [HBM] * 4 + [whole((1, part))] * 2 + [whole(came.shape), whole(came_out.shape)],
        [whole((2 * part + 16, width)), whole((2 * part, out_width))],
        [
            pltpu.VMEM((part, q_cols), BF),
            pltpu.VMEM((part, 2 * k_cols), BF),
            pltpu.VMEM((part, 2 * k_cols), BF),
            pltpu.VMEM((out_width, part), BF),
            pltpu.SemaphoreType.DMA((4,)),
        ],
        prefetch=1,
        mib=58,
    )(core, w_query, w_key, w_value, w_output, gain_attend, gain_mixer, came, came_out)


def mixer_rows(core, w_gate, w_up, w_down, came):
    part, units = w_gate.shape[0], w_gate.shape[1] // 2

    def body(core_ref, gate_ref, up_ref, down_ref, came_ref, both_ref, turned_ref, gate_mem, up_mem, down_mem, sem):
        here = core_ref[0]
        fetch(
            [
                (columns(gate_ref, here), gate_mem),
                (columns(up_ref, here), up_mem),
                (rows_of(down_ref, here), down_mem),
            ],
            sem,
        )
        for i, mem in enumerate((gate_mem, up_mem)):
            cols = slice(i * units, (i + 1) * units)
            put_rows(core_ref, both_ref, mem[...], came_ref[:, cols], part, cols)
        put_rows(core_ref, turned_ref, turned(down_mem[...]), came_ref[:, 2 * units :], part)

    shapes = [(2 * part, 2 * units), (2 * part, units)]
    return call(
        body,
        "mixer_rows",
        [struct(shape, BF) for shape in shapes],
        (1,),
        [HBM] * 3 + [whole(came.shape)],
        [whole(shape) for shape in shapes],
        [pltpu.VMEM((part, units), BF)] * 2
        + [pltpu.VMEM((units, part), BF), pltpu.SemaphoreType.DMA((3,))],
        prefetch=1,
        mib=58,
    )(core, w_gate, w_up, w_down, came)


def beside(core, mine, came, turn):
    part, width = mine.shape
    shape = (2 * width, part) if turn else (part, 2 * width)

    def body(core_ref, mine_ref, came_ref, out_ref):
        def put(low, high):
            if turn:
                out_ref[:width], out_ref[width:] = low[...].T, high[...].T
            else:
                out_ref[:, :width], out_ref[:, width:] = low[...], high[...]

        @pl.when(core_ref[0] == 0)
        def _():
            put(mine_ref, came_ref)

        @pl.when(core_ref[0] == 1)
        def _():
            put(came_ref, mine_ref)

    return call(
        body,
        "beside",
        struct(shape, F32),
        (1,),
        [whole((part, width))] * 2,
        whole(shape),
        prefetch=1,
        mib=16,
    )(core, mine, came)


def after(value, *others):
    return lax.optimization_barrier((value,) + others)[0]


class Ring:
    def __init__(self, devices):
        self.n = devices // 2
        n = self.n
        order = list(range(0, n, 2)) + list(range(n - 1 - n % 2, 0, -2))
        self.order = order
        place = [0] * n
        for position, chip in enumerate(order):
            place[chip] = position
        self.place = place
        self.steps = {1: [], -1: []}
        for position, chip in enumerate(order):
            then = order[(position + 1) % n]
            for core in (0, 1):
                self.steps[1].append((2 * chip + core, 2 * then + core))
                self.steps[-1].append((2 * then + core, 2 * chip + core))
        self.cores = [(i, i ^ 1) for i in range(devices)]
        self.hops = n // 2

    def pass_on(self, block, way):
        return lax.ppermute(block, "dp", self.steps[way])

    def halves(self, width):
        cut = min(width, (width // 2 + 127) // 128 * 128)
        return slice(0, cut), slice(cut, width)

    def swap(self, block):
        return lax.ppermute(block, "dp", self.cores)


class Gather:
    def __init__(self, ring, block):
        self.ring, self.hop = ring, 0
        self.found = [[block]] + [None] * (ring.n - 1)
        self.last = (block,)

    def step(self, *others):
        ring, n = self.ring, self.ring.n
        self.hop += 1
        hop = self.hop
        if 2 * hop > n:
            return
        before = [self.found[(hop - 1) * way % n][0] for way in (1, -1)]
        if others:
            before = [after(b, *others) for b in before]
        if 2 * hop < n:
            for way, block in zip((1, -1), before):
                self.found[hop * way % n] = [ring.pass_on(block, way)]
            self.last = tuple(self.found[hop * way % n][0] for way in (1, -1))
        else:
            parts = ring.halves(before[0].shape[1])
            self.found[hop] = [
                ring.pass_on(b[:, part], way) for b, way, part in zip(before, (1, -1), parts)
            ]
            self.last = tuple(self.found[hop])

    def finish(self):
        while 2 * (self.hop + 1) <= self.ring.n:
            self.step()
        return self.found


class Line:
    def __init__(self):
        self.marks = ()

    def after(self, value):
        return after(value, *self.marks) if self.marks else value

    def mark(self, *found):
        self.marks = found

    def wait(self, *found):
        self.marks = self.marks + found


class Scatter:
    def __init__(self, ring, line, field, grads):
        self.ring, self.line, self.field, self.grads = ring, line, field, grads
        self.width, self.hop = grads.shape[1], 0
        self.wide = field.shape[1] // ring.n
        self.held = {1: None, -1: None}
        self.last = ()

    def term(self, i, part):
        field = self.line.after(self.field)
        return dot_tn(field[:, i * self.wide : (i + 1) * self.wide], self.grads[:, part])

    def step(self):
        ring, n = self.ring, self.ring.n
        far = n // 2 - self.hop
        if far == 0:
            return
        self.hop += 1
        for way, part in zip((1, -1), ring.halves(self.width)):
            if 2 * far == n:
                total = self.term(far, part)
            else:
                part = slice(0, self.width)
                total = self.term(-far * way % n, part) + self.came(way)
            total = total.astype(BF)
            self.line.mark(total)
            self.held[way] = (ring.pass_on(total, way), part)
        self.last = tuple(self.held[way][0] for way in (1, -1))

    def came(self, way):
        if self.held[way] is None:
            return 0.0
        came, part = self.held[way]
        edges = ((0, 0, 0), (part.start, self.width - part.stop, 0))
        return lax.pad(came.astype(F32), jnp.zeros((), F32), edges)

    def finish(self):
        while self.hop < self.ring.n // 2:
            self.step()
        total = self.term(0, slice(0, self.width)) + self.came(1) + self.came(-1)
        self.line.mark(total)
        return total


def half_of(w, half, axis):
    size = w.shape[axis] // 2
    return lax.dynamic_slice_in_dim(w, half * size, size, axis)


def slow_rows(core, swap, pick):
    mine, came = pick(core), swap(pick(1 - core))
    first = core == 0
    return jnp.where(first, mine, came), jnp.where(first, came, mine)


def slow_attend_rows(core, swap, w_query, w_key, w_value, w_output, gain_attend, gain_mixer):
    part = w_query.shape[0]
    qkv = slow_rows(
        core,
        swap,
        lambda half: jnp.concatenate([half_of(w, half, 1) for w in (w_query, w_key, w_value)], axis=1),
    )
    out = slow_rows(core, swap, lambda half: half_of(w_output, half, 0).T)
    gains = slow_rows(core, swap, lambda half: jnp.concatenate([gain_attend, gain_mixer]))
    below = jnp.concatenate(gains, axis=1)
    below = jnp.pad(below, ((0, 14), (0, qkv[0].shape[1] - 2 * part)))
    return jnp.concatenate(qkv + (below,)), jnp.concatenate(out)


def slow_mixer_rows(core, swap, w_gate, w_up, w_down):
    picks = (
        lambda half: half_of(w_gate, half, 1),
        lambda half: half_of(w_up, half, 1),
        lambda half: half_of(w_down, half, 0).T,
    )
    gate, up, down = [jnp.concatenate(slow_rows(core, swap, pick)) for pick in picks]
    return jnp.concatenate([gate, up], axis=1), down


def per_device(
    shape,
    tokens,
    segments,
    gain_attend,
    w_query,
    w_key,
    w_value,
    w_output,
    gain_mixer,
    w_gate,
    w_up,
    w_down,
    cotangent,
):
    devices, tensors = shape
    ring = Ring(devices)
    swap = ring.swap
    n = ring.n
    rows, depth = tokens.shape
    part = depth // devices
    wide = 2 * part
    index = lax.axis_index("dp")
    core = index % 2
    first = core == 0
    position = jnp.asarray(ring.place, jnp.int32)[index // 2]
    blocks = jnp.asarray(ring.order, jnp.int32)[(position - jnp.arange(n, dtype=jnp.int32)) % n]

    def across(block):
        if tensors == 1:
            return jnp.zeros_like(block)
        return lax.ppermute(block, "tensor", [(i, i ^ 1) for i in range(tensors)])

    line = Line()

    q_cols = w_query.shape[1] // 2
    k_cols = w_key.shape[1] // 2
    all_cols = q_cols + 2 * k_cols
    attend = (w_query, w_key, w_value, w_output, gain_attend[None], gain_mixer[None])
    mixer = (w_gate, w_up, w_down)
    which = core.astype(jnp.int32)[None]
    if part % 128:
        tokens_came, cotangent_came, segments_came = swap(tokens), swap(cotangent), swap(segments)
        qkv_block, out_block = slow_attend_rows(core, swap, *attend)
        both_block, down_block = slow_mixer_rows(core, swap, *mixer)
    else:
        sent = halves(which, *attend)
        line.mark(*sent)
        sent_mixer = mixer_halves(line.after(which), *mixer)
        line.mark(sent_mixer)
        sent = [swap(s) for s in sent]
        segments_came = swap(segments)
        tokens_came, cotangent_came = swap(after(tokens, *sent)), swap(after(cotangent, *sent))
        mixer_came = swap(after(sent_mixer, *sent))
        qkv_block, out_block = chip_rows(line.after(which), *attend, *sent)
        came = (tokens_came, cotangent_came, segments_came, mixer_came)
        qkv_block, out_block = after(qkv_block, *came), after(out_block, *came)
        line.mark(qkv_block)
        both_block, down_block = mixer_rows(line.after(which), *mixer, mixer_came)
        line.mark(both_block)

    ring_q, ring_o = Gather(ring, qkv_block), Gather(ring, out_block)
    ring_q.step()
    ring_o.step()
    segs = jnp.stack([segments, segments_came])
    places = jnp.arange(rows, dtype=jnp.int32)
    fresh = jnp.concatenate([jnp.ones((2, 1), dtype=bool), segs[:, 1:] != segs[:, :-1]], axis=1)
    starts = lax.cummax(jnp.where(fresh, places, 0), axis=1)
    lanes = jnp.arange(128, dtype=jnp.int32)
    freqs = jnp.exp((lanes % (HD // 2)).astype(F32) * (-2.0 * math.log(10000.0) / HD))
    angle = (places - starts).astype(F32).reshape(2 * rows, 1) * freqs[None, :]
    seg_row, seg_col = segs.reshape(2, 1, rows), segs.reshape(2, rows, 1)
    x = to_ring(line.after(tokens), tokens_came, blocks, wide)
    line.mark(x, *ring_q.last)
    ring_q.step(x)
    angle = line.after(angle)
    cosine = jnp.cos(angle)
    sine = jnp.sin(angle) * jnp.where(lanes % HD < HD // 2, -1.0, 1.0)
    line.mark(cosine, *ring_o.last)
    ring_o.step(cosine)
    dy = to_ring(line.after(cotangent), cotangent_came, blocks, wide)
    line.mark(dy, *ring_q.last)
    ring_q.step(dy)
    line.wait(*ring_o.last)
    ring_o.step(dy)
    line.wait(*ring_q.last)
    ring_q.step()
    line.wait(*ring_o.last)
    ring_o.step()
    line.wait(*ring_q.last, *ring_o.last)
    qkv_parts = ring_q.finish()
    w_out = Slots(ring_o.finish(), wide)
    w_qkv = Slots(qkv_parts, wide)
    ring_g, ring_d = Gather(ring, both_block), Gather(ring, down_block)
    ring_g.step(*ring_q.last, *ring_o.last)

    def gain_of(row):
        return jnp.concatenate(
            [p[0][wide + row : wide + row + 1, :wide] for p in qkv_parts], axis=1
        ).astype(F32)

    gain_one, gain_two = gain_of(0), gain_of(1)

    def swap_all(pieces):
        return [swap(piece) for piece in pieces]

    def swap_late(pieces):
        return [swap(line.after(piece)) for piece in pieces]

    def joined(mine, came):
        mine = join_cores(line.after(mine), came)
        line.mark(mine)
        return mine

    def own(field, which):
        return lax.dynamic_slice_in_dim(field, which * part, part, 0)

    def send(field):
        rows_there = own(line.after(field), 1 - core)
        line.mark(rows_there)
        return field, swap(rows_there)

    def spread(pair):
        mine, came = own(line.after(pair[0]), core), pair[1]
        return jnp.where(first, mine, came), jnp.where(first, came, mine)

    def spread_turned(pair):
        mine, came = own(line.after(pair[0]), core), pair[1]
        if part % 128:
            low, high = jnp.where(first, mine, came), jnp.where(first, came, mine)
            return jnp.concatenate([low, high], axis=1).T
        return beside(which, mine, came, True)

    def done(*found):
        line.mark(*found)
        return found[0]

    def gain_grad(pairs):
        return sum(jnp.sum(w.astype(F32) * g, axis=1) for w, g in pairs)

    normed_one, queries, kv = qkv_forward(line.after(x), gain_one, w_qkv, cosine, sine)
    line.mark(normed_one)
    attended, lse = attention_forward(line.after(queries), kv, seg_row, seg_col, rows)
    line.mark(attended, *ring_g.last)
    ring_g.step(attended)
    mine, theirs = project([line.after(attended)], [w_out], rows, "attended_out", 3, 58)
    line.mark(mine)
    mine = joined(mine, swap_late(theirs))
    other = across(mine)
    line.wait(*ring_g.last)
    ring_g.step(*line.marks)
    ring_d.step(*line.marks)
    resid, normed_mine = norm_forward(x, line.after(mine), other, gain_two, rows)
    line.mark(resid, *ring_g.last)
    came = swap(line.after(normed_mine))
    ring_g.step(resid)
    both = Slots(ring_g.finish(), wide)
    line.wait(*ring_d.last)
    ring_d.step()
    *first_rows, mark = mixer_forward(line.after(normed_mine), both, 0, 2 * rows)
    line.mark(mark, *ring_d.last)
    ring_d.step(*line.marks)
    lin, act, normed_two, mark = mixer_forward(line.after(came), both, rows, 2 * rows, first_rows)
    line.mark(mark)

    grad_down = Scatter(ring, line, dy, act)
    grad_down.step()
    line.wait(*ring_d.last)
    ring_d.step(*line.marks)
    grad_down.step()
    line.wait(*ring_d.last)
    down = Slots(ring_d.finish(), wide)
    grad_lin = mixer_backward(line.after(dy), down, lin)
    line.mark(grad_lin)
    grad_both = Scatter(ring, line, normed_two, grad_lin)
    grad_both.step()
    line.wait(*grad_down.last)
    grad_down.step()
    mine, theirs = project([line.after(grad_lin)], [both], rows, "grad_normed_two")
    line.mark(mine, *grad_both.last, *grad_down.last)
    came = swap_late(theirs)
    grad_both.step()
    mine = joined(mine, came)
    other = across(mine)
    grad_down.step()
    out_mine, out_theirs = project([line.after(act)], [down], rows, "act_out")
    line.mark(out_mine, *grad_both.last)
    came = swap_late(out_theirs)
    grad_both.step()
    out_mine = joined(out_mine, came)
    line.wait(other, *grad_down.last)
    out_other = across(line.after(out_mine))
    branch_mine = list(norm_backward(resid, line.after(mine), other, dy, gain_two, rows))
    branch_parts = list(branch_mine)
    line.mark(*branch_mine)
    came = swap_all(branch_mine)
    branch_mine[0] = line.after(branch_mine[0])
    grad_attended, grad_branch = attended_backward(branch_mine, came, w_out)
    line.mark(grad_attended)
    pieces = (kv, grad_attended, lse, seg_row, seg_col, cosine, sine, rows)
    grad_qkv = attention_backward(line.after(queries), *pieces, 0)
    line.mark(grad_qkv)
    grad_qkv = attention_backward(line.after(queries), *pieces, 1, grad_qkv)
    line.mark(grad_qkv, *grad_both.last)
    grad_out = Scatter(ring, line, grad_branch, attended)
    grad_out.step()
    grad_projections = Scatter(ring, line, normed_one, grad_qkv)
    grad_projections.step()
    mine, theirs = project([line.after(grad_qkv)], [w_qkv], rows, "grad_normed_one")
    line.mark(mine, *grad_out.last, *grad_projections.last)
    grad_projections.step()
    grad_both.step()
    line.wait(out_other)
    came = swap_late(theirs)
    mine = joined(mine, came)
    other = across(mine)
    line.wait(*grad_projections.last)
    grad_out.step()
    down_sum = send(grad_down.finish())
    output = leave_ring(
        lambda r, m, o, _: r + (m.astype(F32) + o.astype(F32)),
        [line.after(resid), out_mine, out_other],
        gain_two,
        blocks,
        wide,
        rows,
        "leave_output",
    )
    line.mark(output)
    g_down = done(spread_turned(down_sum))
    grad_projections.step()

    def leave(mine, other, x, low, high, gain):
        x = x.astype(F32)
        grad_resid = jnp.concatenate([low.astype(F32), high.astype(F32)], axis=1)
        grad_normed = mine.astype(F32) + other.astype(F32)
        return grad_resid + norm_back(x, rms_scale(x), gain, grad_normed)

    line.wait(other, *grad_both.last)
    grad_out.step()
    grad_projections.step()
    both_sum = grad_both.finish()
    grad_out.step()
    grad_tokens = leave_ring(
        leave, [mine, other, line.after(x), *branch_parts], gain_one, blocks, wide, rows, "leave_grad_tokens"
    )
    line.mark(grad_tokens)
    qkv_sum = grad_projections.finish()
    out_sum = grad_out.finish()
    qkv_sum, both_sum, out_sum = send(qkv_sum), send(both_sum), send(out_sum)
    low, high = spread(both_sum)
    units = low.shape[1] // 2
    g_gate = done(jnp.concatenate([low[:, :units], high[:, :units]], axis=1))
    g_up = done(jnp.concatenate([low[:, units:], high[:, units:]], axis=1))
    g_two = done(gain_grad([(line.after(w_gate), g_gate), (w_up, g_up)]))
    g_two = (g_two + across(line.after(g_two))) / gain_mixer.astype(F32)
    low, high = spread(qkv_sum)
    g_out = spread_turned(out_sum)

    def sides(begin, finish):
        return jnp.concatenate([low[:, begin:finish], high[:, begin:finish]], axis=1)

    g_query = sides(0, q_cols)
    g_key = sides(q_cols, q_cols + k_cols)
    g_value = sides(q_cols + k_cols, all_cols)
    g_one = gain_grad([(w_query, g_query), (w_key, g_key), (w_value, g_value)])
    g_one = (g_one + across(g_one)) / gain_attend.astype(F32)
    return output, grad_tokens, g_one, g_query, g_key, g_value, g_out, g_two, g_gate, g_up, g_down


def solution(mesh):
    shape = (mesh.shape["dp"], mesh.shape["tensor"])
    rows, weight_in, weight_out = P("dp", None), P("dp", "tensor"), P("tensor", "dp")
    attend = (P("dp"), weight_in, weight_in, weight_in, weight_out)
    mixer = (P("dp"), weight_in, weight_in, weight_out)

    def layer(*arguments):
        return per_device(shape, *arguments)

    return jax.shard_map(
        layer,
        mesh=mesh,
        in_specs=(rows, P("dp")) + attend + mixer + (rows,),
        out_specs=(rows, rows) + attend + mixer,
        check_vma=False,
    )
```

```python
import functools
import math

import jax
import jax.numpy as jnp
from jax import lax
from jax.experimental import pallas as pl
from jax.experimental.pallas import tpu as pltpu
from jax.sharding import PartitionSpec as P

HD = 64
EPSILON = 1e-05
BF = jnp.bfloat16
F32 = jnp.float32
TILE = 256


def rms_scale(values):
    return lax.rsqrt(jnp.mean(values * values, axis=-1, keepdims=True) + EPSILON)


def norm_back(resid, rstd, gain, grad_normed):
    scaled = gain * grad_normed
    inner = jnp.mean(scaled * resid, axis=-1, keepdims=True)
    return rstd * scaled - resid * (rstd * rstd * rstd) * inner


def dot(a, b):
    return jnp.dot(a, b, preferred_element_type=F32)


def dot_tn(a, b):
    return lax.dot_general(a, b, (((0,), (0,)), ((), ())), preferred_element_type=F32)


def dot_nt(a, b):
    return lax.dot_general(a, b, (((1,), (1,)), ((), ())), preferred_element_type=F32)


def call(body, name, out_shape, grid, in_specs, out_specs, scratch=(), prefetch=0, mib=24):
    spec = pltpu.PrefetchScalarGridSpec(
        num_scalar_prefetch=prefetch,
        grid=grid,
        in_specs=in_specs,
        out_specs=out_specs,
        scratch_shapes=list(scratch),
    )
    return pl.pallas_call(
        body,
        out_shape=out_shape,
        grid_spec=spec,
        name=name,
        compiler_params=pltpu.CompilerParams(
            vmem_limit_bytes=mib * 2**20, dimension_semantics=("arbitrary",) * len(grid)
        ),
        cost_estimate=pl.CostEstimate(flops=0, bytes_accessed=0, transcendentals=0),
    )


def struct(shape, dtype):
    return jax.ShapeDtypeStruct(shape, dtype)


def tiles(width, tile=TILE):
    return pl.BlockSpec((tile, width), lambda i, *_: (i, 0))


def whole(shape):
    return pl.BlockSpec(shape, lambda *_: (0,) * len(shape), pipeline_mode=pl.Buffered(1))


HBM = pl.BlockSpec(memory_space=pltpu.HBM)


class Slots:
    def __init__(self, parts, step):
        self.parts = parts
        self.step = step
        self.shape = (len(parts) * step, sum(p.shape[1] for p in parts[0]))

    def flat(self):
        return [p for pieces in self.parts for p in pieces]

    def scratch(self):
        return [pltpu.VMEM(self.shape, BF), pltpu.SemaphoreType.DMA((len(self.flat()),))]

    def copies(self, refs, buffer, sem):
        found, k = [], 0
        for i, pieces in enumerate(self.parts):
            at, mine = 0, []
            for piece in pieces:
                source, cols = refs[k], piece.shape[1]
                if piece.shape[0] != self.step:
                    source = source.at[pl.ds(0, self.step), :]
                target = buffer.at[pl.ds(i * self.step, self.step), pl.ds(at, cols)]
                mine.append(pltpu.make_async_copy(source, target, sem.at[k]))
                at += cols
                k += 1
            found.append(mine)
        return found


def started(copies):
    for pieces in copies:
        for copy in pieces:
            copy.start()
    return copies


def product_as_it_comes(x, copies, buffer, step):
    total = None
    group = max(1, 512 // step)
    for i in range(0, len(copies), group):
        for pieces in copies[i : i + group]:
            for copy in pieces:
                copy.wait()
        rows = slice(i * step, min(i + group, len(copies)) * step)
        term = dot(x[:, rows], buffer[rows])
        total = term if total is None else total + term
    return total


def lane_blocks(width, wide):
    return [slice(i * wide, (i + 1) * wide) for i in range(width // wide)]


def to_ring(mine, theirs, order, wide):
    rows, depth = mine.shape
    n = depth // wide
    if wide % 128 or rows % TILE:
        both = jnp.concatenate([mine, theirs], axis=0)
        return jnp.take(both.reshape(2 * rows, n, wide), order, axis=1).reshape(2 * rows, depth)
    half = rows // TILE

    def body(order_ref, mine_ref, theirs_ref, out_ref):
        def put(ref):
            for i, block in enumerate(lane_blocks(depth, wide)):
                out_ref[:, block] = ref[:, pl.ds(pl.multiple_of(order_ref[i] * wide, wide), wide)]

        @pl.when(pl.program_id(0) < half)
        def _():
            put(mine_ref)

        @pl.when(pl.program_id(0) >= half)
        def _():
            put(theirs_ref)

    return call(
        body,
        "to_ring",
        struct((2 * rows, depth), mine.dtype),
        (2 * half,),
        [
            pl.BlockSpec((TILE, depth), lambda i, o: (jnp.minimum(i, half - 1), 0)),
            pl.BlockSpec((TILE, depth), lambda i, o: (jnp.maximum(i - half, 0), 0)),
        ],
        pl.BlockSpec((TILE, depth), lambda i, o: (i, 0)),
        prefetch=1,
        mib=12,
    )(order, mine, theirs)


def rope(block, cosine, sine):
    lane = lax.broadcasted_iota(jnp.int32, block.shape, 1)
    low = lane % HD < HD // 2
    other = jnp.where(low, pltpu.roll(block, 128 - HD // 2, 1), pltpu.roll(block, HD // 2, 1))
    return block * cosine + other * sine


def rope_kv(block, cosine, sine):
    lane = lax.broadcasted_iota(jnp.int32, block.shape, 1)
    return jnp.where(lane < HD, rope(block, cosine, sine), block)


def qkv_forward(x, gain, slots, cosine, sine):
    rows, depth = x.shape
    width = slots.shape[1]
    arrays = slots.flat()

    def body(x_ref, gain_ref, cos_ref, sin_ref, *refs):
        weights, (normed_ref, q_ref, kv_ref), (buffer, sem, qkv_ref) = (
            refs[: len(arrays)],
            refs[len(arrays) : -3],
            refs[-3:],
        )
        field = x_ref[...].astype(F32)
        normed = (field * rms_scale(field) * gain_ref[...]).astype(BF)
        normed_ref[...] = normed

        @pl.when(pl.program_id(0) == 0)
        def _():
            copies = started(slots.copies(weights, buffer, sem))
            qkv_ref[...] = product_as_it_comes(normed, copies, buffer, slots.step)

        @pl.when(pl.program_id(0) > 0)
        def _():
            qkv_ref[...] = dot(normed, buffer[...])

        cosv, sinv = cos_ref[...], sin_ref[...]
        for block in lane_blocks(width - 128, 128):
            q_ref[:, block] = rope(qkv_ref[:, block], cosv, sinv).astype(BF)
        kv_ref[...] = rope_kv(qkv_ref[:, width - 128 :], cosv, sinv).astype(BF)

    return call(
        body,
        "qkv_forward",
        [
            struct((rows, depth), BF),
            struct((rows, width - 128), BF),
            struct((rows, 128), BF),
        ],
        (rows // TILE,),
        [tiles(depth), whole((1, depth)), tiles(128), tiles(128)] + [HBM] * len(arrays),
        [tiles(depth), tiles(width - 128), tiles(128)],
        slots.scratch() + [pltpu.VMEM((TILE, width), F32)],
        mib=58,
    )(x, gain, cosine, sine, *arrays)


def masks(seg_row, seg_col, rows, begin, finish):
    key = lax.broadcasted_iota(jnp.int32, (finish, finish - begin), 0)
    query = lax.broadcasted_iota(jnp.int32, (finish, finish - begin), 1) + begin
    return (seg_col[:finish] == seg_row[:, begin:finish]) & (key <= query)


def query_blocks(rows):
    half = rows // 2
    return [(0, half), (half, rows)] if half % 128 == 0 else [(0, rows)]


def attention_forward(q, kv, seg_row, seg_col, rows):
    width = q.shape[1]
    heads = width // HD
    groups = q.shape[0] // rows

    def body(q_ref, kv_ref, row_ref, col_ref, out_ref, lse_ref, turned):
        keys = kv_ref[:, :HD]
        values = kv_ref[...].astype(F32).T[HD:].astype(BF)
        for begin, finish in query_blocks(rows):
            allowed = masks(row_ref[0], col_ref[0], rows, begin, finish)
            for h in range(heads):
                scores = dot_nt(keys[:finish], q_ref[begin:finish, h * HD : (h + 1) * HD]) * 0.125
                scores = jnp.where(allowed, scores, -1e30)
                top = jnp.max(scores, axis=0, keepdims=True)
                expo = jnp.exp(scores - top)
                total = jnp.sum(expo, axis=0, keepdims=True)
                probs = (expo * (1.0 / total)).astype(BF)
                turned[h * HD : (h + 1) * HD, begin:finish] = dot(values[:, :finish], probs)
                lse_ref[0, h : h + 1, begin:finish] = top + jnp.log(total)
        out_ref[...] = turned[...].T.astype(BF)

    return call(
        body,
        "attention_forward",
        [struct(q.shape, BF), struct((groups, heads, rows), F32)],
        (groups,),
        [
            pl.BlockSpec((rows, width), lambda i: (i, 0)),
            pl.BlockSpec((rows, 128), lambda i: (i, 0)),
            pl.BlockSpec((1, 1, rows), lambda i: (i, 0, 0)),
            pl.BlockSpec((1, rows, 1), lambda i: (i, 0, 0)),
        ],
        [
            pl.BlockSpec((rows, width), lambda i: (i, 0)),
            pl.BlockSpec((1, heads, rows), lambda i: (i, 0, 0)),
        ],
        [pltpu.VMEM((width, rows), F32)],
        mib=16,
    )(q, kv, seg_row, seg_col)


def attention_backward(q, kv, grad, lse, seg_row, seg_col, cosine, sine, rows, which, before=None):
    width = q.shape[1]
    heads = width // HD
    old = [] if before is None else [before]

    def body(q_ref, kv_ref, grad_ref, lse_ref, row_ref, col_ref, cos_ref, sin_ref, *refs):
        out_ref, turned, total_k, total_v = refs[len(old) :]
        keys = kv_ref[:, :HD]
        values = kv_ref[:, HD:]
        keys_t = kv_ref[...].astype(F32).T[:HD].astype(BF)
        total_k[...] = jnp.zeros_like(total_k)
        total_v[...] = jnp.zeros_like(total_v)
        for begin, finish in query_blocks(rows):
            allowed = masks(row_ref[0], col_ref[0], rows, begin, finish)
            for h in range(heads):
                head = slice(h * HD, (h + 1) * HD)
                query, grads = q_ref[begin:finish, head], grad_ref[begin:finish, head]
                scores = dot_nt(keys[:finish], query) * 0.125
                scores = jnp.where(allowed, scores, -1e30)
                probs = jnp.exp(scores - lse_ref[0, h : h + 1, begin:finish])
                grad_probs = dot_nt(values[:finish], grads)
                inner = jnp.sum(probs * grad_probs, axis=0, keepdims=True)
                grad_scores = (probs * (grad_probs - inner)).astype(BF)
                turned[head, begin:finish] = dot(keys_t[:, :finish], grad_scores)
                total_k[:finish] += dot(grad_scores, query)
                total_v[:finish] += dot(probs.astype(BF), grads)
        cosv, sinv = cos_ref[...], -sin_ref[...]
        grad_q = turned[...].T * 0.125
        for block in lane_blocks(width, 128):
            out_ref[:, block] = rope(grad_q[:, block], cosv, sinv).astype(BF)
        grad_kv = jnp.concatenate([total_k[...] * 0.125, total_v[...]], axis=1)
        out_ref[:, width:] = rope_kv(grad_kv, cosv, sinv).astype(BF)

    group = lambda w: pl.BlockSpec((rows, w), lambda i: (which, 0))
    one = lambda *shape: pl.BlockSpec((1,) + shape, lambda i: (which, 0, 0))
    return pl.pallas_call(
        body,
        out_shape=struct((q.shape[0], width + 128), BF),
        grid=(1,),
        in_specs=[group(width), group(128), group(width), one(heads, rows), one(1, rows), one(rows, 1)]
        + [group(128), group(128)]
        + [HBM] * len(old),
        out_specs=group(width + 128),
        scratch_shapes=[
            pltpu.VMEM((width, rows), F32),
            pltpu.VMEM((rows, HD), F32),
            pltpu.VMEM((rows, HD), F32),
        ],
        input_output_aliases={8: 0} if old else {},
        name="attention_backward",
        compiler_params=pltpu.CompilerParams(vmem_limit_bytes=20 * 2**20),
        cost_estimate=pl.CostEstimate(flops=0, bytes_accessed=0, transcendentals=0),
    )(q, kv, grad, lse, seg_row, seg_col, cosine, sine, *old)


def pieces_of(rows, count):
    each = -(-rows // 16 // count) * 16
    cuts = [min(rows, i * each) for i in range(count)] + [rows]
    return [slice(x, y) for x, y in zip(cuts[:-1], cuts[1:])]


def project(lefts, slots, rows, name, split=2, mib=28):
    depth = slots[0].shape[0]
    cols = min(256, depth)
    per = cols // slots[0].step
    counts = [len(s.flat()) for s in slots]
    arrays = [b for s in slots for b in s.flat()]
    k, a = len(lefts), len(arrays)

    def body(*refs):
        left_refs, weights, out_refs = refs[:k], refs[k:][:a], refs[k + a :][: 1 + split]
        scratch = refs[k + a + 1 + split :]
        step = pl.program_id(0)
        copies, at = [], 0
        for j, (s, count) in enumerate(zip(slots, counts)):
            copies.append(s.copies(weights[at : at + count], scratch[2 * j], scratch[2 * j + 1]))
            at += count

        @pl.when(step == 0)
        def _():
            for i in range(len(copies[0])):
                for chain in copies:
                    for copy in chain[i]:
                        copy.start()

        for i in range(len(copies[0])):

            @pl.when(step == i // per)
            def _():
                for chain in copies:
                    for copy in chain[i]:
                        copy.wait()

        total = None
        block = pl.ds(pl.multiple_of(step * cols, cols), cols)
        for j in range(k):
            term = dot_nt(left_refs[j][...], scratch[2 * j][block, :])
            total = term if total is None else total + term
        out_refs[0][...] = total[:rows].astype(BF)
        for ref, part in zip(out_refs[1:], pieces):
            ref[...] = total[rows + part.start : rows + part.stop].astype(BF)

    pieces = pieces_of(rows, split)
    column = lambda r: pl.BlockSpec((r, cols), lambda i: (0, i))
    mine, *theirs = call(
        body,
        name,
        [struct((rows, depth), BF)] + [struct((p.stop - p.start, depth), BF) for p in pieces],
        (depth // cols,),
        [whole((2 * rows, left.shape[1])) for left in lefts] + [HBM] * a,
        [column(rows)] + [column(p.stop - p.start) for p in pieces],
        [x for s in slots for x in s.scratch()],
        mib=mib,
    )(*lefts, *arrays)
    return mine, theirs


def parts_of(depth, count):
    tiles_each = -(-depth // 128 // count)
    cuts = [min(depth, i * tiles_each * 128) for i in range(count)] + [depth]
    return [slice(x, y) for x, y in zip(cuts[:-1], cuts[1:])]


def join_cores(mine, came):
    rows, depth = mine.shape

    def body(mine_ref, *refs):
        at = 0
        for ref in refs[:-1]:
            part = slice(at, at + ref.shape[0])
            refs[-1][part] = (mine_ref[part].astype(F32) + ref[...].astype(F32)).astype(BF)
            at = part.stop

    return call(
        body,
        "join_cores",
        struct((rows, depth), BF),
        (1,),
        [whole((rows, depth))] + [whole(c.shape) for c in came],
        whole((rows, depth)),
        mib=16,
    )(mine, *came)


def mixer_forward(field, both, begin, rows, before=None):
    tile, depth = field.shape
    units = both.shape[1] // 2
    at = begin // tile
    arrays = both.flat()
    old = [] if before is None else list(before)

    def body(*refs):
        x = refs[0][...]
        weights, refs = refs[1 : 1 + len(arrays)], refs[1 + len(arrays) + len(old) :]
        lin_ref, act_ref, x_ref, mark_ref, mem, sem = refs
        x_ref[...] = x
        mark_ref[...] = jnp.zeros_like(mark_ref)
        copies = started(both.copies(weights, mem, sem))
        lin = product_as_it_comes(x, copies, mem, both.step)
        lin_ref[...] = lin.astype(BF)
        gate_value, lifted = lin[:, :units], lin[:, units:]
        act_ref[...] = (gate_value * jax.nn.sigmoid(gate_value) * lifted).astype(BF)

    block = lambda w: pl.BlockSpec((tile, w), lambda i: (at, 0))
    first = 1 + len(arrays)
    widths = [2 * units, units, depth]
    return pl.pallas_call(
        body,
        out_shape=[struct((rows, w), BF) for w in widths] + [struct((8, 128), F32)],
        grid=(1,),
        in_specs=[whole((tile, depth))] + [HBM] * (len(arrays) + len(old)),
        out_specs=[block(w) for w in widths] + [whole((8, 128))],
        scratch_shapes=both.scratch(),
        input_output_aliases={first + i: i for i in range(len(old))},
        name="mixer_forward",
        compiler_params=pltpu.CompilerParams(vmem_limit_bytes=58 * 2**20),
        cost_estimate=pl.CostEstimate(flops=0, bytes_accessed=0, transcendentals=0),
    )(field, *arrays, *old)


def mixer_backward(dy, down, lin):
    rows, depth = dy.shape
    units = down.shape[1]
    arrays = down.flat()
    tile = min(256, rows)

    def body(dy_ref, lin_ref, *refs):
        weights, grad_ref, (buffer, sem, act_ref) = refs[: len(arrays)], refs[-4], refs[-3:]

        @pl.when(pl.program_id(0) == 0)
        def _():
            copies = started(down.copies(weights, buffer, sem))
            act_ref[...] = product_as_it_comes(dy_ref, copies, buffer, down.step)

        @pl.when(pl.program_id(0) > 0)
        def _():
            act_ref[...] = dot(dy_ref[...], buffer[...])

        grad_act, gate_value = act_ref[...], lin_ref[:, :units].astype(F32)
        lifted = lin_ref[:, units:].astype(F32)
        s = jax.nn.sigmoid(gate_value)
        grad_ref[:, :units] = (
            grad_act * lifted * s * (1.0 + gate_value * (1.0 - s))
        ).astype(BF)
        grad_ref[:, units:] = (grad_act * (gate_value * s)).astype(BF)

    return call(
        body,
        "mixer_backward",
        struct((rows, 2 * units), BF),
        (rows // tile,),
        [tiles(depth, tile), tiles(2 * units, tile)] + [HBM] * len(arrays),
        tiles(2 * units, tile),
        down.scratch() + [pltpu.VMEM((tile, units), F32)],
        mib=28,
    )(dy, lin, *arrays)


def attended_backward(mine, theirs, out):
    rows, depth = mine[0].shape[0], out.shape[0]
    width = out.shape[1]
    half = rows // TILE
    arrays = out.flat()
    k = len(mine)

    def body(*refs):
        own = pl.program_id(0) < half
        x = jnp.concatenate(
            [jnp.where(own, a[...], b[...]) for a, b in zip(refs[:k], refs[k : 2 * k])], axis=1
        )
        refs = refs[2 * k :]
        weights, (grad_ref, both_ref), (buffer, sem) = (
            refs[: len(arrays)],
            refs[len(arrays) : -2],
            refs[-2:],
        )
        both_ref[...] = x

        @pl.when(pl.program_id(0) == 0)
        def _():
            copies = started(out.copies(weights, buffer, sem))
            grad_ref[...] = product_as_it_comes(x, copies, buffer, out.step).astype(BF)

        @pl.when(pl.program_id(0) > 0)
        def _():
            grad_ref[...] = dot(x, buffer[...]).astype(BF)

    own_rows = [pl.BlockSpec((TILE, m.shape[1]), lambda i: (jnp.minimum(i, half - 1), 0)) for m in mine]
    their_rows = [pl.BlockSpec((TILE, m.shape[1]), lambda i: (jnp.maximum(i - half, 0), 0)) for m in mine]
    return call(
        body,
        "attended_backward",
        [struct((2 * rows, width), BF), struct((2 * rows, depth), BF)],
        (2 * half,),
        own_rows + their_rows + [HBM] * len(arrays),
        [tiles(width), tiles(depth)],
        out.scratch(),
        mib=16,
    )(*mine, *theirs, *arrays)


def norm_forward(x, mine, other, gain, rows):
    depth = x.shape[1]

    def body(x_ref, gain_ref, mine_ref, other_ref, resid_ref, normed_ref):
        resid = x_ref[...].astype(F32) + (mine_ref[...].astype(F32) + other_ref[...].astype(F32))
        resid_ref[...] = resid
        normed_ref[...] = (resid * rms_scale(resid) * gain_ref[...]).astype(BF)

    return call(
        body,
        "norm_forward",
        [struct((rows, depth), F32), struct((rows, depth), BF)],
        (rows // TILE,),
        [tiles(depth), whole((1, depth)), tiles(depth), tiles(depth)],
        [tiles(depth)] * 2,
        mib=24,
    )(x, gain, mine, other)


def norm_backward(resid, mine, other, dy, gain, rows):
    depth = dy.shape[1]
    parts = parts_of(depth, 2)

    def body(resid_ref, dy_ref, gain_ref, mine_ref, other_ref, *branch_refs):
        resid = resid_ref[...]
        grad_normed = mine_ref[...].astype(F32) + other_ref[...].astype(F32)
        grad = norm_back(resid, rms_scale(resid), gain_ref[...], grad_normed)
        grad = grad + dy_ref[...].astype(F32)
        for ref, block in zip(branch_refs, parts):
            ref[...] = grad[:, block].astype(BF)

    return call(
        body,
        "norm_backward",
        [struct((rows, p.stop - p.start), BF) for p in parts],
        (rows // TILE,),
        [tiles(depth), tiles(depth), whole((1, depth)), tiles(depth), tiles(depth)],
        [tiles(p.stop - p.start) for p in parts],
        mib=28,
    )(resid, dy, gain, mine, other)


def leave_ring(fn, arrays, gain, order, wide, rows, name, mib=32):
    depth = gain.shape[1]
    n = depth // wide
    if wide % 128 or rows % TILE:
        field = fn(*[a[:rows] for a in arrays], gain).astype(BF)
        back = jnp.zeros((n,), jnp.int32).at[order].set(jnp.arange(n, dtype=jnp.int32))
        return jnp.take(field.reshape(rows, n, wide), back, axis=1).reshape(rows, depth)
    k = len(arrays)

    def body(order_ref, *refs):
        field = fn(*[r[...] for r in refs[:k]], refs[k][...]).astype(BF)
        for i, block in enumerate(lane_blocks(depth, wide)):
            refs[k + 1][:, pl.ds(pl.multiple_of(order_ref[i] * wide, wide), wide)] = field[:, block]

    return call(
        body,
        name,
        struct((rows, depth), BF),
        (rows // TILE,),
        [tiles(a.shape[1]) for a in arrays] + [whole((1, depth))],
        tiles(depth),
        prefetch=1,
        mib=mib,
    )(order, *arrays, gain)


def turned(block):
    return block.astype(F32).T.astype(BF)


def fetch(pairs, sem):
    copies = [pltpu.make_async_copy(a, b, sem.at[i]) for i, (a, b) in enumerate(pairs)]
    for copy in copies:
        copy.start()
    for copy in copies:
        copy.wait()


def columns(ref, half):
    size = ref.shape[1] // 2
    return ref.at[:, pl.ds(pl.multiple_of(half * size, 128), size)]


def rows_of(ref, half):
    size = ref.shape[0] // 2
    return ref.at[pl.ds(pl.multiple_of(half * size, 128), size), :]


def gain_tile(one, two):
    row = lax.broadcasted_iota(jnp.int32, (16, one.shape[1]), 0)
    both = jnp.where(row == 0, one.astype(F32), jnp.where(row == 1, two.astype(F32), 0.0))
    return both.astype(BF)


def halves(core, w_query, w_key, w_value, w_output, gain_attend, gain_mixer):
    part, q_cols = w_query.shape[0], w_query.shape[1] // 2
    k_cols = w_key.shape[1] // 2
    width, out_width = q_cols + 2 * k_cols, w_output.shape[0] // 2

    def body(
        core_ref, q_ref, k_ref, v_ref, o_ref, one_ref, two_ref, qkv_ref, out_ref, k_mem, v_mem, o_mem, sem
    ):
        there = 1 - core_ref[0]
        low = there == 0
        fetch(
            [
                (columns(q_ref, there), qkv_ref.at[pl.ds(0, part), pl.ds(0, q_cols)]),
                (k_ref, k_mem),
                (v_ref, v_mem),
                (rows_of(o_ref, there), o_mem),
            ],
            sem,
        )
        k, v = k_mem[...], v_mem[...]
        qkv_ref[:part, q_cols:] = jnp.concatenate(
            [jnp.where(low, w[:, :k_cols], w[:, k_cols:]) for w in (k, v)], axis=1
        )
        qkv_ref[part:, :] = jnp.zeros((16, width), BF)
        qkv_ref[part:, :part] = gain_tile(one_ref[...], two_ref[...])
        out_ref[...] = turned(o_mem[...])

    shapes = [(part + 16, width), (part, out_width)]
    return call(
        body,
        "halves",
        [struct(shape, BF) for shape in shapes],
        (1,),
        [HBM] * 4 + [whole((1, part))] * 2,
        [whole(shape) for shape in shapes],
        [
            pltpu.VMEM((part, 2 * k_cols), BF),
            pltpu.VMEM((part, 2 * k_cols), BF),
            pltpu.VMEM((out_width, part), BF),
            pltpu.SemaphoreType.DMA((4,)),
        ],
        prefetch=1,
        mib=58,
    )(core, w_query, w_key, w_value, w_output, gain_attend, gain_mixer)


def mixer_halves(core, w_gate, w_up, w_down):
    part, units = w_gate.shape[0], w_gate.shape[1] // 2

    def body(core_ref, gate_ref, up_ref, down_ref, mixer_ref, down_mem, sem):
        there = 1 - core_ref[0]
        fetch(
            [
                (columns(gate_ref, there), mixer_ref.at[:, pl.ds(0, units)]),
                (columns(up_ref, there), mixer_ref.at[:, pl.ds(units, units)]),
                (rows_of(down_ref, there), down_mem),
            ],
            sem,
        )
        mixer_ref[:, 2 * units :] = turned(down_mem[...])

    return call(
        body,
        "mixer_halves",
        struct((part, 3 * units), BF),
        (1,),
        [HBM] * 3,
        whole((part, 3 * units)),
        [pltpu.VMEM((units, part), BF), pltpu.SemaphoreType.DMA((3,))],
        prefetch=1,
        mib=58,
    )(core, w_gate, w_up, w_down)


def put_rows(core_ref, out_ref, mine, came, part, cols=slice(None)):
    @pl.when(core_ref[0] == 0)
    def _():
        out_ref[:part, cols], out_ref[part : 2 * part, cols] = mine, came

    @pl.when(core_ref[0] == 1)
    def _():
        out_ref[:part, cols], out_ref[part : 2 * part, cols] = came, mine


def chip_rows(core, w_query, w_key, w_value, w_output, gain_attend, gain_mixer, came, came_out):
    part, q_cols = w_query.shape[0], w_query.shape[1] // 2
    k_cols = w_key.shape[1] // 2
    width, out_width = came.shape[1], came_out.shape[1]

    def body(
        core_ref, q_ref, k_ref, v_ref, o_ref, one_ref, two_ref, came_ref, came_out_ref,
        qkv_ref, out_ref, q_mem, k_mem, v_mem, o_mem, sem,
    ):
        here = core_ref[0]
        first = here == 0
        fetch(
            [
                (columns(q_ref, here), q_mem),
                (k_ref, k_mem),
                (v_ref, v_mem),
                (rows_of(o_ref, here), o_mem),
            ],
            sem,
        )
        k, v = k_mem[...], v_mem[...]
        own = [jnp.where(first, w[:, :k_cols], w[:, k_cols:]) for w in (k, v)]
        put_rows(core_ref, qkv_ref, jnp.concatenate([q_mem[...]] + own, axis=1), came_ref[:part], part)
        put_rows(core_ref, out_ref, turned(o_mem[...]), came_out_ref[...], part)
        qkv_ref[2 * part :, :] = jnp.zeros((16, width), BF)
        own, other = gain_tile(one_ref[...], two_ref[...]), came_ref[part : part + 16, :part]
        qkv_ref[2 * part :, :part] = jnp.where(first, own, other)
        qkv_ref[2 * part :, part : 2 * part] = jnp.where(first, other, own)

    return call(
        body,
        "chip_rows",
        [struct((2 * part + 16, width), BF), struct((2 * part, out_width), BF)],
        (1,),
        [HBM] * 4 + [whole((1, part))] * 2 + [whole(came.shape), whole(came_out.shape)],
        [whole((2 * part + 16, width)), whole((2 * part, out_width))],
        [
            pltpu.VMEM((part, q_cols), BF),
            pltpu.VMEM((part, 2 * k_cols), BF),
            pltpu.VMEM((part, 2 * k_cols), BF),
            pltpu.VMEM((out_width, part), BF),
            pltpu.SemaphoreType.DMA((4,)),
        ],
        prefetch=1,
        mib=58,
    )(core, w_query, w_key, w_value, w_output, gain_attend, gain_mixer, came, came_out)


def mixer_rows(core, w_gate, w_up, w_down, came):
    part, units = w_gate.shape[0], w_gate.shape[1] // 2

    def body(core_ref, gate_ref, up_ref, down_ref, came_ref, both_ref, turned_ref, gate_mem, up_mem, down_mem, sem):
        here = core_ref[0]
        fetch(
            [
                (columns(gate_ref, here), gate_mem),
                (columns(up_ref, here), up_mem),
                (rows_of(down_ref, here), down_mem),
            ],
            sem,
        )
        for i, mem in enumerate((gate_mem, up_mem)):
            cols = slice(i * units, (i + 1) * units)
            put_rows(core_ref, both_ref, mem[...], came_ref[:, cols], part, cols)
        put_rows(core_ref, turned_ref, turned(down_mem[...]), came_ref[:, 2 * units :], part)

    shapes = [(2 * part, 2 * units), (2 * part, units)]
    return call(
        body,
        "mixer_rows",
        [struct(shape, BF) for shape in shapes],
        (1,),
        [HBM] * 3 + [whole(came.shape)],
        [whole(shape) for shape in shapes],
        [pltpu.VMEM((part, units), BF)] * 2
        + [pltpu.VMEM((units, part), BF), pltpu.SemaphoreType.DMA((3,))],
        prefetch=1,
        mib=58,
    )(core, w_gate, w_up, w_down, came)


def beside(core, mine, came, turn):
    part, width = mine.shape
    shape = (2 * width, part) if turn else (part, 2 * width)

    def body(core_ref, mine_ref, came_ref, out_ref):
        def put(low, high):
            if turn:
                out_ref[:width], out_ref[width:] = low[...].T, high[...].T
            else:
                out_ref[:, :width], out_ref[:, width:] = low[...], high[...]

        @pl.when(core_ref[0] == 0)
        def _():
            put(mine_ref, came_ref)

        @pl.when(core_ref[0] == 1)
        def _():
            put(came_ref, mine_ref)

    return call(
        body,
        "beside",
        struct(shape, F32),
        (1,),
        [whole((part, width))] * 2,
        whole(shape),
        prefetch=1,
        mib=16,
    )(core, mine, came)


def after(value, *others):
    return lax.optimization_barrier((value,) + others)[0]


class Ring:
    def __init__(self, devices):
        self.n = devices // 2
        n = self.n
        order = list(range(0, n, 2)) + list(range(n - 1 - n % 2, 0, -2))
        self.order = order
        place = [0] * n
        for position, chip in enumerate(order):
            place[chip] = position
        self.place = place
        self.steps = {1: [], -1: []}
        for position, chip in enumerate(order):
            then = order[(position + 1) % n]
            for core in (0, 1):
                self.steps[1].append((2 * chip + core, 2 * then + core))
                self.steps[-1].append((2 * then + core, 2 * chip + core))
        self.cores = [(i, i ^ 1) for i in range(devices)]
        self.hops = n // 2

    def pass_on(self, block, way):
        return lax.ppermute(block, "dp", self.steps[way])

    def halves(self, width):
        cut = min(width, (width // 2 + 127) // 128 * 128)
        return slice(0, cut), slice(cut, width)

    def swap(self, block):
        return lax.ppermute(block, "dp", self.cores)


class Gather:
    def __init__(self, ring, block):
        self.ring, self.hop = ring, 0
        self.found = [[block]] + [None] * (ring.n - 1)
        self.last = (block,)

    def step(self, *others):
        ring, n = self.ring, self.ring.n
        self.hop += 1
        hop = self.hop
        if 2 * hop > n:
            return
        before = [self.found[(hop - 1) * way % n][0] for way in (1, -1)]
        if others:
            before = [after(b, *others) for b in before]
        if 2 * hop < n:
            for way, block in zip((1, -1), before):
                self.found[hop * way % n] = [ring.pass_on(block, way)]
            self.last = tuple(self.found[hop * way % n][0] for way in (1, -1))
        else:
            parts = ring.halves(before[0].shape[1])
            self.found[hop] = [
                ring.pass_on(b[:, part], way) for b, way, part in zip(before, (1, -1), parts)
            ]
            self.last = tuple(self.found[hop])

    def finish(self):
        while 2 * (self.hop + 1) <= self.ring.n:
            self.step()
        return self.found


class Line:
    def __init__(self):
        self.marks = ()

    def after(self, value):
        return after(value, *self.marks) if self.marks else value

    def mark(self, *found):
        self.marks = found

    def wait(self, *found):
        self.marks = self.marks + found


class Scatter:
    def __init__(self, ring, line, field, grads):
        self.ring, self.line, self.field, self.grads = ring, line, field, grads
        self.width, self.hop = grads.shape[1], 0
        self.wide = field.shape[1] // ring.n
        self.held = {1: None, -1: None}
        self.last = ()

    def term(self, i, part):
        field = self.line.after(self.field)
        return dot_tn(field[:, i * self.wide : (i + 1) * self.wide], self.grads[:, part])

    def step(self):
        ring, n = self.ring, self.ring.n
        far = n // 2 - self.hop
        if far == 0:
            return
        self.hop += 1
        for way, part in zip((1, -1), ring.halves(self.width)):
            if 2 * far == n:
                total = self.term(far, part)
            else:
                part = slice(0, self.width)
                total = self.term(-far * way % n, part) + self.came(way)
            total = total.astype(BF)
            self.line.mark(total)
            self.held[way] = (ring.pass_on(total, way), part)
        self.last = tuple(self.held[way][0] for way in (1, -1))

    def came(self, way):
        if self.held[way] is None:
            return 0.0
        came, part = self.held[way]
        edges = ((0, 0, 0), (part.start, self.width - part.stop, 0))
        return lax.pad(came.astype(F32), jnp.zeros((), F32), edges)

    def finish(self):
        while self.hop < self.ring.n // 2:
            self.step()
        total = self.term(0, slice(0, self.width)) + self.came(1) + self.came(-1)
        self.line.mark(total)
        return total


def half_of(w, half, axis):
    size = w.shape[axis] // 2
    return lax.dynamic_slice_in_dim(w, half * size, size, axis)


def slow_rows(core, swap, pick):
    mine, came = pick(core), swap(pick(1 - core))
    first = core == 0
    return jnp.where(first, mine, came), jnp.where(first, came, mine)


def slow_attend_rows(core, swap, w_query, w_key, w_value, w_output, gain_attend, gain_mixer):
    part = w_query.shape[0]
    qkv = slow_rows(
        core,
        swap,
        lambda half: jnp.concatenate([half_of(w, half, 1) for w in (w_query, w_key, w_value)], axis=1),
    )
    out = slow_rows(core, swap, lambda half: half_of(w_output, half, 0).T)
    gains = slow_rows(core, swap, lambda half: jnp.concatenate([gain_attend, gain_mixer]))
    below = jnp.concatenate(gains, axis=1)
    below = jnp.pad(below, ((0, 14), (0, qkv[0].shape[1] - 2 * part)))
    return jnp.concatenate(qkv + (below,)), jnp.concatenate(out)


def slow_mixer_rows(core, swap, w_gate, w_up, w_down):
    picks = (
        lambda half: half_of(w_gate, half, 1),
        lambda half: half_of(w_up, half, 1),
        lambda half: half_of(w_down, half, 0).T,
    )
    gate, up, down = [jnp.concatenate(slow_rows(core, swap, pick)) for pick in picks]
    return jnp.concatenate([gate, up], axis=1), down


def per_device(
    shape,
    tokens,
    segments,
    gain_attend,
    w_query,
    w_key,
    w_value,
    w_output,
    gain_mixer,
    w_gate,
    w_up,
    w_down,
    cotangent,
):
    devices, tensors = shape
    ring = Ring(devices)
    swap = ring.swap
    n = ring.n
    rows, depth = tokens.shape
    part = depth // devices
    wide = 2 * part
    index = lax.axis_index("dp")
    core = index % 2
    first = core == 0
    position = jnp.asarray(ring.place, jnp.int32)[index // 2]
    blocks = jnp.asarray(ring.order, jnp.int32)[(position - jnp.arange(n, dtype=jnp.int32)) % n]

    def across(block):
        if tensors == 1:
            return jnp.zeros_like(block)
        return lax.ppermute(block, "tensor", [(i, i ^ 1) for i in range(tensors)])

    line = Line()

    q_cols = w_query.shape[1] // 2
    k_cols = w_key.shape[1] // 2
    all_cols = q_cols + 2 * k_cols
    attend = (w_query, w_key, w_value, w_output, gain_attend[None], gain_mixer[None])
    mixer = (w_gate, w_up, w_down)
    which = core.astype(jnp.int32)[None]
    if part % 128:
        tokens_came, cotangent_came, segments_came = swap(tokens), swap(cotangent), swap(segments)
        qkv_block, out_block = slow_attend_rows(core, swap, *attend)
        both_block, down_block = slow_mixer_rows(core, swap, *mixer)
    else:
        sent = halves(which, *attend)
        line.mark(*sent)
        sent_mixer = mixer_halves(line.after(which), *mixer)
        line.mark(sent_mixer)
        sent = [swap(s) for s in sent]
        segments_came = swap(segments)
        tokens_came, cotangent_came = swap(after(tokens, *sent)), swap(after(cotangent, *sent))
        mixer_came = swap(after(sent_mixer, *sent))
        qkv_block, out_block = chip_rows(line.after(which), *attend, *sent)
        came = (tokens_came, cotangent_came, segments_came, mixer_came)
        qkv_block, out_block = after(qkv_block, *came), after(out_block, *came)
        line.mark(qkv_block)
        both_block, down_block = mixer_rows(line.after(which), *mixer, mixer_came)
        line.mark(both_block)

    ring_q, ring_o = Gather(ring, qkv_block), Gather(ring, out_block)
    ring_q.step()
    ring_o.step()
    segs = jnp.stack([segments, segments_came])
    places = jnp.arange(rows, dtype=jnp.int32)
    fresh = jnp.concatenate([jnp.ones((2, 1), dtype=bool), segs[:, 1:] != segs[:, :-1]], axis=1)
    starts = lax.cummax(jnp.where(fresh, places, 0), axis=1)
    lanes = jnp.arange(128, dtype=jnp.int32)
    freqs = jnp.exp((lanes % (HD // 2)).astype(F32) * (-2.0 * math.log(10000.0) / HD))
    angle = (places - starts).astype(F32).reshape(2 * rows, 1) * freqs[None, :]
    seg_row, seg_col = segs.reshape(2, 1, rows), segs.reshape(2, rows, 1)
    x = to_ring(line.after(tokens), tokens_came, blocks, wide)
    line.mark(x, *ring_q.last)
    ring_q.step(x)
    angle = line.after(angle)
    cosine = jnp.cos(angle)
    sine = jnp.sin(angle) * jnp.where(lanes % HD < HD // 2, -1.0, 1.0)
    line.mark(cosine, *ring_o.last)
    ring_o.step(cosine)
    dy = to_ring(line.after(cotangent), cotangent_came, blocks, wide)
    line.mark(dy, *ring_q.last)
    ring_q.step(dy)
    line.wait(*ring_o.last)
    ring_o.step(dy)
    line.wait(*ring_q.last)
    ring_q.step()
    line.wait(*ring_o.last)
    ring_o.step()
    line.wait(*ring_q.last, *ring_o.last)
    qkv_parts = ring_q.finish()
    w_out = Slots(ring_o.finish(), wide)
    w_qkv = Slots(qkv_parts, wide)
    ring_g, ring_d = Gather(ring, both_block), Gather(ring, down_block)
    ring_g.step(*ring_q.last, *ring_o.last)

    def gain_of(row):
        return jnp.concatenate(
            [p[0][wide + row : wide + row + 1, :wide] for p in qkv_parts], axis=1
        ).astype(F32)

    gain_one, gain_two = gain_of(0), gain_of(1)

    def swap_all(pieces):
        return [swap(piece) for piece in pieces]

    def swap_late(pieces):
        return [swap(line.after(piece)) for piece in pieces]

    def joined(mine, came):
        mine = join_cores(line.after(mine), came)
        line.mark(mine)
        return mine

    def own(field, which):
        return lax.dynamic_slice_in_dim(field, which * part, part, 0)

    def send(field):
        rows_there = own(line.after(field), 1 - core)
        line.mark(rows_there)
        return field, swap(rows_there)

    def spread(pair):
        mine, came = own(line.after(pair[0]), core), pair[1]
        return jnp.where(first, mine, came), jnp.where(first, came, mine)

    def spread_turned(pair):
        mine, came = own(line.after(pair[0]), core), pair[1]
        if part % 128:
            low, high = jnp.where(first, mine, came), jnp.where(first, came, mine)
            return jnp.concatenate([low, high], axis=1).T
        return beside(which, mine, came, True)

    def done(*found):
        line.mark(*found)
        return found[0]

    def gain_grad(pairs):
        return sum(jnp.sum(w.astype(F32) * g, axis=1) for w, g in pairs)

    normed_one, queries, kv = qkv_forward(line.after(x), gain_one, w_qkv, cosine, sine)
    line.mark(normed_one)
    attended, lse = attention_forward(line.after(queries), kv, seg_row, seg_col, rows)
    line.mark(attended, *ring_g.last)
    ring_g.step(attended)
    mine, theirs = project([line.after(attended)], [w_out], rows, "attended_out", 3, 58)
    line.mark(mine)
    mine = joined(mine, swap_late(theirs))
    other = across(mine)
    line.wait(*ring_g.last)
    ring_g.step(*line.marks)
    ring_d.step(*line.marks)
    resid, normed_mine = norm_forward(x, line.after(mine), other, gain_two, rows)
    line.mark(resid, *ring_g.last)
    came = swap(line.after(normed_mine))
    ring_g.step(resid)
    both = Slots(ring_g.finish(), wide)
    line.wait(*ring_d.last)
    ring_d.step()
    *first_rows, mark = mixer_forward(line.after(normed_mine), both, 0, 2 * rows)
    line.mark(mark, *ring_d.last)
    ring_d.step(*line.marks)
    lin, act, normed_two, mark = mixer_forward(line.after(came), both, rows, 2 * rows, first_rows)
    line.mark(mark)

    grad_down = Scatter(ring, line, dy, act)
    grad_down.step()
    line.wait(*ring_d.last)
    ring_d.step(*line.marks)
    grad_down.step()
    line.wait(*ring_d.last)
    down = Slots(ring_d.finish(), wide)
    grad_lin = mixer_backward(line.after(dy), down, lin)
    line.mark(grad_lin)
    grad_both = Scatter(ring, line, normed_two, grad_lin)
    grad_both.step()
    line.wait(*grad_down.last)
    grad_down.step()
    mine, theirs = project([line.after(grad_lin)], [both], rows, "grad_normed_two")
    line.mark(mine, *grad_both.last, *grad_down.last)
    came = swap_late(theirs)
    grad_both.step()
    mine = joined(mine, came)
    other = across(mine)
    grad_down.step()
    out_mine, out_theirs = project([line.after(act)], [down], rows, "act_out")
    line.mark(out_mine, *grad_both.last)
    came = swap_late(out_theirs)
    grad_both.step()
    out_mine = joined(out_mine, came)
    line.wait(other, *grad_down.last)
    out_other = across(line.after(out_mine))
    branch_mine = list(norm_backward(resid, line.after(mine), other, dy, gain_two, rows))
    branch_parts = list(branch_mine)
    line.mark(*branch_mine)
    came = swap_all(branch_mine)
    branch_mine[0] = line.after(branch_mine[0])
    grad_attended, grad_branch = attended_backward(branch_mine, came, w_out)
    line.mark(grad_attended)
    pieces = (kv, grad_attended, lse, seg_row, seg_col, cosine, sine, rows)
    grad_qkv = attention_backward(line.after(queries), *pieces, 0)
    line.mark(grad_qkv)
    grad_qkv = attention_backward(line.after(queries), *pieces, 1, grad_qkv)
    line.mark(grad_qkv, *grad_both.last)
    grad_out = Scatter(ring, line, grad_branch, attended)
    grad_out.step()
    grad_projections = Scatter(ring, line, normed_one, grad_qkv)
    grad_projections.step()
    mine, theirs = project([line.after(grad_qkv)], [w_qkv], rows, "grad_normed_one")
    line.mark(mine, *grad_out.last, *grad_projections.last)
    grad_projections.step()
    grad_both.step()
    line.wait(out_other)
    came = swap_late(theirs)
    mine = joined(mine, came)
    other = across(mine)
    line.wait(*grad_projections.last)
    grad_out.step()
    down_sum = send(grad_down.finish())
    output = leave_ring(
        lambda r, m, o, _: r + (m.astype(F32) + o.astype(F32)),
        [line.after(resid), out_mine, out_other],
        gain_two,
        blocks,
        wide,
        rows,
        "leave_output",
    )
    line.mark(output)
    g_down = done(spread_turned(down_sum))
    grad_projections.step()

    def leave(mine, other, x, low, high, gain):
        x = x.astype(F32)
        grad_resid = jnp.concatenate([low.astype(F32), high.astype(F32)], axis=1)
        grad_normed = mine.astype(F32) + other.astype(F32)
        return grad_resid + norm_back(x, rms_scale(x), gain, grad_normed)

    line.wait(other, *grad_both.last)
    grad_out.step()
    grad_projections.step()
    both_sum = grad_both.finish()
    grad_out.step()
    grad_tokens = leave_ring(
        leave, [mine, other, line.after(x), *branch_parts], gain_one, blocks, wide, rows, "leave_grad_tokens"
    )
    line.mark(grad_tokens)
    qkv_sum = grad_projections.finish()
    out_sum = grad_out.finish()
    qkv_sum, both_sum, out_sum = send(qkv_sum), send(both_sum), send(out_sum)
    low, high = spread(both_sum)
    units = low.shape[1] // 2
    g_gate = done(jnp.concatenate([low[:, :units], high[:, :units]], axis=1))
    g_up = done(jnp.concatenate([low[:, units:], high[:, units:]], axis=1))
    g_two = done(gain_grad([(line.after(w_gate), g_gate), (w_up, g_up)]))
    g_two = (g_two + across(line.after(g_two))) / gain_mixer.astype(F32)
    low, high = spread(qkv_sum)
    g_out = spread_turned(out_sum)

    def sides(begin, finish):
        return jnp.concatenate([low[:, begin:finish], high[:, begin:finish]], axis=1)

    g_query = sides(0, q_cols)
    g_key = sides(q_cols, q_cols + k_cols)
    g_value = sides(q_cols + k_cols, all_cols)
    g_one = gain_grad([(w_query, g_query), (w_key, g_key), (w_value, g_value)])
    g_one = (g_one + across(g_one)) / gain_attend.astype(F32)
    return output, grad_tokens, g_one, g_query, g_key, g_value, g_out, g_two, g_gate, g_up, g_down


def solution(mesh):
    shape = (mesh.shape["dp"], mesh.shape["tensor"])
    rows, weight_in, weight_out = P("dp", None), P("dp", "tensor"), P("tensor", "dp")
    attend = (P("dp"), weight_in, weight_in, weight_in, weight_out)
    mixer = (P("dp"), weight_in, weight_in, weight_out)

    def layer(*arguments):
        return per_device(shape, *arguments)

    return jax.shard_map(
        layer,
        mesh=mesh,
        in_specs=(rows, P("dp")) + attend + mixer + (rows,),
        out_specs=(rows, rows) + attend + mixer,
        check_vma=False,
    )
```
